32 devices in a mesh: dp: 4 (over z), row: 2 (over y), col: 4 (over x, core).
Axes of the slice: x: 2, y: 2, z: 4, core: 2. Of those that a mesh axis runs over, the one named last changes fastest.
Arguments:
- tokens: bfloat16 [2, 8, 512, 768], P(None, ('dp', 'row'), 'col'), may hold values from -6 to 6
- segments: int32 [2, 8, 512], P(None, ('dp', 'row')), may hold values from 0 to 7, never falling along the last dimension, each value on 1 to 256 neighbouring positions
- routes: int32 [2, 8, 512, 1], P(None, ('dp', 'row'), 'col'), may hold values from 0 to 15; in each aligned block of 128 rows (0 to 127, 128 to 255, ..., all dimensions but the last counted through in order) at most 16 rows name the same one
- buckets: int32 [1023], replicated, may hold values from 0 to 31
- gain_attn: float32 [768], replicated, may hold values from 0.5 to 1.5
- w_qkv: bfloat16 [768, 3, 768], P(('dp', 'row'), None, 'col'), may hold values from -0.109375 to 0.109375
- w_out: bfloat16 [768, 768], P('col', ('dp', 'row')), may hold values from -1.75 to 1.75
- rel_table: float32 [32, 12], P(None, 'col'), may hold values from -4 to 4
- gain_ffn: float32 [768], replicated, may hold values from 0.5 to 1.5
- router: float32 [768, 16], replicated, may hold values from -0.109375 to 0.109375
- w_in: bfloat16 [16, 768, 3072], P(('dp', 'col'), 'row'), may hold values from -0.21875 to 0.21875
- w_down: bfloat16 [16, 3072, 768], P(('dp', 'col'), None, 'row'), may hold values from -7.5 to 7.5
- cotangent: bfloat16 [2, 8, 512, 768], P(None, ('dp', 'row'), 'col'), may hold values from -6 to 6
Outputs:
- layer_out: bfloat16 [2, 8, 512, 768], P(None, ('dp', 'row'), 'col')
- grad_tokens: float32 [2, 8, 512, 768], P(None, ('dp', 'row'), 'col')
- grad_gain_attn: float32 [768], replicated
- grad_w_qkv: float32 [768, 3, 768], P(('dp', 'row'), None, 'col')
- grad_w_out: float32 [768, 768], P('col', ('dp', 'row'))
- grad_rel_table: float32 [32, 12], P(None, 'col')
- grad_gain_ffn: float32 [768], replicated
- grad_router: float32 [768, 16], replicated
- grad_w_in: float32 [16, 768, 3072], P(('dp', 'col'), 'row')
- grad_w_down: float32 [16, 3072, 768], P(('dp', 'col'), None, 'row')
The draws below stay inside these ranges and needn't reach their ends.
Inputs may be any that keep to these rules, and one draw needn't show every extreme that they name: `routes`: in the 128 rows of one device in one micro-batch (aligned blocks of rows), no expert is named more than 16 times, and in some blocks some expert exactly 16 times. `segments`: document numbers never fall along a packed sequence.
All inputs are finite; a program needn't handle non-finite values.
Results may differ from the reference program's by a relative error of at most 0.018.
Values may be sent and summed in bfloat16 or wider, within the bound.
A program may use at most 192 MiB of HBM per device.

```python
import math
import jax
import jax.numpy as jnp
import numpy as np
from jax import lax

D = 768
HEADS = 12
HEAD_DIM = 64
FF = 3072
NBUCK = 32
SEQ = 512
MB = 2
NSEQ = 8
TOK_DEV = 128
EXPERTS = 16
CAP = 16


def touch_ends(values, rng, smallest, high):
    spot = [jax.random.randint(jax.random.fold_in(rng, axis), (), 0, length) for axis, length in enumerate(values.shape)]
    longest = values.shape.index(max(values.shape))
    next_to = spot[:longest] + [(spot[longest] + 1) % values.shape[longest]] + spot[longest + 1:]
    return values.at[tuple(spot)].set(smallest).at[tuple(next_to)].set(high)


def block_scale(stream_key, dims, cuts, least, high):
    factor_of = 1.0
    for position, blocks in cuts:
        draws = jax.random.uniform(jax.random.fold_in(jax.random.fold_in(stream_key, 6), position), (blocks,), jnp.float32, least / len(cuts), high / len(cuts))
        factor_of = factor_of * jnp.repeat(jnp.exp(draws), dims[position] // blocks).reshape((-1,) + (1,) * (len(dims) - 1 - position))
    return factor_of


def length_profile(amount, total, limit, skew):
    portions = [(1 << 20) // math.isqrt(rank ** skew) + 1 for rank in range(2, amount + 1)]
    rest, given = total - limit - (amount - 1), [1] * (amount - 1)
    while rest > 0:
        free = [i for i in range(amount - 1) if given[i] < limit]
        pool, budget = sum([portions[i] for i in free]), rest
        for i in free:
            addition = min(limit - given[i], max(1, budget * portions[i] // pool), rest)
            given[i] = given[i] + addition
            rest = rest - addition
    return np.array([limit] + given)


def uneven_parts(key, number_of, total, reach, skew):
    if number_of == 2:
        one = jax.random.randint(key, (), max(1, total - reach), min(reach, total - 1) + 1)
        return jnp.stack([one, total - one])
    sizes = jnp.asarray(length_profile(number_of, total, reach, skew), jnp.int32)
    couples = (number_of - 1) // 2
    giver, sink = sizes[1:1 + 2 * couples:2], sizes[2:2 + 2 * couples:2]
    margin = jnp.minimum(giver - 1, reach - sink)
    shifted = jax.random.randint(jax.random.fold_in(key, 1), (couples,), 0, 1 << 20) % (margin + 1)
    sizes = sizes.at[1:1 + 2 * couples:2].set(giver - shifted).at[2:2 + 2 * couples:2].set(sink + shifted)
    return sizes[jax.random.permutation(jax.random.fold_in(key, 2), number_of)]


def assign_block(rng, own, number, rows, count, top, most, skew):
    order = jax.random.permutation(rng, count)
    heavy_load, common = portions_of(count, rows * top, most, skew, True), portions_of(count, rows * top, most, skew, False)
    places = jnp.arange(count)

    def named(sizes, turn):
        used = int((sizes > 0).sum())
        fixed = max(1, used // 4)
        moved = fixed + (places - fixed + turn * (used - fixed)) % max(1, count - fixed)
        return jnp.zeros((count,), jnp.int32).at[order[jnp.where(places < fixed, places, moved)]].set(jnp.asarray(sizes, jnp.int32))

    sizes = jnp.where(number % 4 == 0, named(heavy_load, number // 4), named(common, number - number // 4 - 1))
    mixed = jax.random.permutation(jax.random.fold_in(own, 3), count)
    source_of, taker = mixed[0:count // 2 * 2:2], mixed[1:count // 2 * 2:2]
    margin = jnp.minimum(sizes[source_of] - 1, most - sizes[taker]) // 2
    margin = jnp.where((source_of == order[0]) | (taker == order[0]) | (sizes[taker] == 0), 0, jnp.maximum(margin, 0))
    moved = jax.random.randint(jax.random.fold_in(own, 4), (count // 2,), 0, 1 << 20) % (margin + 1)
    sizes = sizes.at[source_of].add(-moved).at[taker].add(moved)
    items = jnp.searchsorted(jnp.cumsum(sizes), jnp.arange(rows * top), side="right").astype(jnp.int32)
    table = items.reshape(top, rows).T
    table = table[jax.random.permutation(jax.random.fold_in(own, 1), rows)]
    turn = jax.random.randint(jax.random.fold_in(own, 2), (rows, 1), 0, top)
    return jnp.take_along_axis(table, (jnp.arange(top)[None, :] + turn) % top, axis=1)


def portions_of(number_of, total, reach, slope, full):
    loads = [(1 << 20) // math.isqrt(standing ** slope) + 1 for standing in range(1, number_of + 1)]
    largest = reach if full else min(reach, max(-(-total // number_of), total * loads[0] // sum(loads)))
    least = 1 if total - largest >= number_of - 1 else 0
    holding, surplus = [largest] + [least] * (number_of - 1), total - largest - least * (number_of - 1)
    while surplus > 0:
        candidates = [i for i in range(1, number_of) if holding[i] < largest] or [i for i in range(1, number_of) if holding[i] < reach]
        whole, budget = sum([loads[i] for i in candidates]), surplus
        for i in candidates:
            more = min(reach - holding[i], max(1, budget * loads[i] // whole), surplus)
            holding[i] = holding[i] + more
            surplus = surplus - more
    return np.array(holding)


def centred(rng, dims, deviation, bound, pieces=(), kind=jnp.bfloat16):
    entries = deviation * jax.random.normal(rng, dims, jnp.float32)
    if pieces:
        entries = entries * block_scale(rng, dims, pieces, -0.22, 0.18)
    return jnp.clip(entries, -bound, bound).astype(kind)


def setup_inputs(seed: int = 0) -> dict:
    splits = jax.random.split(jax.random.key(seed), 14)
    tokens = centred(splits[0], (MB, NSEQ, SEQ, D), 1.0, 6.0, ((1, 8), (2, 4)))
    segments = jax.vmap(lambda own: jnp.searchsorted(jnp.cumsum(uneven_parts(own, 8, SEQ, SEQ // 2, 1)), jnp.arange(SEQ), side="right"))(jax.random.split(splits[1], MB * NSEQ)).reshape((MB, NSEQ, SEQ)).astype(jnp.int32)
    routes_keys = jax.random.split(jax.random.fold_in(splits[2], 1), MB * NSEQ * SEQ // TOK_DEV)
    routes_turns = jax.random.permutation(jax.random.fold_in(splits[2], 3), MB * NSEQ * SEQ // TOK_DEV)
    routes = jax.vmap(lambda own, number: assign_block(jax.random.fold_in(splits[2], 2), own, number, TOK_DEV, EXPERTS, 1, CAP, 2))(routes_keys, routes_turns).reshape((MB, NSEQ, SEQ, 1))
    buckets = touch_ends(jax.random.randint(splits[3], (2 * SEQ - 1,), 0, NBUCK), jax.random.fold_in(splits[3], 1), 0, NBUCK - 1).astype(jnp.int32)
    gain_attn = jnp.clip(1.0 + 0.1 * jax.random.normal(splits[4], (D,), jnp.float32), 0.5, 1.5)
    w_qkv = centred(splits[5], (D, 3, D), (4 * D) ** -0.5, 0.109375, ((0, 8), (2, 4)))
    w_out = centred(splits[6], (D, D), (D // 64) ** -0.5, 1.75, ((0, 4), (1, 8)))
    rel_table = centred(splits[7], (NBUCK, HEADS), 1.0, 4.0, ((1, 4),), jnp.float32)
    gain_ffn = jnp.clip(1.0 + 0.1 * jax.random.normal(splits[8], (D,), jnp.float32), 0.5, 1.5)
    router = centred(splits[9], (D, EXPERTS), (4 * D) ** -0.5, 0.109375, (), jnp.float32)
    w_in = centred(splits[10], (EXPERTS, D, FF), D ** -0.5, 0.21875, ((0, 16), (1, 2)))
    w_down = centred(splits[11], (EXPERTS, FF, D), 1.25, 7.5, ((0, 16), (2, 2)))
    cotangent = centred(splits[12], (MB, NSEQ, SEQ, D), 1.0, 6.0, ((1, 8), (2, 4)))
    return {"tokens": tokens, "segments": segments, "routes": routes, "buckets": buckets, "gain_attn": gain_attn, "w_qkv": w_qkv, "w_out": w_out, "rel_table": rel_table, "gain_ffn": gain_ffn, "router": router, "w_in": w_in, "w_down": w_down, "cotangent": cotangent}


EPSILON = 1e-06
HIGHEST = lax.Precision.HIGHEST
MASKED = -1000000000.0

@jax.custom_vjp
def low(v):
    return lax.optimization_barrier(v.astype(jnp.bfloat16)).astype(jnp.float32)

@jax.custom_vjp
def low_back(v):
    return v

def low_keep(v):
    return (low(v), None)

def low_pass(kept, grad):
    return (grad,)

def back_keep(v):
    return (v, None)

def back_low(kept, grad):
    return (low(grad),)
low.defvjp(low_keep, low_pass)
low_back.defvjp(back_keep, back_low)

def rms_scale(values, gain_vec):
    return values * lax.rsqrt(lax.optimization_barrier(jnp.mean(values * values, axis=-1, keepdims=True)) + EPSILON) * gain_vec

def attention_rows(packed, marks, gain_attn, w_qkv, w_out, offsets_bias):
    groups = packed.shape[0]
    normed = low(rms_scale(packed, gain_attn))
    joined = low_back(low(jnp.einsum('gtd,dcf->gtcf', normed, w_qkv, precision=HIGHEST)))
    queries = joined[:, :, 0].reshape(groups, SEQ, HEADS, HEAD_DIM)
    key_rows = joined[:, :, 1].reshape(groups, SEQ, HEADS, HEAD_DIM)
    value_rows = joined[:, :, 2].reshape(groups, SEQ, HEADS, HEAD_DIM)
    scores = jnp.einsum('gqhd,gkhd->ghqk', queries, key_rows, precision=HIGHEST) + offsets_bias[None]
    same_doc = marks[:, :, None] == marks[:, None, :]
    scores = low_back(jnp.where(same_doc[:, None], scores, MASKED))
    weights = low(jax.nn.softmax(scores, axis=-1))
    mixed = jnp.einsum('ghqk,gkhd->gqhd', weights, value_rows, precision=HIGHEST).reshape(groups, SEQ, D)
    mixed = low_back(low(mixed))
    return packed + low_back(jnp.einsum('gtf,fe->gte', mixed, w_out, precision=HIGHEST))

def experts_part(hidden, routes, gain_ffn, router, w_in, w_down):
    flat_hidden = hidden.reshape(-1, D)
    normed = rms_scale(flat_hidden, gain_ffn)
    logits = jnp.dot(normed, router, precision=HIGHEST)
    chances = jax.nn.softmax(logits, axis=-1)
    chosen = routes.reshape(-1).astype(jnp.int32)
    picked = chosen[:, None] == jnp.arange(EXPERTS, dtype=jnp.int32)[None, :]
    gate_value = lax.optimization_barrier(jnp.sum(jnp.where(picked, chances, 0.0), axis=-1))
    blocks = chosen.shape[0] // TOK_DEV
    by_block = picked.reshape(blocks, TOK_DEV, EXPERTS).astype(jnp.int32)
    ranks = lax.optimization_barrier(jnp.sum((jnp.cumsum(by_block, axis=1) - by_block) * by_block, axis=-1)).reshape(-1).astype(jnp.int32)
    block_ids = (jnp.arange(chosen.shape[0], dtype=jnp.int32) // TOK_DEV).astype(jnp.int32)
    target = (chosen * (blocks * CAP) + block_ids * CAP + ranks).astype(jnp.int32)
    sent = low_back(low(normed))
    slots = jnp.zeros((EXPERTS * blocks * CAP, D), jnp.float32).at[target].set(sent)

    def one_expert(item):
        arrived, weight_in, weight_down = item
        before = low_back(jnp.dot(arrived, weight_in, precision=HIGHEST))
        active = low(jax.nn.gelu(before, approximate=True))
        return low_back(low(jnp.dot(active, weight_down, precision=HIGHEST)))
    results = lax.map(jax.checkpoint(one_expert), (slots.reshape(EXPERTS, blocks * CAP, D), w_in, w_down))
    returned = results.reshape(-1, D)[target]
    return (flat_hidden + gate_value[:, None] * returned).reshape(hidden.shape)

def reference(tokens, segments, routes, buckets, gain_attn, w_qkv, w_out, rel_table, gain_ffn, router, w_in, w_down, cotangent):
    positions = jnp.arange(SEQ, dtype=jnp.int32)
    bucket_grid = buckets[(positions[None, :] - positions[:, None] + SEQ - 1).astype(jnp.int32)]
    rows_all = MB * NSEQ
    group_size = math.gcd(rows_all, 4)

    def layer_forward(inputs, gain_a, weight_qkv, weight_out, table, gain_f, router_w, weight_in, weight_down):
        offsets_bias = jnp.transpose(table[bucket_grid], (2, 0, 1))
        packed = inputs.reshape(rows_all // group_size, group_size, SEQ, D)
        marks = segments.reshape(rows_all // group_size, group_size, SEQ)

        def one_group(item):
            return attention_rows(item[0], item[1], gain_a, weight_qkv, weight_out, offsets_bias)
        hidden = lax.map(jax.checkpoint(one_group), (packed, marks))
        return experts_part(hidden.reshape(inputs.shape), routes, gain_f, router_w, weight_in, weight_down)
    result, pull_back = jax.vjp(layer_forward, tokens.astype(jnp.float32), gain_attn, w_qkv.astype(jnp.float32), w_out.astype(jnp.float32), rel_table, gain_ffn, router, w_in.astype(jnp.float32), w_down.astype(jnp.float32))
    grads = pull_back(cotangent.astype(jnp.float32))
    return (result.astype(jnp.bfloat16), grads[0], grads[1], grads[2], grads[3], grads[4], grads[5], grads[6], grads[7], grads[8])
```

```python
import functools
import types

import jax
import jax.numpy as jnp
from jax import lax
from jax.experimental import pallas as pl
from jax.experimental.pallas import tpu as pltpu
from jax.sharding import PartitionSpec as P

EPSILON = 1e-06
HIGHEST = lax.Precision.HIGHEST
MASKED = -1000000000.0
MESH = pl.DeviceIdType.MESH
F32 = jnp.float32
BF16 = jnp.bfloat16
NN = (((1,), (0,)), ((), ()))
NT = (((1,), (1,)), ((), ()))
TN = (((0,), (0,)), ((), ()))
PAIRS = 192


def mm(left, right, dims=NN, precision=None):
    return lax.dot_general(left, right, dims, precision=precision, preferred_element_type=F32)


def rows(first, count):
    return pl.ds(pl.multiple_of(first, count), count)


class Links:
    def __init__(self, send_sem, recv_sem):
        self.send_sem, self.recv_sem, self.used, self.started = send_sem, recv_sem, 0, []

    def send(self, src, dst, device):
        k = self.used
        self.used += 1
        copy = pltpu.make_async_remote_copy(
            src_ref=src, dst_ref=dst, send_sem=self.send_sem.at[k], recv_sem=self.recv_sem.at[k],
            device_id=device, device_id_type=MESH,
        )
        copy.start()
        self.started.append(copy)
        return copy

    def finish(self):
        for copy in self.started:
            copy.wait_send()


class Place:
    def __init__(self, z):
        self.dp, self.row, self.col = lax.axis_index("dp"), lax.axis_index("row"), lax.axis_index("col")
        dp, row, col = self.dp, self.row, self.col
        self.dps = [lax.rem(dp + i, z.ndp) for i in range(z.ndp)]
        self.rws = [lax.rem(row + i, z.nrow) for i in range(z.nrow)]
        self.cls = [lax.rem(col + i, z.ncol) for i in range(z.ncol)]
        self.dps_back = [lax.rem(dp + z.ndp - i, z.ndp) for i in range(z.ndp)]
        self.rws_back = [lax.rem(row + z.nrow - i, z.nrow) for i in range(z.nrow)]
        self.cls_back = [lax.rem(col + z.ncol - i, z.ncol) for i in range(z.ncol)]
        self.across = lax.rem(col + 2, z.ncol)
        self.beside = col + 1 - 2 * lax.rem(col, 2)
        self.far = lax.rem(self.beside + 2, z.ncol)


def greet(devices):
    barrier = pltpu.get_barrier_semaphore()
    for device in devices:
        pl.semaphore_signal(barrier, inc=1, device_id=device, device_id_type=MESH)
    return lambda: pl.semaphore_wait(barrier, len(devices))


def norm_rows(values):
    return lax.rsqrt(jnp.mean(values * values, axis=-1, keepdims=True) + EPSILON)


def make_bias(z, rb, rel, bias):
    ids = lax.broadcasted_iota(jnp.int32, (z.nbuck, 2 * z.length), 0)
    table = (ids == rb[...]).astype(F32)
    offsets = mm(rel[...], table, TN, HIGHEST)
    for h in range(z.heads):
        spread = jnp.broadcast_to(offsets[h : h + 1, :], (z.length, 2 * z.length))
        turned = pltpu.roll(spread, z.length + 1, 1, stride=1, stride_axis=0)
        bias[h] = turned[:, : z.length]


def routing(z, chosen):
    ids = lax.broadcasted_iota(jnp.int32, (z.tok, z.experts), 1)
    picked = chosen == ids
    before = (
        lax.broadcasted_iota(jnp.int32, (z.tok, z.tok), 0) > lax.broadcasted_iota(jnp.int32, (z.tok, z.tok), 1)
    ).astype(BF16)
    counts = mm(before, picked.astype(BF16))
    ranks = jnp.sum(jnp.where(picked, counts, 0.0), axis=1, keepdims=True).astype(jnp.int32)
    slot = chosen * z.slots_each + ranks
    placement = (slot == lax.broadcasted_iota(jnp.int32, (z.tok, z.slots), 1)).astype(BF16)
    return picked, placement


def softmax_rows(logits):
    top = jnp.exp(logits - jnp.max(logits, axis=-1, keepdims=True))
    return top / jnp.sum(top, axis=-1, keepdims=True)


def attention_forward(z, m, qkv_t, seg_r, seg_c, bias, lse, mix):
    same = seg_c[m] == seg_r[m]
    parts = []
    for h in range(z.heads):
        q_t, k_t, v_t = (qkv_t[m, pl.ds((c + 1) * z.width + h * z.head, z.head), :] for c in range(3))
        scores = jnp.where(same, mm(k_t, q_t, TN) + bias[h], MASKED)
        highest = jnp.max(scores, axis=0, keepdims=True)
        raised = jnp.exp(scores - highest)
        total = jnp.sum(raised, axis=0, keepdims=True)
        lse[m, pl.ds(h, 1), :] = highest + jnp.log(total)
        probs = (raised * (1.0 / total)).astype(BF16)
        parts.append(mm(v_t, probs))
    mixed = jnp.concatenate(parts, axis=0).T.astype(BF16)
    for c in range(z.ncol):
        mix[m, c] = mixed[c * z.tok : (c + 1) * z.tok]


def kernel_one(z, tok, seg_r, seg_c, rb, rel, gain, dense_in, gain_ffn, router, routes, cot, w_in, w_down,
               nrm, qkv_t, lse, mix, hidden, slots, dense, wi, wd,
               bias, wo_all, mown, send_sem, recv_sem, here_sem):
    me = Place(z)
    dp, row, col = me.dp, me.row, me.col
    links = Links(send_sem, recv_sem)
    arrived = greet(
        [(dp, row, c) for c in me.cls[1:]] + [(d, row, col) for d in me.dps[1:]] + [(dp, r, col) for r in me.rws[1:]]
    )
    for m in range(z.micro):
        values = tok[m].astype(F32)
        nrm[m, rows(col * z.tok, z.tok), :] = (values * norm_rows(values) * gain[...]).astype(BF16)
    own = [
        pltpu.make_async_copy(w_in.at[:, rows(row * z.ffh, z.ffh)], wi.at[rows(row * z.dr, z.dr), :], here_sem.at[0]),
        pltpu.make_async_copy(w_down.at[rows(row * z.ffh, z.ffh), :], wd.at[row], here_sem.at[1]),
    ]
    for copy in own:
        copy.start()
    arrived()
    block = lambda m, c: nrm.at[m, rows(c * z.tok, z.tok), :]
    xs = [links.send(block(m, col), block(m, col), (dp, row, me.across)) for m in range(z.micro)]
    cs = [links.send(block(m, col), block(m, col), (dp, row, me.beside)) for m in range(z.micro)]
    piece = lambda p: dense.at[rows(p * z.piece, z.piece), :]
    dense_y = []
    if z.gather:
        pid = dp * z.nrow + row
        dense[rows(pid * z.piece, z.piece), :] = dense_in[...]
        dense_z = [links.send(piece(pid), piece(pid), (d, row, col)) for d in me.dps[1:]]
        dense_y = [links.send(piece(pid), piece(pid), (dp, r, col)) for r in me.rws[1:]]
    else:
        dense[...] = dense_in[...]
    make_bias(z, rb, rel, bias)
    fs = []
    for m in range(z.micro):
        xs[m].wait_recv()
        fs.append(links.send(block(m, me.across), block(m, me.across), (dp, row, me.beside)))
    if z.gather:
        for i, copy in enumerate(dense_z):
            copy.wait_recv()
            pid = me.dps_back[i + 1] * z.nrow + row
            dense_y += [links.send(piece(pid), piece(pid), (dp, r, col)) for r in me.rws[1:]]
    experts = []
    for r in me.rws[1:]:
        experts.append(links.send(w_in.at[:, rows(r * z.ffh, z.ffh)], wi.at[rows(row * z.dr, z.dr), :], (dp, r, col)))
        experts.append(links.send(w_down.at[rows(r * z.ffh, z.ffh), :], wd.at[row], (dp, r, col)))
    for copy in dense_y + cs + fs:
        copy.wait_recv()
    wo_all[col] = dense[:, : z.width]
    wx = links.send(wo_all.at[col], wo_all.at[col], (dp, row, me.across))
    wc = links.send(wo_all.at[col], wo_all.at[col], (dp, row, me.beside))
    swaps = []
    for m in range(z.micro):
        qkv_t[m] = mm(nrm[m], dense[...]).astype(BF16).T
        attention_forward(z, m, qkv_t, seg_r, seg_c, bias, lse, mix)
        swaps.append([links.send(mix.at[m, c], mown.at[m, col], (dp, row, c)) for c in me.cls[1:]])
        mown[m, col] = mix[m, col]
        if m == 0:
            wx.wait_recv()
            wf = links.send(wo_all.at[me.across], wo_all.at[me.across], (dp, row, me.beside))
    wc.wait_recv()
    wf.wait_recv()
    for m in range(z.micro):
        for copy in swaps[m]:
            copy.wait_recv()
        values = tok[m].astype(F32)
        for c in range(z.ncol):
            values = values + mm(mown[m, c], wo_all[c], NT)
        hidden[m] = values
        normed = values * norm_rows(values) * gain_ffn[...]
        chances = softmax_rows(mm(normed, router[...], NN, HIGHEST))
        picked, placement = routing(z, routes[m])
        gate = jnp.sum(jnp.where(picked, chances, 0.0), axis=-1, keepdims=True)
        sent = jnp.concatenate([normed.astype(BF16), (gate * cot[m].astype(F32)).astype(BF16)], axis=1)
        slots[m] = mm(placement, sent, TN).astype(BF16)
    for copy in own:
        copy.wait()
    for copy in experts:
        copy.wait_recv()
    links.finish()


def gelu_both(before):
    inner = 0.7978845608 * (before + 0.044715 * before * before * before)
    t = jnp.tanh(inner)
    half = 0.5 * (1.0 + t)
    slope = half + 0.5 * before * (1.0 - t * t) * (0.7978845608 * (1.0 + 3.0 * 0.044715 * before * before))
    return before * half, slope


def kernel_two(z, slots, wi_h, wd_h, ret, gwi, gwd,
               wi, wd, arr, own_part, psend, precv, back, act, gpre, xt, send_sem, recv_sem, here_sem):
    me = Place(z)
    dp, row, col = me.dp, me.row, me.col
    links = Links(send_sem, recv_sem)
    plane = [(i, j) for i in range(z.ndp) for j in range(z.ncol) if (i, j) != (0, 0)]
    arrived = greet([(me.dps[i], row, me.cls[j]) for i, j in plane] + [(dp, r, col) for r in me.rws[1:]])
    loads = [
        pltpu.make_async_copy(wi_h, wi, here_sem.at[0]),
        pltpu.make_async_copy(wd_h, wd, here_sem.at[1]),
    ]
    for copy in loads:
        copy.start()
    arrived()
    mine = dp * z.ncol + col
    each = z.slots_each
    dispatch = []
    for m in range(z.micro):
        copies = {}
        for i, j in plane[::-1]:
            e = me.dps[i] * z.ncol + me.cls[j]
            copies[i, j] = links.send(
                slots.at[m, rows(e * each, each), :], arr.at[m, row, rows(mine * each, each), :], (me.dps[i], row, me.cls[j])
            )
        dispatch.append(copies)
        arr[m, row, rows(mine * each, each), :] = slots[m, rows(mine * each, each), :]
    group = z.ncol * each
    for copy in loads:
        copy.wait()
    returns = []

    def expert(m, r, store):
        x = arr[m, r, :, : z.d]
        g = arr[m, r, :, z.d :]
        chunk = z.chunk
        result = jnp.zeros((z.slots, z.d), F32)
        sent = jnp.zeros((z.slots, z.d), F32)
        for k in range(z.ffh // chunk):
            cut = pl.ds(k * chunk, chunk)
            w = wi[:, cut]
            v = jnp.concatenate([wd[p, cut, :] for p in range(z.nrow)], axis=1)
            value, slope = gelu_both(mm(x, w))
            value = value.astype(BF16)
            act[m, r, :, cut] = value
            result = result + mm(value, v)
            pre = (mm(g, v, NT) * slope).astype(BF16)
            gpre[m, r, :, cut] = pre
            sent = sent + mm(pre, w, NT)
        store(result, sent)

    def store_own(result, sent):
        own_part[:, : z.d] = result
        own_part[:, z.d :] = sent

    for m in range(z.micro):
        forwards = {}
        for i in range(z.ndp):
            for j in range(z.ncol):
                if (i, j) != (0, 0):
                    dispatch[m][i, j].wait_recv()
            part = arr.at[m, row, rows(me.dps_back[i] * group, group), :]
            for s, r in enumerate(me.rws[1:]):
                forwards[i, s] = links.send(part, part, (dp, r, col))
        expert(m, row, store_own)
        for s in range(z.nrow - 1):
            for i in range(z.ndp):
                forwards[i, s].wait_recv()
        partials = []
        for s, r in enumerate(me.rws[1:]):

            def store(result, sent, s=s):
                psend[m, s, :, : z.d] = result.astype(BF16)
                psend[m, s, :, z.d :] = sent.astype(BF16)

            expert(m, r, store)
            partials.append(links.send(psend.at[m, s], precv.at[m, s], (dp, r, col)))
        total = own_part[...]
        for s in range(z.nrow - 1):
            partials[s].wait_recv()
            total = total + precv[m, s].astype(F32)
        back[m] = total.astype(BF16)
        home = []
        for i, j in plane[::-1]:
            e = me.dps[i] * z.ncol + me.cls[j]
            home.append(
                links.send(
                    back.at[m, rows(e * each, each), :], ret.at[m, rows(mine * each, each), :], (me.dps[i], row, me.cls[j])
                )
            )
        ret[m, rows(mine * each, each), :] = back[m, rows(mine * each, each), :]
        returns += home
    blocks = [(m, r) for m in range(z.micro) for r in range(z.nrow)]
    for b, (m, r) in enumerate(blocks):
        xt[:, b * z.slots : (b + 1) * z.slots] = arr[m, r, :, : z.d].T
    chunk = z.chunk
    for k in range(z.ffh // chunk):
        cut = pl.ds(k * chunk, chunk)
        pre = jnp.concatenate([gpre[m, r, :, cut] for m, r in blocks], axis=0)
        value = jnp.concatenate([act[m, r, :, cut] for m, r in blocks], axis=0)
        g = jnp.concatenate([arr[m, r, :, z.d :] for m, r in blocks], axis=0)
        grad_in = mm(xt[...], pre).astype(BF16)
        grad_down = mm(value, g, TN).astype(BF16)
        for p in range(z.nrow):
            gwi[p, :, cut] = grad_in[p * z.dr : (p + 1) * z.dr]
            gwd[p, cut, :] = grad_down[:, p * z.dr : (p + 1) * z.dr]
    for copy in returns:
        copy.wait_recv()
    links.finish()


def norm_back(grad_into, values, factor, gain_vec):
    scaled = grad_into * gain_vec
    inner = jnp.mean(scaled * values, axis=-1, keepdims=True)
    return (
        factor * (scaled - values * factor * factor * inner),
        jnp.sum(grad_into * values * factor, axis=0, keepdims=True),
    )


def partner(index, step):
    return index + step - 2 * step * lax.rem(index // step, 2)


def reduce_all(z, me, links, buf, got, finish):
    dp, row, col = me.dp, me.row, me.col
    stages = []
    for size, place in ((z.ndp, lambda s: (partner(dp, s), row, col)), (z.nrow, lambda s: (dp, partner(row, s), col)),
                        (z.ncol, lambda s: (dp, row, partner(col, s)))):
        step = 1
        while step < size:
            stages.append(place(step))
            step *= 2
    for k, device in enumerate(stages):
        copy = links.send(buf.at[k], got.at[k], device)
        yield
        copy.wait_recv()
        buf[k + 1] = buf[k] + got[k]
        finish(k + 1)


def gather_offsets(values):
    count = values.shape[0] // 2
    while count >= 1:
        values = pltpu.roll(values[:count], count, 1) + values[count:]
        count //= 2
    return values


def attention_backward(z, m, qkv_t, seg_r, seg_c, bias, lse, grad_t, gsum, gj_t):
    same = seg_c[m] == seg_r[m]
    for h in range(z.heads):
        q_t, k_t, v_t = (qkv_t[m, pl.ds((c + 1) * z.width + h * z.head, z.head), :] for c in range(3))
        g_t = grad_t[h * z.head : (h + 1) * z.head, :]
        scores = jnp.where(same, mm(k_t, q_t, TN) + bias[h], MASKED)
        probs = jnp.exp(scores - lse[m, pl.ds(h, 1), :])
        grad_probs = mm(v_t, g_t, TN)
        delta = jnp.sum(probs * grad_probs, axis=0, keepdims=True)
        grads = (probs * (grad_probs - delta)).astype(BF16)
        if m == 0:
            gsum[h] = grads.astype(F32)
        else:
            gsum[h] = gsum[h] + grads.astype(F32)
        for c, part in enumerate((mm(k_t, grads), mm(q_t, grads, NT), mm(g_t, probs.astype(BF16), NT))):
            gj_t[pl.ds((c + 1) * z.width + h * z.head, z.head), :] = part.astype(BF16)


def kernel_three(z, ret, routes, hidden, tok, cot, nrm, qkv_t, lse, mix, dense, gain, gain_ffn, router, seg_r, seg_c, rb, rel,
                 gwi, gwd,
                 layer_out, grad_tok, grad_dense, small, late, gwi_r, gwd_r,
                 bias, pc, gh, gsum, gj_t, gdf, pb, pr, px, xsum, ds, yr, zs, zr, ebuf, egot, lbuf, lgot, keep,
                 send_sem, recv_sem, here_sem):
    me = Place(z)
    dp, row, col = me.dp, me.row, me.col
    links = Links(send_sem, recv_sem)
    arrived = greet(
        [(dp, row, c) for c in me.cls[1:]] + [(d, row, col) for d in me.dps[1:]] + [(dp, r, col) for r in me.rws[1:]]
    )
    own = [pltpu.make_async_copy(gwi.at[row], gwi_r.at[row], here_sem.at[0]),
           pltpu.make_async_copy(gwd.at[row], gwd_r.at[row], here_sem.at[1])]
    for copy in own:
        copy.start()
    arrived()
    experts = []
    for r in me.rws[1:]:
        experts.append(links.send(gwi.at[r], gwi_r.at[row], (dp, r, col)))
        experts.append(links.send(gwd.at[r], gwd_r.at[row], (dp, r, col)))
    gain_two = jnp.zeros((1, z.d), F32)
    router_t = jnp.zeros((z.experts, z.d), F32)
    pcs = []
    for m in range(z.micro):
        values = hidden[m]
        factor = norm_rows(values)
        normed = values * factor * gain_ffn[...]
        chances = softmax_rows(mm(normed, router[...], NN, HIGHEST))
        picked, placement = routing(z, routes[m])
        gate = jnp.sum(jnp.where(picked, chances, 0.0), axis=-1, keepdims=True)
        came = mm(placement, ret[m])
        returned, grad_sent = came[:, : z.d], came[:, z.d :]
        layer_out[m] = (values + gate * returned).astype(BF16)
        upstream = cot[m].astype(F32)
        grad_gate = jnp.sum(upstream * returned, axis=-1, keepdims=True)
        grad_logits = grad_gate * gate * (picked.astype(F32) - chances)
        router_t = router_t + mm(grad_logits, normed, TN, HIGHEST)
        grad_normed = grad_sent + mm(grad_logits, router[...], NT, HIGHEST)
        part, gain_part = norm_back(grad_normed, values, factor, gain_ffn[...])
        gain_two = gain_two + gain_part
        grad_hidden = upstream + part
        gh[m] = grad_hidden
        pc[m, col] = grad_hidden.astype(BF16)
        pcs.append([links.send(pc.at[m, col], pc.at[m, col], (dp, row, c)) for c in (me.across, me.beside)])
    ebuf[0] = jnp.concatenate([router_t, gain_two, jnp.zeros((7, z.d), F32)], axis=0)

    def early_done(k):
        pass

    early = reduce_all(z, me, links, ebuf, egot, early_done)
    step = lambda run: next(run, None)
    step(early)
    make_bias(z, rb, rel, bias)
    for m in range(z.micro):
        pcs[m][0].wait_recv()
        pcs[m].append(links.send(pc.at[m, me.across], pc.at[m, me.across], (dp, row, me.beside)))
    grads_one = []
    wire = []
    for m in range(z.micro):
        pcs[m][1].wait_recv()
        pcs[m][2].wait_recv()
        piece = pc[m].reshape(z.length, z.d)
        grad_mixed = mm(piece, dense[:, : z.width]).astype(BF16)
        step(early)
        gj_t[: z.width, :] = jnp.zeros((z.width, z.length), BF16)
        attention_backward(z, m, qkv_t, seg_r, seg_c, bias, lse, grad_mixed.T, gsum, gj_t)
        step(early)
        gj = gj_t[...].T
        partial = mm(gj, dense[...], NT).astype(BF16)
        for c in range(z.ncol):
            pb[m, c] = partial[c * z.tok : (c + 1) * z.tok]
        wire.append([links.send(pb.at[m, me.beside], pr.at[m, 0], (dp, row, me.beside)),
                     links.send(pb.at[m, me.far], pr.at[m, 1], (dp, row, me.beside))])
        step(early)
        total = mm(nrm[m], gj, TN)
        out_part = mm(piece, mix[m].reshape(z.length, z.width), TN)
        if m == 0:
            gdf[...] = total
            gdf[:, : z.width] = out_part
        else:
            gdf[...] = gdf[...] + total
            gdf[:, : z.width] = gdf[:, : z.width] + out_part
        wire[m][1].wait_recv()
        xsum[m] = (pb[m, me.across].astype(F32) + pr[m, 1].astype(F32)).astype(BF16)
        wire[m].append(links.send(xsum.at[m], px.at[m], (dp, row, me.across)))
    block = lambda d, r: gdf[rows((d * z.nrow + r) * z.piece, z.piece), :]
    ys = []
    for s, r in enumerate(me.rws[1:]):
        for i, d in enumerate(me.dps):
            ds[s, i] = block(d, r).astype(BF16)
        ys.append(links.send(ds.at[s], yr.at[s], (dp, r, col)))
    offsets = jnp.concatenate([
        gather_offsets(jnp.concatenate([gsum[h], jnp.zeros((z.length, z.length), F32)], axis=1)) for h in range(z.heads)
    ], axis=0)
    ids = lax.broadcasted_iota(jnp.int32, (z.nbuck, 2 * z.length), 0)
    table = (ids == rb[...]).astype(F32)
    grad_rel = mm(offsets, table, NT, HIGHEST)
    gain_one = jnp.zeros((1, z.d), F32)
    for m in range(z.micro):
        wire[m][0].wait_recv()
        wire[m][2].wait_recv()
        grad_normed = pb[m, col].astype(F32) + pr[m, 0].astype(F32) + px[m].astype(F32)
        values = tok[m].astype(F32)
        part, gain_part = norm_back(grad_normed, values, norm_rows(values), gain[...])
        gain_one = gain_one + gain_part
        grad_tok[m] = gh[m] + part
    lbuf[0, pl.ds(0, 1), :] = gain_one
    lbuf[0, pl.ds(1, 7), :] = jnp.zeros((7, z.d), F32)
    lbuf[0, pl.ds(1, z.heads), : z.nbuck] = grad_rel
    inner = (z.ndp * z.nrow).bit_length() - 1

    def late_done(k):
        if k == inner:
            keep[...] = lbuf[k]

    final = reduce_all(z, me, links, lbuf, lgot, late_done)
    step(final)
    for copy in ys:
        copy.wait_recv()
    zsent = []
    for i, d in enumerate(me.dps):
        total = block(d, row)
        for s in range(z.nrow - 1):
            total = total + yr[s, i].astype(F32)
        if i == 0:
            mine = total
        else:
            zs[i - 1] = total.astype(BF16)
            zsent.append(links.send(zs.at[i - 1], zr.at[i - 1], (d, row, col)))
    step(final)
    step(early)
    for copy in zsent:
        copy.wait_recv()
    for i in range(z.ndp - 1):
        mine = mine + zr[i].astype(F32)
    grad_dense[...] = mine
    for run in (early, final):
        for _ in run:
            pass
    stages = (z.ndp * z.nrow * z.ncol).bit_length() - 1
    small[...] = ebuf[stages]
    late[...] = keep[...]
    late[pl.ds(0, 1), :] = lbuf[stages, pl.ds(0, 1), :]
    for copy in own:
        copy.wait()
    for copy in experts:
        copy.wait_recv()
    links.finish()


def sizes(mesh_shape, tokens, segments, buckets, rel_table, w_in, router):
    z = types.SimpleNamespace()
    z.ndp, z.nrow, z.ncol = mesh_shape
    z.micro, z.tok, z.d = tokens.shape[0], tokens.shape[2], tokens.shape[3]
    z.length = segments.shape[2]
    z.nbuck, z.heads = rel_table.shape
    z.width = z.d // z.ncol
    z.head = z.width // z.heads
    z.ff = w_in.shape[2]
    z.ffh, z.dr = z.ff // z.nrow, z.d // z.nrow
    z.experts = router.shape[1]
    z.slots_each = max(2, 2 * z.tok // z.experts)
    z.slots = z.experts * z.slots_each
    z.piece = z.d // (z.ndp * z.nrow)
    z.gather = True
    z.chunk = min(512, z.ffh)
    return z


def params(kernel_id):
    return pltpu.CompilerParams(collective_id=kernel_id, has_side_effects=True, vmem_limit_bytes=58 * 2**20)


VM = pl.BlockSpec(memory_space=pltpu.VMEM)
ANY = pl.BlockSpec(memory_space=pl.ANY)


def fast(mesh_shape, tokens, segments, routes, buckets, gain_attn, w_qkv, w_out, rel_table, gain_ffn, router, w_in,
         w_down, cotangent):
    z = sizes(mesh_shape, tokens, segments, buckets, rel_table, w_in, router)
    S = jax.ShapeDtypeStruct
    tok, cot = tokens[:, 0], cotangent[:, 0]
    seg_r = segments
    seg_c = jnp.swapaxes(segments, 1, 2)
    rb = jnp.concatenate([buckets[::-1], jnp.full((1,), -1, jnp.int32)])[None]
    dense_in = jnp.concatenate([w_out.T, w_qkv.reshape(z.piece, -1)], axis=1)
    routes_c = routes[:, 0]
    sem = pltpu.SemaphoreType.DMA
    one = pl.pallas_call(
        functools.partial(kernel_one, z),
        out_shape=[
            S((z.micro, z.length, z.d), BF16),
            S((z.micro, z.d, z.length), BF16),
            S((z.micro, 8, z.length), F32),
            S((z.micro, z.ncol, z.tok, z.width), BF16),
            S((z.micro, z.tok, z.d), F32),
            S((z.micro, z.slots, 2 * z.d), BF16),
            S((z.d, z.d), BF16),
            S((z.d, z.ffh), BF16),
            S((z.nrow, z.ffh, z.dr), BF16),
        ],
        in_specs=[VM] * 11 + [ANY] * 2,
        out_specs=[VM] * 7 + [ANY] * 2,
        scratch_shapes=[
            pltpu.VMEM((z.heads, z.length, z.length), F32),
            pltpu.VMEM((z.ncol, z.d, z.width), BF16),
            pltpu.VMEM((z.micro, z.ncol, z.tok, z.width), BF16),
            sem((64,)),
            sem((64,)),
            sem((4,)),
        ],
        compiler_params=params(1),
        name="attention_forward",
    )
    nrm, qkv_t, lse, mix, hidden, slots, dense, wi, wd = one(
        tok, seg_r, seg_c, rb, rel_table, gain_attn[None], dense_in, gain_ffn[None], router, routes_c, cot, w_in[0], w_down[0]
    )
    two = pl.pallas_call(
        functools.partial(kernel_two, z),
        out_shape=[
            S((z.micro, z.slots, 2 * z.d), BF16),
            S((z.nrow, z.dr, z.ffh), BF16),
            S((z.nrow, z.ffh, z.dr), BF16),
        ],
        in_specs=[VM, ANY, ANY],
        out_specs=[VM] * 3,
        scratch_shapes=[
            pltpu.VMEM((z.d, z.ffh), BF16),
            pltpu.VMEM((z.nrow, z.ffh, z.dr), BF16),
            pltpu.VMEM((z.micro, z.nrow, z.slots, 2 * z.d), BF16),
            pltpu.VMEM((z.slots, 2 * z.d), F32),
            pltpu.VMEM((z.micro, z.nrow - 1, z.slots, 2 * z.d), BF16),
            pltpu.VMEM((z.micro, z.nrow - 1, z.slots, 2 * z.d), BF16),
            pltpu.VMEM((z.micro, z.slots, 2 * z.d), BF16),
            pltpu.VMEM((z.micro, z.nrow, z.slots, z.ffh), BF16),
            pltpu.VMEM((z.micro, z.nrow, z.slots, z.ffh), BF16),
            pltpu.VMEM((z.d, z.micro * z.nrow * z.slots), BF16),
            sem((80,)),
            sem((80,)),
            sem((4,)),
        ],
        compiler_params=params(2),
        name="experts",
    )
    ret, gwi, gwd = two(slots, wi, wd)
    stages = (z.ndp * z.nrow * z.ncol).bit_length()
    three = pl.pallas_call(
        functools.partial(kernel_three, z),
        out_shape=[
            S((z.micro, z.tok, z.d), BF16),
            S((z.micro, z.tok, z.d), F32),
            S((z.piece, z.d), F32),
            S((z.experts + 8, z.d), F32),
            S((8, z.d), F32),
            S((z.nrow, z.dr, z.ffh), BF16),
            S((z.nrow, z.ffh, z.dr), BF16),
        ],
        in_specs=[VM] * 17 + [ANY] * 2,
        out_specs=[VM] * 5 + [ANY] * 2,
        scratch_shapes=[
            pltpu.VMEM((z.heads, z.length, z.length), F32),
            pltpu.VMEM((z.micro, z.ncol, z.tok, z.d), BF16),
            pltpu.VMEM((z.micro, z.tok, z.d), F32),
            pltpu.VMEM((z.heads, z.length, z.length), F32),
            pltpu.VMEM((z.d, z.length), BF16),
            pltpu.VMEM((z.d, z.d), F32),
            pltpu.VMEM((z.micro, z.ncol, z.tok, z.d), BF16),
            pltpu.VMEM((z.micro, 2, z.tok, z.d), BF16),
            pltpu.VMEM((z.micro, z.tok, z.d), BF16),
            pltpu.VMEM((z.micro, z.tok, z.d), BF16),
            pltpu.VMEM((z.nrow - 1, z.ndp, z.piece, z.d), BF16),
            pltpu.VMEM((z.nrow - 1, z.ndp, z.piece, z.d), BF16),
            pltpu.VMEM((z.ndp - 1, z.piece, z.d), BF16),
            pltpu.VMEM((z.ndp - 1, z.piece, z.d), BF16),
            pltpu.VMEM((stages, z.experts + 8, z.d), F32),
            pltpu.VMEM((stages, z.experts + 8, z.d), F32),
            pltpu.VMEM((stages, 8, z.d), F32),
            pltpu.VMEM((stages, 8, z.d), F32),
            pltpu.VMEM((8, z.d), F32),
            sem((64,)),
            sem((64,)),
            sem((4,)),
        ],
        compiler_params=params(3),
        name="attention_backward",
    )
    layer_out, grad_tok, grad_dense, small, late, gwi_r, gwd_r = three(
        ret, routes_c, hidden, tok, cot, nrm, qkv_t, lse, mix, dense, gain_attn[None], gain_ffn[None], router, seg_r, seg_c,
        rb, rel_table, gwi, gwd,
    )
    grad_in = jnp.moveaxis(gwi_r, 0, 1).reshape(z.dr, z.ff).astype(F32)
    grad_down = gwd_r.reshape(z.ff, z.dr).astype(F32)
    return (
        layer_out[:, None],
        grad_tok[:, None],
        late[0],
        grad_dense[:, z.width :].reshape(z.piece, 3, z.width),
        grad_dense[:, : z.width].T,
        late[1 : 1 + z.heads, : z.nbuck].T,
        small[z.experts],
        small[: z.experts].T,
        grad_in[None],
        grad_down[None],
    )


def smooth_act(values):
    return jax.nn.gelu(values, approximate=True)


def plain_normalize(values, gain_vec):
    factor = lax.rsqrt(jnp.mean(values * values, axis=-1, keepdims=True) + EPSILON)
    return (values * factor * gain_vec, factor)


def plain_norm_back(grad_into, values, factor, gain_vec):
    scaled = grad_into * gain_vec
    inner = jnp.mean(scaled * values, axis=-1, keepdims=True)
    return (
        factor * (scaled - values * factor * factor * inner),
        jnp.sum(grad_into * values * factor, axis=0),
    )


def contract_rows(left, right, precision=None):
    return lax.dot_general(
        left,
        right,
        (((0,), (0,)), ((), ())),
        precision=precision,
        preferred_element_type=jnp.float32,
    )


def contract_cols(left, right, precision=None):
    return lax.dot_general(
        left,
        right,
        (((1,), (1,)), ((), ())),
        precision=precision,
        preferred_element_type=jnp.float32,
    )


def spread_rows(offsets, row_first, row_count, length):
    shifted = jnp.roll(offsets, row_first, axis=-1)
    span_width = 2 * length - 1
    tiled_rows = jnp.tile(shifted, (1, row_count))[:, : row_count * span_width]
    return tiled_rows.reshape(offsets.shape[0], row_count, span_width)[:, :, length - 1 :]


def plain_gather_offsets(grads, row_first, length):
    heads_here = grads.shape[0]
    row_count = grads.shape[1]
    span_width = 2 * length - 1
    widened = jnp.pad(grads, ((0, 0), (0, 0), (length - 1, 0)))
    flat_rows = jnp.pad(
        widened.reshape(heads_here, row_count * span_width), ((0, 0), (0, row_count))
    )
    folded = jnp.sum(flat_rows.reshape(heads_here, row_count, 2 * length), axis=1)
    return jnp.roll(folded, -row_first, axis=-1)


def score_block(query_part, key_rows, bias_part, marks_query, marks_keys):
    scores = (
        jnp.einsum("qhd,khd->hqk", query_part, key_rows, preferred_element_type=jnp.float32)
        + bias_part
    )
    same_doc = marks_query[:, None] == marks_keys[None, :]
    return jnp.where(same_doc[None], scores, MASKED)


def fetch_dense(w_qkv, w_out):
    return (
        lax.all_gather(w_qkv, ("dp", "row"), axis=0, tiled=True),
        lax.all_gather(w_out, ("dp", "row"), axis=1, tiled=True),
    )


def fetch_experts(w_in, w_down):
    grown_in, grown_down = (
        lax.all_gather(w_in, "row", axis=1, tiled=True),
        lax.all_gather(w_down, "row", axis=2, tiled=True),
    )
    return (grown_in[0], grown_down[0])


def plain_shards(
    tokens,
    segments,
    routes,
    buckets,
    gain_attn,
    w_qkv,
    w_out,
    rel_table,
    gain_ffn,
    router,
    w_in,
    w_down,
    cotangent,
):
    micro_count = tokens.shape[0]
    tok_rows = tokens.shape[2]
    model_width = tokens.shape[3]
    length = segments.shape[2]
    local_heads = rel_table.shape[1]
    head_size = w_out.shape[0] // local_heads
    local_width = local_heads * head_size
    experts_all = router.shape[1]
    hidden_units = w_in.shape[2]
    capacity = max(2, 2 * tok_rows // experts_all)
    query_block = min(512, length)
    block_starts = list(range(0, length, query_block))
    padded_ids = jnp.concatenate([buckets, jnp.full((1,), -1, jnp.int32)])
    offset_table = (
        padded_ids[:, None] == jnp.arange(rel_table.shape[0], dtype=jnp.int32)[None, :]
    ).astype(jnp.float32)
    offset_bias = jnp.dot(offset_table, rel_table, precision=HIGHEST).T
    block_bias = [
        spread_rows(offset_bias, row_start, query_block, length) for row_start in block_starts
    ]
    expert_ids = jnp.arange(experts_all, dtype=jnp.int32)
    slot_ids = jnp.arange(experts_all * capacity, dtype=jnp.int32)
    saved = []
    outputs = []
    for micro_index in range(micro_count):
        full_qkv, full_out = fetch_dense(w_qkv, w_out)
        full_in, full_down = fetch_experts(w_in, w_down)
        own_rows = tokens[micro_index, 0].astype(jnp.float32)
        whole_rows = lax.all_gather(tokens[micro_index, 0], "col", axis=0, tiled=True).astype(
            jnp.float32
        )
        normed_one = plain_normalize(whole_rows, gain_attn)[0].astype(jnp.bfloat16)
        joined = jnp.einsum(
            "td,dcf->tcf", normed_one, full_qkv, preferred_element_type=jnp.float32
        ).astype(jnp.bfloat16)
        queries = joined[:, 0].reshape(length, local_heads, head_size)
        key_rows = joined[:, 1].reshape(length, local_heads, head_size)
        value_rows = joined[:, 2].reshape(length, local_heads, head_size)
        marks = segments[micro_index, 0]
        mixed_parts = []
        log_sums = []
        for block_index, row_start in enumerate(block_starts):
            scores = score_block(queries, key_rows, block_bias[block_index], marks, marks)
            highest = jnp.max(scores, axis=-1, keepdims=True)
            log_sum = highest + jnp.log(jnp.sum(jnp.exp(scores - highest), axis=-1, keepdims=True))
            weights = jnp.exp(scores - log_sum).astype(jnp.bfloat16)
            mixed_parts.append(
                jnp.einsum(
                    "hqk,khd->qhd", weights, value_rows, preferred_element_type=jnp.float32
                ).astype(jnp.bfloat16)
            )
            log_sums.append(log_sum)
        mixed = mixed_parts[0].reshape(length, local_width)
        hidden = own_rows + lax.psum_scatter(
            jnp.dot(mixed, full_out, preferred_element_type=jnp.float32),
            "col",
            scatter_dimension=0,
            tiled=True,
        )
        normed_two, factor_two = plain_normalize(hidden, gain_ffn)
        chances = jax.nn.softmax(jnp.dot(normed_two, router, precision=HIGHEST), axis=-1)
        chosen = routes[micro_index, 0, :, 0]
        picked = chosen[:, None] == expert_ids[None, :]
        gate_value = jnp.sum(jnp.where(picked, chances, 0.0), axis=-1)
        picked_int = picked.astype(jnp.int32)
        ranks = jnp.sum((jnp.cumsum(picked_int, axis=0) - picked_int) * picked_int, axis=1)
        placement = ((chosen * capacity + ranks)[:, None] == slot_ids[None, :]).astype(jnp.bfloat16)
        outgoing = contract_rows(placement, normed_two.astype(jnp.bfloat16)).astype(jnp.bfloat16)
        outgoing = outgoing.reshape(experts_all, capacity, model_width)
        arrived = lax.all_to_all(outgoing, ("dp", "col"), split_axis=0, concat_axis=0, tiled=True)
        flat_in = arrived.reshape(-1, model_width)
        before = jnp.dot(flat_in, full_in, preferred_element_type=jnp.float32)
        active = smooth_act(before).astype(jnp.bfloat16)
        result = jnp.dot(active, full_down, preferred_element_type=jnp.float32).astype(jnp.bfloat16)
        sent_back = lax.all_to_all(
            result.reshape(arrived.shape), ("dp", "col"), split_axis=0, concat_axis=0, tiled=True
        )
        sent_back, arrived, before_all = (
            sent_back,
            arrived,
            before.reshape(arrived.shape[0], arrived.shape[1], hidden_units),
        )
        expert_out = jnp.dot(
            placement, sent_back.reshape(-1, model_width), preferred_element_type=jnp.float32
        )
        outputs.append((hidden + gate_value[:, None] * expert_out).astype(jnp.bfloat16))
        saved.append(
            (
                own_rows,
                normed_one,
                queries,
                key_rows,
                value_rows,
                marks,
                log_sums,
                mixed,
                hidden,
                normed_two,
                factor_two,
                chances,
                picked,
                gate_value,
                placement,
                expert_out,
                arrived,
                before_all,
            )
        )
    grad_qkv_sum = jnp.zeros((model_width, 3, local_width), jnp.float32)
    grad_out_sum = jnp.zeros((local_width, model_width), jnp.float32)
    grad_in_sum = jnp.zeros((model_width, hidden_units), jnp.float32)
    grad_down_sum = jnp.zeros((hidden_units, model_width), jnp.float32)
    grad_offsets = jnp.zeros((local_heads, 2 * length), jnp.float32)
    grad_gain_one = jnp.zeros((model_width,), jnp.float32)
    grad_gain_two = jnp.zeros((model_width,), jnp.float32)
    grad_router_sum = jnp.zeros(router.shape, jnp.float32)
    grads_input = []
    for micro_index in range(micro_count):
        (
            own_rows,
            normed_one,
            queries,
            key_rows,
            value_rows,
            marks,
            log_sums,
            mixed,
            hidden,
            normed_two,
            factor_two,
            chances,
            picked,
            gate_value,
            placement,
            expert_out,
            arrived,
            before_all,
        ) = saved[micro_index]
        full_qkv, full_out = fetch_dense(w_qkv, w_out)
        full_in, full_down = fetch_experts(w_in, w_down)
        upstream = cotangent[micro_index, 0].astype(jnp.float32)
        grad_gate = jnp.sum(upstream * expert_out, axis=-1)
        grad_result = (gate_value[:, None] * upstream).astype(jnp.bfloat16)
        to_slots = contract_rows(placement, grad_result).astype(jnp.bfloat16)
        to_slots = to_slots.reshape(experts_all, capacity, model_width)
        at_expert = lax.all_to_all(
            to_slots, ("dp", "col"), split_axis=0, concat_axis=0, tiled=True
        ).reshape(-1, model_width)
        flat_before = before_all.reshape(-1, hidden_units)
        act_value, act_pull = jax.vjp(smooth_act, flat_before)
        flat_active = act_value.astype(jnp.bfloat16)
        grad_down_sum = grad_down_sum + contract_rows(flat_active, at_expert)
        grad_active = contract_cols(at_expert, full_down)
        grad_before = act_pull(grad_active)[0].astype(jnp.bfloat16)
        grad_in_sum = grad_in_sum + contract_rows(arrived.reshape(-1, model_width), grad_before)
        grad_sent = (
            contract_cols(grad_before, full_in)
            .astype(jnp.bfloat16)
            .reshape(experts_all, capacity, model_width)
        )
        came_back = lax.all_to_all(
            grad_sent, ("dp", "col"), split_axis=0, concat_axis=0, tiled=True
        )
        grad_normed_two = jnp.dot(
            placement, came_back.reshape(-1, model_width), preferred_element_type=jnp.float32
        )
        grad_logits = (grad_gate * gate_value)[:, None] * (picked.astype(jnp.float32) - chances)
        grad_router_sum = grad_router_sum + contract_rows(normed_two, grad_logits, HIGHEST)
        grad_normed_two = grad_normed_two + contract_cols(grad_logits, router, HIGHEST)
        grad_norm_part, gain_part = plain_norm_back(grad_normed_two, hidden, factor_two, gain_ffn)
        grad_gain_two = grad_gain_two + gain_part
        grad_hidden = upstream + grad_norm_part
        piece = lax.all_gather(grad_hidden.astype(jnp.bfloat16), "col", axis=0, tiled=True)
        total_out = grad_out_sum
        total_out = total_out + contract_rows(mixed, piece)
        spread_grad = contract_cols(piece, full_out)
        grad_out_sum = total_out
        grad_mixed = spread_grad
        grad_mixed = grad_mixed.astype(jnp.bfloat16).reshape(length, local_heads, head_size)
        grad_keys = jnp.zeros((length, local_heads, head_size), jnp.float32)
        grad_values = jnp.zeros((length, local_heads, head_size), jnp.float32)
        query_grads = []
        for block_index, row_start in enumerate(block_starts):
            scores = score_block(queries, key_rows, block_bias[block_index], marks, marks)
            weights = jnp.exp(scores - log_sums[block_index])
            grad_values = jnp.einsum(
                "hqk,qhd->khd",
                weights.astype(jnp.bfloat16),
                grad_mixed,
                preferred_element_type=jnp.float32,
            )
            grad_weights = jnp.einsum(
                "qhd,khd->hqk", grad_mixed, value_rows, preferred_element_type=jnp.float32
            )
            grad_scores = (
                weights * (grad_weights - jnp.sum(weights * grad_weights, axis=-1, keepdims=True))
            ).astype(jnp.bfloat16)
            grad_offsets = grad_offsets + plain_gather_offsets(
                grad_scores.astype(jnp.float32), row_start, length
            )
            query_grads.append(
                jnp.einsum(
                    "hqk,khd->qhd", grad_scores, key_rows, preferred_element_type=jnp.float32
                )
            )
            grad_keys = jnp.einsum(
                "hqk,qhd->khd", grad_scores, queries, preferred_element_type=jnp.float32
            )
        grad_joined = jnp.stack([query_grads[0], grad_keys, grad_values], axis=1)
        grad_joined = grad_joined.reshape(length, 3, local_width).astype(jnp.bfloat16)
        grad_qkv_sum = grad_qkv_sum + jnp.einsum(
            "td,tcf->dcf", normed_one, grad_joined, preferred_element_type=jnp.float32
        )
        grad_normed_one = lax.psum_scatter(
            jnp.einsum(
                "tcf,dcf->td", grad_joined, full_qkv, preferred_element_type=jnp.float32
            ).astype(jnp.bfloat16),
            "col",
            scatter_dimension=0,
            tiled=True,
        ).astype(jnp.float32)
        factor_one = plain_normalize(own_rows, gain_attn)[1]
        grad_input_part, gain_part = plain_norm_back(grad_normed_one, own_rows, factor_one, gain_attn)
        grad_gain_one = grad_gain_one + gain_part
        grads_input.append(grad_hidden + grad_input_part)
    grad_rel_mine = jnp.dot(offset_table.T, grad_offsets.T, precision=HIGHEST)
    heads_all = local_heads * lax.axis_size("col")
    head_first = lax.axis_index("col") * local_heads
    rel_full = lax.dynamic_update_slice_in_dim(
        jnp.zeros((rel_table.shape[0], heads_all), jnp.float32), grad_rel_mine, head_first, 1
    )
    total_gain_one, total_gain_two, total_router, total_rel = lax.psum(
        (grad_gain_one, grad_gain_two, grad_router_sum, rel_full), ("dp", "row", "col")
    )
    rel_out = lax.dynamic_slice_in_dim(total_rel, head_first, local_heads, 1)
    dense_qkv, dense_out = (
        lax.psum_scatter(grad_qkv_sum, ("dp", "row"), scatter_dimension=0, tiled=True),
        lax.psum_scatter(grad_out_sum, ("dp", "row"), scatter_dimension=1, tiled=True),
    )
    expert_in, expert_down = (
        lax.psum_scatter(
            grad_in_sum[None].astype(jnp.bfloat16), "row", scatter_dimension=1, tiled=True
        ).astype(jnp.float32),
        lax.psum_scatter(
            grad_down_sum[None].astype(jnp.bfloat16), "row", scatter_dimension=2, tiled=True
        ).astype(jnp.float32),
    )
    layer_out = jnp.stack(outputs)[:, None]
    grad_tokens = jnp.stack(grads_input)[:, None]
    return (
        layer_out,
        grad_tokens,
        total_gain_one,
        dense_qkv,
        dense_out,
        rel_out,
        total_gain_two,
        total_router,
        expert_in,
        expert_down,
    )


def solution(mesh):
    shape = tuple(mesh.shape[a] for a in ("dp", "row", "col"))
    token_spec, expert_in, expert_down = P(None, ("dp", "row"), "col", None), P(("dp", "col"), "row", None), P(("dp", "col"), None, "row")
    qkv_spec, out_spec = P(("dp", "row"), None, "col"), P("col", ("dp", "row"))
    in_specs = (
        token_spec, P(None, ("dp", "row"), None), token_spec, P(), P(), qkv_spec, out_spec, P(None, "col"), P(), P(),
        expert_in, expert_down, token_spec,
    )
    out_specs = (token_spec, token_spec, P(), qkv_spec, out_spec, P(None, "col"), P(), P(), expert_in, expert_down)

    def run(*args):
        piece, each = args[5].shape[0] // (shape[0] * shape[1]), 2 * args[0].shape[2] // shape[2] // args[9].shape[1]
        whole_tiles = piece % 16 == 0 and each % 16 == 0 and shape[2] == 4
        body = functools.partial(fast, shape) if whole_tiles else plain_shards
        return jax.shard_map(body, mesh=mesh, in_specs=in_specs, out_specs=out_specs, check_vma=False)(*args)

    return run
```

```python
import functools
import types

import jax
import jax.numpy as jnp
from jax import lax
from jax.experimental import pallas as pl
from jax.experimental.pallas import tpu as pltpu
from jax.sharding import PartitionSpec as P

EPSILON = 1e-06
HIGHEST = lax.Precision.HIGHEST
MASKED = -1000000000.0
MESH = pl.DeviceIdType.MESH
F32 = jnp.float32
BF16 = jnp.bfloat16
NN = (((1,), (0,)), ((), ()))
NT = (((1,), (1,)), ((), ()))
TN = (((0,), (0,)), ((), ()))


def mm(left, right, dims=NN, precision=None):
    return lax.dot_general(left, right, dims, precision=precision, preferred_element_type=F32)


def rows(first, count):
    return pl.ds(pl.multiple_of(first, count), count)


class Links:
    def __init__(self, send_sem, recv_sem):
        self.send_sem, self.recv_sem, self.used, self.started = send_sem, recv_sem, 0, []

    def send(self, src, dst, device):
        k = self.used
        self.used += 1
        copy = pltpu.make_async_remote_copy(
            src_ref=src, dst_ref=dst, send_sem=self.send_sem.at[k], recv_sem=self.recv_sem.at[k],
            device_id=device, device_id_type=MESH,
        )
        copy.start()
        self.started.append(copy)
        return copy

    def finish(self):
        for copy in self.started:
            copy.wait_send()


class Place:
    def __init__(self, z):
        self.dp, self.row, self.col = lax.axis_index("dp"), lax.axis_index("row"), lax.axis_index("col")
        dp, row, col = self.dp, self.row, self.col
        self.dps = [lax.rem(dp + i, z.ndp) for i in range(z.ndp)]
        self.rws = [lax.rem(row + i, z.nrow) for i in range(z.nrow)]
        self.cls = [lax.rem(col + i, z.ncol) for i in range(z.ncol)]
        self.dps_back = [lax.rem(dp + z.ndp - i, z.ndp) for i in range(z.ndp)]
        self.rws_back = [lax.rem(row + z.nrow - i, z.nrow) for i in range(z.nrow)]
        self.cls_back = [lax.rem(col + z.ncol - i, z.ncol) for i in range(z.ncol)]
        self.across = lax.rem(col + 2, z.ncol)
        self.beside = col + 1 - 2 * lax.rem(col, 2)
        self.far = lax.rem(self.beside + 2, z.ncol)


def greet(devices):
    barrier = pltpu.get_barrier_semaphore()
    for device in devices:
        pl.semaphore_signal(barrier, inc=1, device_id=device, device_id_type=MESH)
    return lambda: pl.semaphore_wait(barrier, len(devices))


def norm_rows(values):
    return lax.rsqrt(jnp.mean(values * values, axis=-1, keepdims=True) + EPSILON)


def norm_back(grad_into, values, factor, gain_vec):
    scaled = grad_into * gain_vec
    inner = jnp.mean(scaled * values, axis=-1, keepdims=True)
    return (
        factor * (scaled - values * factor * factor * inner),
        jnp.sum(grad_into * values * factor, axis=0, keepdims=True),
    )


def column(line):
    return jnp.broadcast_to(line.astype(F32), (8, line.shape[1])).T[:, :1]


def offset_table(z, rb):
    ids = lax.broadcasted_iota(jnp.int32, (z.nbuck, 2 * z.length), 0)
    return (ids == rb[...]).astype(F32)


def make_bias(z, rb, rel, bias):
    offsets = mm(rel[...], offset_table(z, rb), NN, HIGHEST)
    for h in range(z.heads):
        spread = jnp.broadcast_to(offsets[h : h + 1, :], (z.length, 2 * z.length))
        turned = pltpu.roll(spread, z.length + 1, 1, stride=1, stride_axis=0)
        bias[h] = turned[:, : z.length]


def gather_offsets(values):
    count = values.shape[0] // 2
    while count >= 1:
        values = pltpu.roll(values[:count], count, 1) + values[count:]
        count //= 2
    return values


def routing(z, chosen):
    ids = lax.broadcasted_iota(jnp.int32, (z.tok, z.experts), 1).astype(F32)
    picked = chosen == ids
    before = (
        lax.broadcasted_iota(jnp.int32, (z.tok, z.tok), 0) > lax.broadcasted_iota(jnp.int32, (z.tok, z.tok), 1)
    ).astype(BF16)
    counts = mm(before, picked.astype(BF16))
    ranks = jnp.sum(jnp.where(picked, counts, 0.0), axis=1, keepdims=True)
    slot = chosen * z.slots_each + ranks
    placement = (slot == lax.broadcasted_iota(jnp.int32, (z.tok, z.slots), 1).astype(F32)).astype(BF16)
    return picked, placement


def softmax_rows(logits):
    top = jnp.exp(logits - jnp.max(logits, axis=-1, keepdims=True))
    return top / jnp.sum(top, axis=-1, keepdims=True)


def gelu_both(before):
    inner = 0.7978845608 * (before + 0.044715 * before * before * before)
    t = jnp.tanh(inner)
    half = 0.5 * (1.0 + t)
    slope = half + 0.5 * before * (1.0 - t * t) * (0.7978845608 * (1.0 + 3.0 * 0.044715 * before * before))
    return before * half, slope


def partner(index, step):
    return index + step - 2 * step * lax.rem(index // step, 2)


def reduce_all(z, me, links, buf, got, finish):
    dp, row, col = me.dp, me.row, me.col
    stages = []
    for size, place in ((z.ndp, lambda s: (partner(dp, s), row, col)), (z.nrow, lambda s: (dp, partner(row, s), col)),
                        (z.ncol, lambda s: (dp, row, partner(col, s)))):
        step = 1
        while step < size:
            stages.append(place(step))
            step *= 2
    for k, device in enumerate(stages):
        copy = links.send(buf.at[k], got.at[k], device)
        yield
        copy.wait_recv()
        buf[k + 1] = buf[k] + got[k]
        finish(k + 1)


def attention_forward(z, r, m):
    seg = r.seg[m]
    same = column(seg) == seg.astype(F32)
    parts = []
    for h in range(z.heads):
        q_t, k_t, v_t = (r.qkv_t[m, pl.ds((c + 1) * z.width + h * z.head, z.head), :] for c in range(3))
        scores = jnp.where(same, mm(k_t, q_t, TN) + r.bias[h], MASKED)
        highest = jnp.max(scores, axis=0, keepdims=True)
        raised = jnp.exp(scores - highest)
        total = jnp.sum(raised, axis=0, keepdims=True)
        r.lse[m, pl.ds(h, 1), :] = highest + jnp.log(total)
        probs = (raised * (1.0 / total)).astype(BF16)
        parts.append(mm(v_t, probs))
    mixed = jnp.concatenate(parts, axis=0).T.astype(BF16)
    for c in range(z.ncol):
        r.mix[m, c] = mixed[c * z.tok : (c + 1) * z.tok]


def attention_backward(z, r, m, grad_t):
    seg = r.seg[m]
    same = column(seg) == seg.astype(F32)
    for h in range(z.heads):
        q_t, k_t, v_t = (r.qkv_t[m, pl.ds((c + 1) * z.width + h * z.head, z.head), :] for c in range(3))
        g_t = grad_t[h * z.head : (h + 1) * z.head, :]
        scores = jnp.where(same, mm(k_t, q_t, TN) + r.bias[h], MASKED)
        probs = jnp.exp(scores - r.lse[m, pl.ds(h, 1), :])
        grad_probs = mm(v_t, g_t, TN)
        delta = jnp.sum(probs * grad_probs, axis=0, keepdims=True)
        grads = (probs * (grad_probs - delta)).astype(BF16)
        r.gkeep[m, h] = grads
        for c, part in enumerate((mm(k_t, grads), mm(q_t, grads, NT), mm(g_t, probs.astype(BF16), NT))):
            r.gj_t[pl.ds((c + 1) * z.width + h * z.head, z.head), :] = part.astype(BF16)


def layer_kernel(z, names, *refs):
    r = types.SimpleNamespace(**dict(zip(names, refs, strict=True)))
    me = Place(z)
    dp, row, col = me.dp, me.row, me.col
    links = Links(r.send_sem, r.recv_sem)
    plane = [(i, j) for i in range(z.ndp) for j in range(z.ncol) if (i, j) != (0, 0)]
    arrived = greet([(me.dps[i], row, me.cls[j]) for i, j in plane] + [(dp, w, col) for w in me.rws[1:]])
    gain, gain_ffn = r.gain[...], r.gain_ffn[...]
    micros = range(z.micro)

    own = [
        pltpu.make_async_copy(r.w_in.at[:, rows(row * z.ffh, z.ffh)], r.wi.at[rows(row * z.dr, z.dr), :], r.here_sem.at[0]),
        pltpu.make_async_copy(r.w_down.at[rows(row * z.ffh, z.ffh), :], r.wd.at[row], r.here_sem.at[1]),
    ]
    for copy in own:
        copy.start()
    pid = dp * z.nrow + row
    piece = lambda p: r.dense.at[rows(p * z.piece, z.piece), :]
    r.dense[rows(pid * z.piece, z.piece), :] = r.dense_in[...]
    for m in micros:
        values = r.tok[m].astype(F32)
        r.nrm[m, rows(col * z.tok, z.tok), :] = (values * norm_rows(values) * gain).astype(BF16)
    arrived()

    dense_y = [links.send(piece(pid), piece(pid), (dp, w, col)) for w in me.rws[1:]]
    dense_z = [links.send(piece(pid), piece(pid), (d, row, col)) for d in me.dps[1:]]
    block = lambda m, c: r.nrm.at[m, rows(c * z.tok, z.tok), :]
    xs = [links.send(block(m, col), block(m, col), (dp, row, me.across)) for m in micros]
    cs = [links.send(block(m, col), block(m, col), (dp, row, me.beside)) for m in micros]
    for s, copy in enumerate(dense_y):
        copy.wait_recv()
        p = dp * z.nrow + me.rws_back[s + 1]
        dense_z += [links.send(piece(p), piece(p), (d, row, col)) for d in me.dps[1:]]
    experts = []
    for w in me.rws[1:]:
        experts.append(links.send(r.w_in.at[:, rows(w * z.ffh, z.ffh)], r.wi.at[rows(row * z.dr, z.dr), :], (dp, w, col)))
        experts.append(links.send(r.w_down.at[rows(w * z.ffh, z.ffh), :], r.wd.at[row], (dp, w, col)))
    make_bias(z, r.rb, r.rel, r.bias)
    fs = []
    for m in micros:
        xs[m].wait_recv()
        fs.append(links.send(block(m, me.across), block(m, me.across), (dp, row, me.beside)))
    for copy in dense_z + cs + fs:
        copy.wait_recv()

    r.wo[col] = r.dense[:, : z.width]
    wx = links.send(r.wo.at[col], r.wo.at[col], (dp, row, me.across))
    wc = links.send(r.wo.at[col], r.wo.at[col], (dp, row, me.beside))
    swaps = []
    for m in micros:
        r.qkv_t[m] = mm(r.nrm[m], r.dense[...]).astype(BF16).T
        attention_forward(z, r, m)
        swaps.append([links.send(r.mix.at[m, c], r.mown.at[m, col], (dp, row, c)) for c in me.cls[1:]])
        r.mown[m, col] = r.mix[m, col]
        if m == 0:
            wx.wait_recv()
            wf = links.send(r.wo.at[me.across], r.wo.at[me.across], (dp, row, me.beside))
    wc.wait_recv()
    wf.wait_recv()

    mine = dp * z.ncol + col
    each = z.slots_each
    group = z.ncol * each
    dispatch = []
    for m in micros:
        for copy in swaps[m]:
            copy.wait_recv()
        values = r.tok[m].astype(F32)
        for c in range(z.ncol):
            values = values + mm(r.mown[m, c], r.wo[c], NT)
        r.hidden[m] = values
        normed = values * norm_rows(values) * gain_ffn
        chances = softmax_rows(mm(normed, r.router[...], NT, HIGHEST))
        picked, placement = routing(z, column(r.routes[m]))
        gate = jnp.sum(jnp.where(picked, chances, 0.0), axis=-1, keepdims=True)
        sent = jnp.concatenate([normed.astype(BF16), (gate * r.cot[m].astype(F32)).astype(BF16)], axis=1)
        r.slots[m] = mm(placement, sent, TN).astype(BF16)
        copies = {}
        for i, j in plane[::-1]:
            e = me.dps[i] * z.ncol + me.cls[j]
            copies[i, j] = links.send(
                r.slots.at[m, rows(e * each, each), :], r.arr.at[m, row, rows(mine * each, each), :],
                (me.dps[i], row, me.cls[j]),
            )
        dispatch.append(copies)
        r.arr[m, row, rows(mine * each, each), :] = r.slots[m, rows(mine * each, each), :]

    forwards = []
    for m in micros:
        copies = {}
        for i in range(z.ndp):
            for j in range(z.ncol):
                if (i, j) != (0, 0):
                    dispatch[m][i, j].wait_recv()
            part = r.arr.at[m, row, rows(me.dps_back[i] * group, group), :]
            for s, w in enumerate(me.rws[1:]):
                copies[i, s] = links.send(part, part, (dp, w, col))
        forwards.append(copies)

    def expert(m, w, store):
        x = r.arr[m, w, :, : z.d]
        g = r.arr[m, w, :, z.d :]
        result = jnp.zeros((z.slots, z.d), F32)
        grad = jnp.zeros((z.slots, z.d), F32)
        for k in range(z.ffh // z.chunk):
            cut = pl.ds(k * z.chunk, z.chunk)
            w_one = r.wi[:, cut]
            w_two = jnp.concatenate([r.wd[p, cut, :] for p in range(z.nrow)], axis=1)
            value, slope = gelu_both(mm(x, w_one))
            value = value.astype(BF16)
            r.act[m, w, :, cut] = value
            result = result + mm(value, w_two)
            pre = (mm(g, w_two, NT) * slope).astype(BF16)
            r.gpre[m, w, :, cut] = pre
            grad = grad + mm(pre, w_one, NT)
        store(result, grad)

    for copy in own:
        copy.wait()
    for copy in experts:
        copy.wait_recv()
    partials = []
    for m in micros:

        def store_own(result, grad, m=m):
            r.own_part[m, :, : z.d] = result
            r.own_part[m, :, z.d :] = grad

        expert(m, row, store_own)
        for copy in forwards[m].values():
            copy.wait_recv()
        copies = []
        for s, w in enumerate(me.rws[1:]):

            def store(result, grad, m=m, s=s):
                r.psend[m, s, :, : z.d] = result.astype(BF16)
                r.psend[m, s, :, z.d :] = grad.astype(BF16)

            expert(m, w, store)
            copies.append(links.send(r.psend.at[m, s], r.precv.at[m, s], (dp, w, col)))
        partials.append(copies)

    blocks = [(m, w) for m in micros for w in range(z.nrow)]
    for b, (m, w) in enumerate(blocks):
        r.xt[:, b * z.slots : (b + 1) * z.slots] = r.arr[m, w, :, : z.d].T
    for k in range(z.ffh // z.chunk):
        cut = pl.ds(k * z.chunk, z.chunk)
        pre = jnp.concatenate([r.gpre[m, w, :, cut] for m, w in blocks], axis=0)
        value = jnp.concatenate([r.act[m, w, :, cut] for m, w in blocks], axis=0)
        g = jnp.concatenate([r.arr[m, w, :, z.d :] for m, w in blocks], axis=0)
        r.wi[:, cut] = mm(r.xt[...], pre).astype(BF16)
        grad_down = mm(value, g, TN).astype(BF16)
        for p in range(z.nrow):
            r.wd[p, cut, :] = grad_down[:, p * z.dr : (p + 1) * z.dr]

    returns = []
    for m in micros:
        total = r.own_part[m]
        for s in range(z.nrow - 1):
            partials[m][s].wait_recv()
            total = total + r.precv[m, s].astype(F32)
        r.back[m] = total.astype(BF16)
        home = []
        for i, j in plane[::-1]:
            e = me.dps[i] * z.ncol + me.cls[j]
            home.append(
                links.send(
                    r.back.at[m, rows(e * each, each), :], r.ret.at[m, rows(mine * each, each), :],
                    (me.dps[i], row, me.cls[j]),
                )
            )
        r.ret[m, rows(mine * each, each), :] = r.back[m, rows(mine * each, each), :]
        returns.append(home)
    kept = [
        pltpu.make_async_copy(r.wi.at[rows(row * z.dr, z.dr), :], r.gwi.at[:, rows(row * z.ffh, z.ffh)], r.here_sem.at[2]),
        pltpu.make_async_copy(r.wd.at[row], r.gwd.at[rows(row * z.ffh, z.ffh), :], r.here_sem.at[3]),
    ]
    for copy in kept:
        copy.start()
    swapped = []
    for w in me.rws[1:]:
        swapped.append(links.send(r.wi.at[rows(w * z.dr, z.dr), :], r.gwi.at[:, rows(row * z.ffh, z.ffh)], (dp, w, col)))
        swapped.append(links.send(r.wd.at[w], r.gwd.at[rows(row * z.ffh, z.ffh), :], (dp, w, col)))

    gain_two = jnp.zeros((1, z.d), F32)
    router_t = jnp.zeros((z.experts, z.d), F32)
    step = lambda run: next(run, None)
    early = iter(())
    wire = []
    for m in micros:
        for copy in returns[m]:
            copy.wait_recv()
        values = r.hidden[m]
        factor = norm_rows(values)
        normed = values * factor * gain_ffn
        chances = softmax_rows(mm(normed, r.router[...], NT, HIGHEST))
        picked, placement = routing(z, column(r.routes[m]))
        gate = jnp.sum(jnp.where(picked, chances, 0.0), axis=-1, keepdims=True)
        came = mm(placement, r.ret[m])
        returned, grad_sent = came[:, : z.d], came[:, z.d :]
        r.layer_out[m] = (values + gate * returned).astype(BF16)
        upstream = r.cot[m].astype(F32)
        grad_gate = jnp.sum(upstream * returned, axis=-1, keepdims=True)
        grad_logits = grad_gate * gate * (picked.astype(F32) - chances)
        grad_normed = grad_sent + mm(grad_logits, r.router[...], NN, HIGHEST)
        part, gain_part = norm_back(grad_normed, values, factor, gain_ffn)
        grad_hidden = upstream + part
        r.gh[m] = grad_hidden
        r.pc[m, col] = grad_hidden.astype(BF16)
        px = links.send(r.pc.at[m, col], r.pc.at[m, col], (dp, row, me.across))
        pb = links.send(r.pc.at[m, col], r.pc.at[m, col], (dp, row, me.beside))
        router_t = router_t + mm(grad_logits, normed, TN, HIGHEST)
        gain_two = gain_two + gain_part
        if m == z.micro - 1:
            r.ebuf[0] = jnp.concatenate([router_t, gain_two, jnp.zeros((7, z.d), F32)], axis=0)
            early = reduce_all(z, me, links, r.ebuf, r.egot, lambda k: None)
            step(early)
        px.wait_recv()
        pf = links.send(r.pc.at[m, me.across], r.pc.at[m, me.across], (dp, row, me.beside))
        pb.wait_recv()
        pf.wait_recv()
        step(early)
        rows_all = r.pc[m].reshape(z.length, z.d)
        grad_mixed = mm(rows_all, r.dense[:, : z.width]).astype(BF16)
        if m == 0:
            r.gj_t[: z.width, :] = jnp.zeros((z.width, z.length), BF16)
        attention_backward(z, r, m, grad_mixed.T)
        step(early)
        gj = r.gj_t[...].T
        partial = mm(gj, r.dense[...], NT).astype(BF16)
        for c in range(z.ncol):
            r.pb[m, c] = partial[c * z.tok : (c + 1) * z.tok]
        wire.append([links.send(r.pb.at[m, me.beside], r.pr.at[m, 0], (dp, row, me.beside)),
                     links.send(r.pb.at[m, me.far], r.pr.at[m, 1], (dp, row, me.beside))])
        total = mm(r.nrm[m], gj, TN)
        out_part = mm(rows_all, r.mix[m].reshape(z.length, z.width), TN)
        if m == 0:
            r.gdf[...] = total
            r.gdf[:, : z.width] = out_part
        else:
            r.gdf[...] = r.gdf[...] + total
            r.gdf[:, : z.width] = r.gdf[:, : z.width] + out_part
        if m == z.micro - 1:
            both = z.nrow * z.piece
            zsent = []
            for i, d in enumerate(me.dps[1:]):
                r.zs[i] = r.gdf[rows(d * both, both), :].astype(BF16)
                zsent.append(links.send(r.zs.at[i], r.zr.at[i], (d, row, col)))
        wire[m][1].wait_recv()
        r.xsum[m] = (r.pb[m, me.across].astype(F32) + r.pr[m, 1].astype(F32)).astype(BF16)
        wire[m].append(links.send(r.xsum.at[m], r.px.at[m], (dp, row, me.across)))
    step(early)
    offsets = []
    for h in range(z.heads):
        total = r.gkeep[0, h].astype(F32)
        for m in range(1, z.micro):
            total = total + r.gkeep[m, h].astype(F32)
        offsets.append(gather_offsets(jnp.concatenate([total, jnp.zeros((z.length, z.length), F32)], axis=1)))
    grad_rel = mm(jnp.concatenate(offsets, axis=0), offset_table(z, r.rb), NT, HIGHEST)
    step(early)
    gain_one = jnp.zeros((1, z.d), F32)
    for m in micros:
        wire[m][0].wait_recv()
        wire[m][2].wait_recv()
        grad_normed = r.pb[m, col].astype(F32) + r.pr[m, 0].astype(F32) + r.px[m].astype(F32)
        values = r.tok[m].astype(F32)
        part, gain_part = norm_back(grad_normed, values, norm_rows(values), gain)
        gain_one = gain_one + gain_part
        r.grad_tok[m] = r.gh[m] + part
    r.lbuf[0, pl.ds(0, 1), :] = gain_one
    r.lbuf[0, pl.ds(1, 7), :] = jnp.zeros((7, z.d), F32)
    r.lbuf[0, pl.ds(1, z.heads), : z.nbuck] = grad_rel
    inner = (z.ndp * z.nrow).bit_length() - 1

    def late_done(k):
        if k == inner:
            r.late[...] = r.lbuf[k]

    final = reduce_all(z, me, links, r.lbuf, r.lgot, late_done)
    step(final)
    for copy in zsent:
        copy.wait_recv()
    ysent = []
    for s, w in enumerate(me.rws):
        spot = rows((dp * z.nrow + w) * z.piece, z.piece)
        total = r.gdf[spot, :]
        for i in range(z.ndp - 1):
            total = total + r.zr[i, rows(w * z.piece, z.piece), :].astype(F32)
        if s == 0:
            mine_sum = total
        else:
            r.ys[s - 1] = total.astype(BF16)
            ysent.append(links.send(r.ys.at[s - 1], r.yr.at[s - 1], (dp, w, col)))
    step(final)
    step(early)
    for s, copy in enumerate(ysent):
        copy.wait_recv()
        mine_sum = mine_sum + r.yr[s].astype(F32)
    r.grad_dense[...] = mine_sum
    for run in (early, final):
        for _ in run:
            pass
    stages = (z.ndp * z.nrow * z.ncol).bit_length() - 1
    r.small[...] = r.ebuf[stages]
    r.late[pl.ds(0, 1), :] = r.lbuf[stages, pl.ds(0, 1), :]
    for copy in kept:
        copy.wait()
    for copy in swapped:
        copy.wait_recv()
    links.finish()


def sizes(mesh_shape, tokens, segments, rel_table, w_in, router):
    z = types.SimpleNamespace()
    z.ndp, z.nrow, z.ncol = mesh_shape
    z.micro, z.tok, z.d = tokens.shape[0], tokens.shape[2], tokens.shape[3]
    z.length = segments.shape[2]
    z.nbuck, z.heads = rel_table.shape
    z.width = z.d // z.ncol
    z.head = z.width // z.heads
    z.ff = w_in.shape[2]
    z.ffh, z.dr = z.ff // z.nrow, z.d // z.nrow
    z.experts = router.shape[1]
    z.slots_each = max(2, 2 * z.tok // z.experts)
    z.slots = z.experts * z.slots_each
    z.piece = z.d // (z.ndp * z.nrow)
    z.chunk = min(512, z.ffh)
    return z


VM = pl.BlockSpec(memory_space=pltpu.VMEM)
ANY = pl.BlockSpec(memory_space=pl.ANY)


def fast(mesh_shape, tokens, segments, routes, buckets, gain_attn, w_qkv, w_out, rel_table, gain_ffn, router, w_in,
         w_down, cotangent):
    z = sizes(mesh_shape, tokens, segments, rel_table, w_in, router)
    S = jax.ShapeDtypeStruct
    V = pltpu.VMEM
    sem = pltpu.SemaphoreType.DMA
    rb = jnp.concatenate([buckets[::-1], jnp.full((1,), -1, jnp.int32)])[None]
    dense_in = jnp.concatenate([w_out.T, w_qkv.reshape(z.piece, -1)], axis=1)
    stages = (z.ndp * z.nrow * z.ncol).bit_length()
    ins = {
        "tok": tokens[:, 0], "seg": segments, "routes": jnp.swapaxes(routes[:, 0], 1, 2), "rb": rb, "gain": gain_attn[None],
        "dense_in": dense_in, "rel": rel_table.T, "gain_ffn": gain_ffn[None], "router": router.T, "cot": cotangent[:, 0],
        "w_in": w_in[0], "w_down": w_down[0],
    }
    outs = {
        "layer_out": S((z.micro, z.tok, z.d), BF16),
        "grad_tok": S((z.micro, z.tok, z.d), F32),
        "grad_dense": S((z.piece, z.d), F32),
        "small": S((z.experts + 8, z.d), F32),
        "late": S((8, z.d), F32),
        "gwi": S((z.dr, z.ff), BF16),
        "gwd": S((z.ff, z.dr), BF16),
    }
    others, both = z.nrow - 1, z.nrow * z.piece
    scratch = {
        "nrm": V((z.micro, z.length, z.d), BF16),
        "qkv_t": V((z.micro, z.d, z.length), BF16),
        "lse": V((z.micro, 8, z.length), F32),
        "mix": V((z.micro, z.ncol, z.tok, z.width), BF16),
        "mown": V((z.micro, z.ncol, z.tok, z.width), BF16),
        "hidden": V((z.micro, z.tok, z.d), F32),
        "slots": V((z.micro, z.slots, 2 * z.d), BF16),
        "dense": V((z.d, z.d), BF16),
        "wo": V((z.ncol, z.d, z.width), BF16),
        "bias": V((z.heads, z.length, z.length), F32),
        "wi": V((z.d, z.ffh), BF16),
        "wd": V((z.nrow, z.ffh, z.dr), BF16),
        "arr": V((z.micro, z.nrow, z.slots, 2 * z.d), BF16),
        "own_part": V((z.micro, z.slots, 2 * z.d), F32),
        "psend": V((z.micro, others, z.slots, 2 * z.d), BF16),
        "precv": V((z.micro, others, z.slots, 2 * z.d), BF16),
        "back": V((z.micro, z.slots, 2 * z.d), BF16),
        "ret": V((z.micro, z.slots, 2 * z.d), BF16),
        "act": V((z.micro, z.nrow, z.slots, z.ffh), BF16),
        "gpre": V((z.micro, z.nrow, z.slots, z.ffh), BF16),
        "xt": V((z.d, z.micro * z.nrow * z.slots), BF16),
        "pc": V((z.micro, z.ncol, z.tok, z.d), BF16),
        "gh": V((z.micro, z.tok, z.d), F32),
        "gkeep": V((z.micro, z.heads, z.length, z.length), BF16),
        "gj_t": V((z.d, z.length), BF16),
        "gdf": V((z.d, z.d), F32),
        "pb": V((z.micro, z.ncol, z.tok, z.d), BF16),
        "pr": V((z.micro, 2, z.tok, z.d), BF16),
        "px": V((z.micro, z.tok, z.d), BF16),
        "xsum": V((z.micro, z.tok, z.d), BF16),
        "zs": V((z.ndp - 1, both, z.d), BF16),
        "zr": V((z.ndp - 1, both, z.d), BF16),
        "ys": V((others, z.piece, z.d), BF16),
        "yr": V((others, z.piece, z.d), BF16),
        "ebuf": V((stages, z.experts + 8, z.d), F32),
        "egot": V((stages - 1, z.experts + 8, z.d), F32),
        "lbuf": V((stages, 8, z.d), F32),
        "lgot": V((stages - 1, 8, z.d), F32),
        "send_sem": sem((200,)),
        "recv_sem": sem((200,)),
        "here_sem": sem((4,)),
    }
    run = pl.pallas_call(
        functools.partial(layer_kernel, z, [*ins, *outs, *scratch]),
        out_shape=list(outs.values()),
        in_specs=[VM] * (len(ins) - 2) + [ANY] * 2,
        out_specs=[VM] * 5 + [ANY] * 2,
        scratch_shapes=list(scratch.values()),
        compiler_params=pltpu.CompilerParams(collective_id=1, has_side_effects=True, vmem_limit_bytes=63 * 2**20),
        name="layer",
    )
    layer_out, grad_tok, grad_dense, small, late, gwi, gwd = run(*ins.values())
    return (
        layer_out[:, None],
        grad_tok[:, None],
        late[0],
        grad_dense[:, z.width :].reshape(z.piece, 3, z.width),
        grad_dense[:, : z.width].T,
        late[1 : 1 + z.heads, : z.nbuck].T,
        small[z.experts],
        small[: z.experts].T,
        gwi.astype(F32)[None],
        gwd.astype(F32)[None],
    )


def smooth_act(values):
    return jax.nn.gelu(values, approximate=True)


def plain_normalize(values, gain_vec):
    factor = lax.rsqrt(jnp.mean(values * values, axis=-1, keepdims=True) + EPSILON)
    return (values * factor * gain_vec, factor)


def plain_norm_back(grad_into, values, factor, gain_vec):
    scaled = grad_into * gain_vec
    inner = jnp.mean(scaled * values, axis=-1, keepdims=True)
    return (
        factor * (scaled - values * factor * factor * inner),
        jnp.sum(grad_into * values * factor, axis=0),
    )


def contract_rows(left, right, precision=None):
    return lax.dot_general(
        left,
        right,
        (((0,), (0,)), ((), ())),
        precision=precision,
        preferred_element_type=jnp.float32,
    )


def contract_cols(left, right, precision=None):
    return lax.dot_general(
        left,
        right,
        (((1,), (1,)), ((), ())),
        precision=precision,
        preferred_element_type=jnp.float32,
    )


def spread_rows(offsets, row_first, row_count, length):
    shifted = jnp.roll(offsets, row_first, axis=-1)
    span_width = 2 * length - 1
    tiled_rows = jnp.tile(shifted, (1, row_count))[:, : row_count * span_width]
    return tiled_rows.reshape(offsets.shape[0], row_count, span_width)[:, :, length - 1 :]


def plain_gather_offsets(grads, row_first, length):
    heads_here = grads.shape[0]
    row_count = grads.shape[1]
    span_width = 2 * length - 1
    widened = jnp.pad(grads, ((0, 0), (0, 0), (length - 1, 0)))
    flat_rows = jnp.pad(
        widened.reshape(heads_here, row_count * span_width), ((0, 0), (0, row_count))
    )
    folded = jnp.sum(flat_rows.reshape(heads_here, row_count, 2 * length), axis=1)
    return jnp.roll(folded, -row_first, axis=-1)


def score_block(query_part, key_rows, bias_part, marks_query, marks_keys):
    scores = (
        jnp.einsum("qhd,khd->hqk", query_part, key_rows, preferred_element_type=jnp.float32)
        + bias_part
    )
    same_doc = marks_query[:, None] == marks_keys[None, :]
    return jnp.where(same_doc[None], scores, MASKED)


def fetch_dense(w_qkv, w_out):
    return (
        lax.all_gather(w_qkv, ("dp", "row"), axis=0, tiled=True),
        lax.all_gather(w_out, ("dp", "row"), axis=1, tiled=True),
    )


def fetch_experts(w_in, w_down):
    grown_in, grown_down = (
        lax.all_gather(w_in, "row", axis=1, tiled=True),
        lax.all_gather(w_down, "row", axis=2, tiled=True),
    )
    return (grown_in[0], grown_down[0])


def plain_shards(
    tokens,
    segments,
    routes,
    buckets,
    gain_attn,
    w_qkv,
    w_out,
    rel_table,
    gain_ffn,
    router,
    w_in,
    w_down,
    cotangent,
):
    micro_count = tokens.shape[0]
    tok_rows = tokens.shape[2]
    model_width = tokens.shape[3]
    length = segments.shape[2]
    local_heads = rel_table.shape[1]
    head_size = w_out.shape[0] // local_heads
    local_width = local_heads * head_size
    experts_all = router.shape[1]
    hidden_units = w_in.shape[2]
    capacity = max(2, 2 * tok_rows // experts_all)
    query_block = min(512, length)
    block_starts = list(range(0, length, query_block))
    padded_ids = jnp.concatenate([buckets, jnp.full((1,), -1, jnp.int32)])
    offset_table = (
        padded_ids[:, None] == jnp.arange(rel_table.shape[0], dtype=jnp.int32)[None, :]
    ).astype(jnp.float32)
    offset_bias = jnp.dot(offset_table, rel_table, precision=HIGHEST).T
    block_bias = [
        spread_rows(offset_bias, row_start, query_block, length) for row_start in block_starts
    ]
    expert_ids = jnp.arange(experts_all, dtype=jnp.int32)
    slot_ids = jnp.arange(experts_all * capacity, dtype=jnp.int32)
    saved = []
    outputs = []
    for micro_index in range(micro_count):
        full_qkv, full_out = fetch_dense(w_qkv, w_out)
        full_in, full_down = fetch_experts(w_in, w_down)
        own_rows = tokens[micro_index, 0].astype(jnp.float32)
        whole_rows = lax.all_gather(tokens[micro_index, 0], "col", axis=0, tiled=True).astype(
            jnp.float32
        )
        normed_one = plain_normalize(whole_rows, gain_attn)[0].astype(jnp.bfloat16)
        joined = jnp.einsum(
            "td,dcf->tcf", normed_one, full_qkv, preferred_element_type=jnp.float32
        ).astype(jnp.bfloat16)
        queries = joined[:, 0].reshape(length, local_heads, head_size)
        key_rows = joined[:, 1].reshape(length, local_heads, head_size)
        value_rows = joined[:, 2].reshape(length, local_heads, head_size)
        marks = segments[micro_index, 0]
        mixed_parts = []
        log_sums = []
        for block_index, row_start in enumerate(block_starts):
            scores = score_block(queries, key_rows, block_bias[block_index], marks, marks)
            highest = jnp.max(scores, axis=-1, keepdims=True)
            log_sum = highest + jnp.log(jnp.sum(jnp.exp(scores - highest), axis=-1, keepdims=True))
            weights = jnp.exp(scores - log_sum).astype(jnp.bfloat16)
            mixed_parts.append(
                jnp.einsum(
                    "hqk,khd->qhd", weights, value_rows, preferred_element_type=jnp.float32
                ).astype(jnp.bfloat16)
            )
            log_sums.append(log_sum)
        mixed = mixed_parts[0].reshape(length, local_width)
        hidden = own_rows + lax.psum_scatter(
            jnp.dot(mixed, full_out, preferred_element_type=jnp.float32),
            "col",
            scatter_dimension=0,
            tiled=True,
        )
        normed_two, factor_two = plain_normalize(hidden, gain_ffn)
        chances = jax.nn.softmax(jnp.dot(normed_two, router, precision=HIGHEST), axis=-1)
        chosen = routes[micro_index, 0, :, 0]
        picked = chosen[:, None] == expert_ids[None, :]
        gate_value = jnp.sum(jnp.where(picked, chances, 0.0), axis=-1)
        picked_int = picked.astype(jnp.int32)
        ranks = jnp.sum((jnp.cumsum(picked_int, axis=0) - picked_int) * picked_int, axis=1)
        placement = ((chosen * capacity + ranks)[:, None] == slot_ids[None, :]).astype(jnp.bfloat16)
        outgoing = contract_rows(placement, normed_two.astype(jnp.bfloat16)).astype(jnp.bfloat16)
        outgoing = outgoing.reshape(experts_all, capacity, model_width)
        arrived = lax.all_to_all(outgoing, ("dp", "col"), split_axis=0, concat_axis=0, tiled=True)
        flat_in = arrived.reshape(-1, model_width)
        before = jnp.dot(flat_in, full_in, preferred_element_type=jnp.float32)
        active = smooth_act(before).astype(jnp.bfloat16)
        result = jnp.dot(active, full_down, preferred_element_type=jnp.float32).astype(jnp.bfloat16)
        sent_back = lax.all_to_all(
            result.reshape(arrived.shape), ("dp", "col"), split_axis=0, concat_axis=0, tiled=True
        )
        sent_back, arrived, before_all = (
            sent_back,
            arrived,
            before.reshape(arrived.shape[0], arrived.shape[1], hidden_units),
        )
        expert_out = jnp.dot(
            placement, sent_back.reshape(-1, model_width), preferred_element_type=jnp.float32
        )
        outputs.append((hidden + gate_value[:, None] * expert_out).astype(jnp.bfloat16))
        saved.append(
            (
                own_rows,
                normed_one,
                queries,
                key_rows,
                value_rows,
                marks,
                log_sums,
                mixed,
                hidden,
                normed_two,
                factor_two,
                chances,
                picked,
                gate_value,
                placement,
                expert_out,
                arrived,
                before_all,
            )
        )
    grad_qkv_sum = jnp.zeros((model_width, 3, local_width), jnp.float32)
    grad_out_sum = jnp.zeros((local_width, model_width), jnp.float32)
    grad_in_sum = jnp.zeros((model_width, hidden_units), jnp.float32)
    grad_down_sum = jnp.zeros((hidden_units, model_width), jnp.float32)
    grad_offsets = jnp.zeros((local_heads, 2 * length), jnp.float32)
    grad_gain_one = jnp.zeros((model_width,), jnp.float32)
    grad_gain_two = jnp.zeros((model_width,), jnp.float32)
    grad_router_sum = jnp.zeros(router.shape, jnp.float32)
    grads_input = []
    for micro_index in range(micro_count):
        (
            own_rows,
            normed_one,
            queries,
            key_rows,
            value_rows,
            marks,
            log_sums,
            mixed,
            hidden,
            normed_two,
            factor_two,
            chances,
            picked,
            gate_value,
            placement,
            expert_out,
            arrived,
            before_all,
        ) = saved[micro_index]
        full_qkv, full_out = fetch_dense(w_qkv, w_out)
        full_in, full_down = fetch_experts(w_in, w_down)
        upstream = cotangent[micro_index, 0].astype(jnp.float32)
        grad_gate = jnp.sum(upstream * expert_out, axis=-1)
        grad_result = (gate_value[:, None] * upstream).astype(jnp.bfloat16)
        to_slots = contract_rows(placement, grad_result).astype(jnp.bfloat16)
        to_slots = to_slots.reshape(experts_all, capacity, model_width)
        at_expert = lax.all_to_all(
            to_slots, ("dp", "col"), split_axis=0, concat_axis=0, tiled=True
        ).reshape(-1, model_width)
        flat_before = before_all.reshape(-1, hidden_units)
        act_value, act_pull = jax.vjp(smooth_act, flat_before)
        flat_active = act_value.astype(jnp.bfloat16)
        grad_down_sum = grad_down_sum + contract_rows(flat_active, at_expert)
        grad_active = contract_cols(at_expert, full_down)
        grad_before = act_pull(grad_active)[0].astype(jnp.bfloat16)
        grad_in_sum = grad_in_sum + contract_rows(arrived.reshape(-1, model_width), grad_before)
        grad_sent = (
            contract_cols(grad_before, full_in)
            .astype(jnp.bfloat16)
            .reshape(experts_all, capacity, model_width)
        )
        came_back = lax.all_to_all(
            grad_sent, ("dp", "col"), split_axis=0, concat_axis=0, tiled=True
        )
        grad_normed_two = jnp.dot(
            placement, came_back.reshape(-1, model_width), preferred_element_type=jnp.float32
        )
        grad_logits = (grad_gate * gate_value)[:, None] * (picked.astype(jnp.float32) - chances)
        grad_router_sum = grad_router_sum + contract_rows(normed_two, grad_logits, HIGHEST)
        grad_normed_two = grad_normed_two + contract_cols(grad_logits, router, HIGHEST)
        grad_norm_part, gain_part = plain_norm_back(grad_normed_two, hidden, factor_two, gain_ffn)
        grad_gain_two = grad_gain_two + gain_part
        grad_hidden = upstream + grad_norm_part
        piece = lax.all_gather(grad_hidden.astype(jnp.bfloat16), "col", axis=0, tiled=True)
        total_out = grad_out_sum
        total_out = total_out + contract_rows(mixed, piece)
        spread_grad = contract_cols(piece, full_out)
        grad_out_sum = total_out
        grad_mixed = spread_grad
        grad_mixed = grad_mixed.astype(jnp.bfloat16).reshape(length, local_heads, head_size)
        grad_keys = jnp.zeros((length, local_heads, head_size), jnp.float32)
        grad_values = jnp.zeros((length, local_heads, head_size), jnp.float32)
        query_grads = []
        for block_index, row_start in enumerate(block_starts):
            scores = score_block(queries, key_rows, block_bias[block_index], marks, marks)
            weights = jnp.exp(scores - log_sums[block_index])
            grad_values = jnp.einsum(
                "hqk,qhd->khd",
                weights.astype(jnp.bfloat16),
                grad_mixed,
                preferred_element_type=jnp.float32,
            )
            grad_weights = jnp.einsum(
                "qhd,khd->hqk", grad_mixed, value_rows, preferred_element_type=jnp.float32
            )
            grad_scores = (
                weights * (grad_weights - jnp.sum(weights * grad_weights, axis=-1, keepdims=True))
            ).astype(jnp.bfloat16)
            grad_offsets = grad_offsets + plain_gather_offsets(
                grad_scores.astype(jnp.float32), row_start, length
            )
            query_grads.append(
                jnp.einsum(
                    "hqk,khd->qhd", grad_scores, key_rows, preferred_element_type=jnp.float32
                )
            )
            grad_keys = jnp.einsum(
                "hqk,qhd->khd", grad_scores, queries, preferred_element_type=jnp.float32
            )
        grad_joined = jnp.stack([query_grads[0], grad_keys, grad_values], axis=1)
        grad_joined = grad_joined.reshape(length, 3, local_width).astype(jnp.bfloat16)
        grad_qkv_sum = grad_qkv_sum + jnp.einsum(
            "td,tcf->dcf", normed_one, grad_joined, preferred_element_type=jnp.float32
        )
        grad_normed_one = lax.psum_scatter(
            jnp.einsum(
                "tcf,dcf->td", grad_joined, full_qkv, preferred_element_type=jnp.float32
            ).astype(jnp.bfloat16),
            "col",
            scatter_dimension=0,
            tiled=True,
        ).astype(jnp.float32)
        factor_one = plain_normalize(own_rows, gain_attn)[1]
        grad_input_part, gain_part = plain_norm_back(grad_normed_one, own_rows, factor_one, gain_attn)
        grad_gain_one = grad_gain_one + gain_part
        grads_input.append(grad_hidden + grad_input_part)
    grad_rel_mine = jnp.dot(offset_table.T, grad_offsets.T, precision=HIGHEST)
    heads_all = local_heads * lax.axis_size("col")
    head_first = lax.axis_index("col") * local_heads
    rel_full = lax.dynamic_update_slice_in_dim(
        jnp.zeros((rel_table.shape[0], heads_all), jnp.float32), grad_rel_mine, head_first, 1
    )
    total_gain_one, total_gain_two, total_router, total_rel = lax.psum(
        (grad_gain_one, grad_gain_two, grad_router_sum, rel_full), ("dp", "row", "col")
    )
    rel_out = lax.dynamic_slice_in_dim(total_rel, head_first, local_heads, 1)
    dense_qkv, dense_out = (
        lax.psum_scatter(grad_qkv_sum, ("dp", "row"), scatter_dimension=0, tiled=True),
        lax.psum_scatter(grad_out_sum, ("dp", "row"), scatter_dimension=1, tiled=True),
    )
    expert_in, expert_down = (
        lax.psum_scatter(
            grad_in_sum[None].astype(jnp.bfloat16), "row", scatter_dimension=1, tiled=True
        ).astype(jnp.float32),
        lax.psum_scatter(
            grad_down_sum[None].astype(jnp.bfloat16), "row", scatter_dimension=2, tiled=True
        ).astype(jnp.float32),
    )
    layer_out = jnp.stack(outputs)[:, None]
    grad_tokens = jnp.stack(grads_input)[:, None]
    return (
        layer_out,
        grad_tokens,
        total_gain_one,
        dense_qkv,
        dense_out,
        rel_out,
        total_gain_two,
        total_router,
        expert_in,
        expert_down,
    )


def solution(mesh):
    shape = tuple(mesh.shape[a] for a in ("dp", "row", "col"))
    token_spec, expert_in, expert_down = P(None, ("dp", "row"), "col", None), P(("dp", "col"), "row", None), P(("dp", "col"), None, "row")
    qkv_spec, out_spec = P(("dp", "row"), None, "col"), P("col", ("dp", "row"))
    in_specs = (
        token_spec, P(None, ("dp", "row"), None), token_spec, P(), P(), qkv_spec, out_spec, P(None, "col"), P(), P(),
        expert_in, expert_down, token_spec,
    )
    out_specs = (token_spec, token_spec, P(), qkv_spec, out_spec, P(None, "col"), P(), P(), expert_in, expert_down)

    def run(*args):
        piece, each = args[5].shape[0] // (shape[0] * shape[1]), 2 * args[0].shape[2] // shape[2] // args[9].shape[1]
        whole_tiles = piece % 16 == 0 and each % 16 == 0 and shape[2] == 4
        body = functools.partial(fast, shape) if whole_tiles else plain_shards
        return jax.shard_map(body, mesh=mesh, in_specs=in_specs, out_specs=out_specs, check_vma=False)(*args)

    return run
```

```python
import functools
import types

import jax
import jax.numpy as jnp
from jax import lax
from jax.experimental import pallas as pl
from jax.experimental.pallas import tpu as pltpu
from jax.sharding import PartitionSpec as P

EPSILON = 1e-06
HIGHEST = lax.Precision.HIGHEST
MASKED = -1000000000.0
MESH = pl.DeviceIdType.MESH
F32 = jnp.float32
BF16 = jnp.bfloat16
NN = (((1,), (0,)), ((), ()))
NT = (((1,), (1,)), ((), ()))
TN = (((0,), (0,)), ((), ()))


def mm(left, right, dims=NN, precision=None):
    return lax.dot_general(left, right, dims, precision=precision, preferred_element_type=F32)


def rows(first, count):
    return pl.ds(pl.multiple_of(first, count), count)


class Links:
    def __init__(self, send_sem, recv_sem):
        self.send_sem, self.recv_sem, self.used, self.started = send_sem, recv_sem, 0, []

    def send(self, src, dst, device):
        k = self.used
        self.used += 1
        copy = pltpu.make_async_remote_copy(
            src_ref=src, dst_ref=dst, send_sem=self.send_sem.at[k], recv_sem=self.recv_sem.at[k],
            device_id=device, device_id_type=MESH,
        )
        copy.start()
        self.started.append(copy)
        return copy

    def finish(self):
        for copy in self.started:
            copy.wait_send()


class Place:
    def __init__(self, z):
        self.dp, self.row, self.col = lax.axis_index("dp"), lax.axis_index("row"), lax.axis_index("col")
        dp, row, col = self.dp, self.row, self.col
        self.dps = [lax.rem(dp + i, z.ndp) for i in range(z.ndp)]
        self.rws = [lax.rem(row + i, z.nrow) for i in range(z.nrow)]
        self.cls = [lax.rem(col + i, z.ncol) for i in range(z.ncol)]
        self.dps_back = [lax.rem(dp + z.ndp - i, z.ndp) for i in range(z.ndp)]
        self.rws_back = [lax.rem(row + z.nrow - i, z.nrow) for i in range(z.nrow)]
        self.cls_back = [lax.rem(col + z.ncol - i, z.ncol) for i in range(z.ncol)]
        self.across = lax.rem(col + 2, z.ncol)
        self.beside = col + 1 - 2 * lax.rem(col, 2)
        self.far = lax.rem(self.beside + 2, z.ncol)


def greet(devices):
    barrier = pltpu.get_barrier_semaphore()
    for device in devices:
        pl.semaphore_signal(barrier, inc=1, device_id=device, device_id_type=MESH)
    return lambda: pl.semaphore_wait(barrier, len(devices))


def norm_rows(values):
    return lax.rsqrt(jnp.mean(values * values, axis=-1, keepdims=True) + EPSILON)


def norm_back(grad_into, values, factor, gain_vec):
    scaled = grad_into * gain_vec
    inner = jnp.mean(scaled * values, axis=-1, keepdims=True)
    return (
        factor * (scaled - values * factor * factor * inner),
        jnp.sum(grad_into * values * factor, axis=0, keepdims=True),
    )


def column(line):
    return jnp.broadcast_to(line.astype(F32), (8, line.shape[1])).T[:, :1]


def offset_table(z, rb):
    ids = lax.broadcasted_iota(jnp.int32, (z.nbuck, 2 * z.length), 0)
    return (ids == rb[...]).astype(F32)


def make_bias(z, rb, rel, bias):
    offsets = mm(rel[...], offset_table(z, rb), NN, HIGHEST)
    for h in range(z.heads):
        spread = jnp.broadcast_to(offsets[h : h + 1, :], (z.length, 2 * z.length))
        turned = pltpu.roll(spread, z.length + 1, 1, stride=1, stride_axis=0)
        bias[h] = turned[:, : z.length]


def gather_offsets(values):
    count = values.shape[0] // 2
    while count >= 1:
        values = pltpu.roll(values[:count], count, 1) + values[count:]
        count //= 2
    return values


def routing(z, chosen):
    ids = lax.broadcasted_iota(jnp.int32, (z.tok, z.experts), 1).astype(F32)
    picked = chosen == ids
    before = (
        lax.broadcasted_iota(jnp.int32, (z.tok, z.tok), 0) > lax.broadcasted_iota(jnp.int32, (z.tok, z.tok), 1)
    ).astype(BF16)
    counts = mm(before, picked.astype(BF16))
    ranks = jnp.sum(jnp.where(picked, counts, 0.0), axis=1, keepdims=True)
    slot = chosen * z.slots_each + ranks
    placement = (slot == lax.broadcasted_iota(jnp.int32, (z.tok, z.slots), 1).astype(F32)).astype(BF16)
    return picked, placement


def softmax_rows(logits):
    top = jnp.exp(logits - jnp.max(logits, axis=-1, keepdims=True))
    return top / jnp.sum(top, axis=-1, keepdims=True)


def gelu_both(before):
    inner = 0.7978845608 * (before + 0.044715 * before * before * before)
    t = jnp.tanh(inner)
    half = 0.5 * (1.0 + t)
    slope = half + 0.5 * before * (1.0 - t * t) * (0.7978845608 * (1.0 + 3.0 * 0.044715 * before * before))
    return before * half, slope


def partner(index, step):
    return index + step - 2 * step * lax.rem(index // step, 2)


def reduce_all(z, me, links, buf, got, finish):
    dp, row, col = me.dp, me.row, me.col
    stages = []
    for size, place in ((z.ndp, lambda s: (partner(dp, s), row, col)), (z.nrow, lambda s: (dp, partner(row, s), col)),
                        (z.ncol, lambda s: (dp, row, partner(col, s)))):
        step = 1
        while step < size:
            stages.append(place(step))
            step *= 2
    for k, device in enumerate(stages):
        copy = links.send(buf.at[k], got.at[k], device)
        yield
        copy.wait_recv()
        buf[k + 1] = buf[k] + got[k]
        finish(k + 1)


def attention_forward(z, r, m):
    seg = r.seg[m]
    same = column(seg) == seg.astype(F32)
    parts = []
    for h in range(z.heads):
        q_t, k_t, v_t = (r.qkv_t[m, pl.ds((c + 1) * z.width + h * z.head, z.head), :] for c in range(3))
        scores = jnp.where(same, mm(k_t, q_t, TN) + r.bias[h], MASKED)
        highest = jnp.max(scores, axis=0, keepdims=True)
        raised = jnp.exp(scores - highest)
        total = jnp.sum(raised, axis=0, keepdims=True)
        r.lse[m, pl.ds(h, 1), :] = highest + jnp.log(total)
        probs = (raised * (1.0 / total)).astype(BF16)
        parts.append(mm(v_t, probs))
    mixed = jnp.concatenate(parts, axis=0).T.astype(BF16)
    for c in range(z.ncol):
        r.mix[m, c] = mixed[c * z.tok : (c + 1) * z.tok]


def attention_backward(z, r, m, grad_t):
    seg = r.seg[m]
    same = column(seg) == seg.astype(F32)
    for h in range(z.heads):
        q_t, k_t, v_t = (r.qkv_t[m, pl.ds((c + 1) * z.width + h * z.head, z.head), :] for c in range(3))
        g_t = grad_t[h * z.head : (h + 1) * z.head, :]
        scores = jnp.where(same, mm(k_t, q_t, TN) + r.bias[h], MASKED)
        probs = jnp.exp(scores - r.lse[m, pl.ds(h, 1), :])
        grad_probs = mm(v_t, g_t, TN)
        delta = jnp.sum(probs * grad_probs, axis=0, keepdims=True)
        grads = (probs * (grad_probs - delta)).astype(BF16)
        r.gkeep[m, h] = grads
        for c, part in enumerate((mm(k_t, grads), mm(q_t, grads, NT), mm(g_t, probs.astype(BF16), NT))):
            r.gj_t[pl.ds((c + 1) * z.width + h * z.head, z.head), :] = part.astype(BF16)


def layer_kernel(z, names, *refs):
    r = types.SimpleNamespace(**dict(zip(names, refs, strict=True)))
    me = Place(z)
    dp, row, col = me.dp, me.row, me.col
    links = Links(r.send_sem, r.recv_sem)
    plane = [(i, j) for i in range(z.ndp) for j in range(z.ncol) if (i, j) != (0, 0)]
    arrived = greet([(me.dps[i], row, me.cls[j]) for i, j in plane] + [(dp, w, col) for w in me.rws[1:]])
    gain, gain_ffn = r.gain[...].reshape(1, z.d), r.gain_ffn[...].reshape(1, z.d)
    micros = range(z.micro)

    own = [
        pltpu.make_async_copy(r.w_in.at[:, rows(row * z.ffh, z.ffh)], r.wi.at[rows(row * z.dr, z.dr), :], r.here_sem.at[0]),
        pltpu.make_async_copy(r.w_down.at[rows(row * z.ffh, z.ffh), :], r.wd.at[row], r.here_sem.at[1]),
    ]
    for copy in own:
        copy.start()
    pid = dp * z.nrow + row
    piece = lambda p: r.dense.at[rows(p * z.piece, z.piece), :]
    r.dense[rows(pid * z.piece, z.piece), :] = jnp.concatenate(
        [r.w_out[...].astype(F32).T.astype(BF16)] + [r.w_qkv[c] for c in range(3)], axis=1
    )
    for m in micros:
        values = r.tok[m].astype(F32)
        r.nrm[m, rows(col * z.tok, z.tok), :] = (values * norm_rows(values) * gain).astype(BF16)
    arrived()

    dense_y = [links.send(piece(pid), piece(pid), (dp, w, col)) for w in me.rws[1:]]
    dense_z = [links.send(piece(pid), piece(pid), (d, row, col)) for d in me.dps[1:]]
    block = lambda m, c: r.nrm.at[m, rows(c * z.tok, z.tok), :]
    xs = [links.send(block(m, col), block(m, col), (dp, row, me.across)) for m in micros]
    cs = [links.send(block(m, col), block(m, col), (dp, row, me.beside)) for m in micros]
    routes = [links.send(r.routes, r.near.at[row], (dp, w, col)) for w in me.rws[1:]]
    experts = []
    for w in me.rws[1:]:
        experts.append(links.send(r.w_in.at[:, rows(w * z.ffh, z.ffh)], r.wi.at[rows(row * z.dr, z.dr), :], (dp, w, col)))
        experts.append(links.send(r.w_down.at[rows(w * z.ffh, z.ffh), :], r.wd.at[row], (dp, w, col)))
    for s, copy in enumerate(dense_y):
        copy.wait_recv()
        p = dp * z.nrow + me.rws_back[s + 1]
        dense_z += [links.send(piece(p), piece(p), (d, row, col)) for d in me.dps[1:]]
    make_bias(z, r.rb, r.rel, r.bias)
    fs = []
    for m in micros:
        xs[m].wait_recv()
        fs.append(links.send(block(m, me.across), block(m, me.across), (dp, row, me.beside)))
    for copy in dense_z + cs + fs:
        copy.wait_recv()

    r.wo[col] = r.dense[:, : z.width]
    wx = links.send(r.wo.at[col], r.wo.at[col], (dp, row, me.across))
    wc = links.send(r.wo.at[col], r.wo.at[col], (dp, row, me.beside))
    swaps = []
    for m in micros:
        r.qkv_t[m] = mm(r.nrm[m], r.dense[...]).astype(BF16).T
        attention_forward(z, r, m)
        swaps.append([links.send(r.mix.at[m, c], r.mown.at[m, col], (dp, row, c)) for c in me.cls[1:]])
        r.mown[m, col] = r.mix[m, col]
        if m == 0:
            wx.wait_recv()
            wf = links.send(r.wo.at[me.across], r.wo.at[me.across], (dp, row, me.beside))
    wc.wait_recv()
    wf.wait_recv()

    mine = dp * z.ncol + col
    each = z.slots_each
    group = z.ncol * each
    dispatch = []

    def spread(m, w, slots):
        r.slots[m, w] = slots
        copies = {}
        for i, j in plane[::-1]:
            e = me.dps[i] * z.ncol + me.cls[j]
            copies[i, j] = links.send(
                r.slots.at[m, w, rows(e * each, each), :], r.arr.at[m, w, rows(mine * each, each), :],
                (me.dps[i], row, me.cls[j]),
            )
        r.arr[m, w, rows(mine * each, each), :] = r.slots[m, w, rows(mine * each, each), :]
        return copies

    for m in micros:
        for copy in swaps[m]:
            copy.wait_recv()
        values = r.tok[m].astype(F32)
        for c in range(z.ncol):
            values = values + mm(r.mown[m, c], r.wo[c], NT)
        r.hidden[m] = values
        normed = values * norm_rows(values) * gain_ffn
        chances = softmax_rows(mm(normed, r.router[...], NT, HIGHEST))
        picked, placement = routing(z, column(r.routes[m]))
        gate = jnp.sum(jnp.where(picked, chances, 0.0), axis=-1, keepdims=True)
        sent = jnp.concatenate([normed.astype(BF16), (gate * r.cot[m].astype(F32)).astype(BF16)], axis=1)
        if m == z.micro - 1:
            r.near_rows[row] = sent
            crossing = [links.send(r.near_rows.at[row], r.near_rows.at[row], (dp, w, col)) for w in me.rws[1:]]
        dispatch.append(spread(m, row, mm(placement, sent, TN).astype(BF16)))

    for copy in routes + crossing:
        copy.wait_recv()
    cross = {}
    for s in range(z.nrow - 1):
        w = me.rws_back[s + 1]
        placement = routing(z, column(r.near[w, z.micro - 1]))[1]
        cross[s] = spread(z.micro - 1, w, mm(placement, r.near_rows[w], TN).astype(BF16))

    forwards = []
    for m in micros[:-1]:
        copies = {}
        for i in range(z.ndp):
            for j in range(z.ncol):
                if (i, j) != (0, 0):
                    dispatch[m][i, j].wait_recv()
            part = r.arr.at[m, row, rows(me.dps_back[i] * group, group), :]
            for s, w in enumerate(me.rws[1:]):
                copies[i, s] = links.send(part, part, (dp, w, col))
        forwards.append(copies)

    def expert(m, w, store):
        x = r.arr[m, w, :, : z.d]
        g = r.arr[m, w, :, z.d :]
        result = jnp.zeros((z.slots, z.d), F32)
        grad = jnp.zeros((z.slots, z.d), F32)
        for k in range(z.ffh // z.chunk):
            cut = pl.ds(k * z.chunk, z.chunk)
            w_one = r.wi[:, cut]
            w_two = jnp.concatenate([r.wd[p, cut, :] for p in range(z.nrow)], axis=1)
            value, slope = gelu_both(mm(x, w_one))
            value = value.astype(BF16)
            r.act[m, w, :, cut] = value
            result = result + mm(value, w_two)
            pre = (mm(g, w_two, NT) * slope).astype(BF16)
            r.gpre[m, w, :, cut] = pre
            grad = grad + mm(pre, w_one, NT)
        store(result, grad)

    for copy in own:
        copy.wait()
    for copy in experts:
        copy.wait_recv()
    partials = []
    order = [*range(1, z.ndp), 0]
    for m in micros:

        def store_own(result, grad, m=m):
            r.own_part[m, :, : z.d] = result
            r.own_part[m, :, z.d :] = grad

        if m == z.micro - 1:
            for copy in dispatch[m].values():
                copy.wait_recv()
        expert(m, row, store_own)
        for copies in (forwards[m],) if m < z.micro - 1 else cross.values():
            for copy in copies.values():
                copy.wait_recv()
        copies = {}
        for s, w in enumerate(me.rws[1:]):

            def store(result, grad, m=m, s=s):
                r.psend[m, s, :, : z.d] = result.astype(BF16)
                r.psend[m, s, :, z.d :] = grad.astype(BF16)

            expert(m, w, store)
            for i in order:
                spot = rows(me.dps[i] * group, group)
                copies[i, s] = links.send(r.psend.at[m, s, spot, :], r.precv.at[m, s, spot, :], (dp, w, col))
        partials.append(copies)

    def go_home(m):
        home = []
        for i in order:
            spot = rows(me.dps[i] * group, group)
            total = r.own_part[m, spot, :]
            for s in range(z.nrow - 1):
                partials[m][i, s].wait_recv()
                total = total + r.precv[m, s, spot, :].astype(F32)
            r.back[m, spot, :] = total.astype(BF16)
            for j in range(z.ncol):
                if (i, j) != (0, 0):
                    e = me.dps[i] * z.ncol + me.cls[j]
                    home.append(
                        links.send(
                            r.back.at[m, rows(e * each, each), :], r.ret.at[m, rows(mine * each, each), :],
                            (me.dps[i], row, me.cls[j]),
                        )
                    )
        r.ret[m, rows(mine * each, each), :] = r.back[m, rows(mine * each, each), :]
        return home

    returns = [go_home(m) for m in micros[:-1]]

    blocks = [(m, w) for m in micros for w in range(z.nrow)]
    for b, (m, w) in enumerate(blocks):
        r.xt[:, b * z.slots : (b + 1) * z.slots] = r.arr[m, w, :, : z.d].T
    for k in range(z.ffh // z.chunk):
        cut = pl.ds(k * z.chunk, z.chunk)
        pre = jnp.concatenate([r.gpre[m, w, :, cut] for m, w in blocks], axis=0)
        value = jnp.concatenate([r.act[m, w, :, cut] for m, w in blocks], axis=0)
        g = jnp.concatenate([r.arr[m, w, :, z.d :] for m, w in blocks], axis=0)
        r.wi[:, cut] = mm(r.xt[...], pre).astype(BF16)
        grad_down = mm(value, g, TN).astype(BF16)
        for p in range(z.nrow):
            r.wd[p, cut, :] = grad_down[:, p * z.dr : (p + 1) * z.dr]

    def token_back(m):
        for copy in returns[m]:
            copy.wait_recv()
        values = r.hidden[m]
        factor = norm_rows(values)
        normed = values * factor * gain_ffn
        chances = softmax_rows(mm(normed, r.router[...], NT, HIGHEST))
        picked, placement = routing(z, column(r.routes[m]))
        gate = jnp.sum(jnp.where(picked, chances, 0.0), axis=-1, keepdims=True)
        came = mm(placement, r.ret[m])
        returned, grad_sent = came[:, : z.d], came[:, z.d :]
        r.layer_out[m] = (values + gate * returned).astype(BF16)
        upstream = r.cot[m].astype(F32)
        grad_gate = jnp.sum(upstream * returned, axis=-1, keepdims=True)
        grad_logits = grad_gate * gate * (picked.astype(F32) - chances)
        grad_normed = grad_sent + mm(grad_logits, r.router[...], NN, HIGHEST)
        part, gain_part = norm_back(grad_normed, values, factor, gain_ffn)
        grad_hidden = upstream + part
        r.gh[m] = grad_hidden
        r.pc[m, col] = grad_hidden.astype(BF16)
        across = links.send(r.pc.at[m, col], r.pc.at[m, col], (dp, row, me.across))
        beside = links.send(r.pc.at[m, col], r.pc.at[m, col], (dp, row, me.beside))
        return across, beside, mm(grad_logits, normed, TN, HIGHEST), gain_part

    gain_two = jnp.zeros((1, z.d), F32)
    router_t = jnp.zeros((z.experts, z.d), F32)
    step = lambda run: next(run, None)
    early = iter(())
    wire = []
    kept = []
    for m in micros:
        across, beside, router_part, gain_part = token_back(m)
        router_t = router_t + router_part
        gain_two = gain_two + gain_part
        if m == z.micro - 2:
            returns.append(go_home(z.micro - 1))
            kept = [
                pltpu.make_async_copy(r.wi.at[rows(row * z.dr, z.dr), :], r.gwi.at[:, rows(row * z.ffh, z.ffh)], r.here_sem.at[2]),
                pltpu.make_async_copy(r.wd.at[row], r.gwd.at[rows(row * z.ffh, z.ffh), :], r.here_sem.at[3]),
            ]
            for copy in kept:
                copy.start()
            swapped = []
            for w in me.rws[1:]:
                swapped.append(links.send(r.wi.at[rows(w * z.dr, z.dr), :], r.gwi.at[:, rows(row * z.ffh, z.ffh)], (dp, w, col)))
                swapped.append(links.send(r.wd.at[w], r.gwd.at[rows(row * z.ffh, z.ffh), :], (dp, w, col)))
        if m == z.micro - 1:
            r.ebuf[0] = jnp.concatenate([router_t, gain_two, jnp.zeros((7, z.d), F32)], axis=0)
            early = reduce_all(z, me, links, r.ebuf, r.egot, lambda k: None)
            step(early)
        across.wait_recv()
        passed = links.send(r.pc.at[m, me.across], r.pc.at[m, me.across], (dp, row, me.beside))
        beside.wait_recv()
        passed.wait_recv()
        step(early)
        rows_all = r.pc[m].reshape(z.length, z.d)
        grad_mixed = mm(rows_all, r.dense[:, : z.width]).astype(BF16)
        if m == 0:
            r.gj_t[: z.width, :] = jnp.zeros((z.width, z.length), BF16)
        attention_backward(z, r, m, grad_mixed.T)
        step(early)
        gj = r.gj_t[...].T
        partial = mm(gj, r.dense[...], NT).astype(BF16)
        for c in range(z.ncol):
            r.pb[m, c] = partial[c * z.tok : (c + 1) * z.tok]
        wire.append([links.send(r.pb.at[m, me.beside], r.pr.at[m, 0], (dp, row, me.beside)),
                     links.send(r.pb.at[m, me.far], r.pr.at[m, 1], (dp, row, me.beside))])
        total = mm(r.nrm[m], gj, TN)
        out_part = mm(rows_all, r.mix[m].reshape(z.length, z.width), TN)
        if m == 0:
            r.gdf[...] = total
            r.gdf[:, : z.width] = out_part
        else:
            r.gdf[...] = r.gdf[...] + total
            r.gdf[:, : z.width] = r.gdf[:, : z.width] + out_part
        if m == z.micro - 1:
            both = z.nrow * z.piece
            zsent = []
            for i, d in enumerate(me.dps[1:]):
                r.zs[i] = r.gdf[rows(d * both, both), :].astype(BF16)
                zsent.append(links.send(r.zs.at[i], r.zr.at[i], (d, row, col)))
        wire[m][1].wait_recv()
        r.xsum[m] = (r.pb[m, me.across].astype(F32) + r.pr[m, 1].astype(F32)).astype(BF16)
        wire[m].append(links.send(r.xsum.at[m], r.px.at[m], (dp, row, me.across)))
    step(early)
    offsets = []
    for h in range(z.heads):
        total = r.gkeep[0, h].astype(F32)
        for m in range(1, z.micro):
            total = total + r.gkeep[m, h].astype(F32)
        offsets.append(gather_offsets(jnp.concatenate([total, jnp.zeros((z.length, z.length), F32)], axis=1)))
    grad_rel = mm(jnp.concatenate(offsets, axis=0), offset_table(z, r.rb), NT, HIGHEST)
    step(early)
    gain_one = jnp.zeros((1, z.d), F32)
    for m in micros:
        wire[m][0].wait_recv()
        wire[m][2].wait_recv()
        grad_normed = r.pb[m, col].astype(F32) + r.pr[m, 0].astype(F32) + r.px[m].astype(F32)
        values = r.tok[m].astype(F32)
        part, gain_part = norm_back(grad_normed, values, norm_rows(values), gain)
        gain_one = gain_one + gain_part
        r.grad_tok[m] = r.gh[m] + part
    r.lbuf[0, pl.ds(0, 1), :] = gain_one
    r.lbuf[0, pl.ds(1, 7), :] = jnp.zeros((7, z.d), F32)
    r.lbuf[0, pl.ds(1, z.heads), : z.nbuck] = grad_rel
    inner = (z.ndp * z.nrow).bit_length() - 1

    def late_done(k):
        if k == inner:
            r.late[...] = r.lbuf[k]

    final = reduce_all(z, me, links, r.lbuf, r.lgot, late_done)
    step(final)
    for copy in zsent:
        copy.wait_recv()
    ysent = []
    for s, w in enumerate(me.rws):
        spot = rows((dp * z.nrow + w) * z.piece, z.piece)
        total = r.gdf[spot, :]
        for i in range(z.ndp - 1):
            total = total + r.zr[i, rows(w * z.piece, z.piece), :].astype(F32)
        if s == 0:
            mine_sum = total
        else:
            r.ys[s - 1] = total.astype(BF16)
            ysent.append(links.send(r.ys.at[s - 1], r.yr.at[s - 1], (dp, w, col)))
    step(final)
    step(early)
    for s, copy in enumerate(ysent):
        copy.wait_recv()
        mine_sum = mine_sum + r.yr[s].astype(F32)
    r.grad_out[...] = mine_sum[:, : z.width].T
    for c in range(3):
        r.grad_qkv[c] = mine_sum[:, (c + 1) * z.width : (c + 2) * z.width]
    for run in (early, final):
        for _ in run:
            pass
    stages = (z.ndp * z.nrow * z.ncol).bit_length() - 1
    r.small[...] = r.ebuf[stages]
    r.late[pl.ds(0, 1), :] = r.lbuf[stages, pl.ds(0, 1), :]
    for copy in kept:
        copy.wait()
    for copy in swapped:
        copy.wait_recv()
    links.finish()


def sizes(mesh_shape, tokens, segments, rel_table, w_in, router):
    z = types.SimpleNamespace()
    z.ndp, z.nrow, z.ncol = mesh_shape
    z.micro, z.tok, z.d = tokens.shape[0], tokens.shape[2], tokens.shape[3]
    z.length = segments.shape[2]
    z.nbuck, z.heads = rel_table.shape
    z.width = z.d // z.ncol
    z.head = z.width // z.heads
    z.ff = w_in.shape[2]
    z.ffh, z.dr = z.ff // z.nrow, z.d // z.nrow
    z.experts = router.shape[1]
    z.slots_each = max(2, 2 * z.tok // z.experts)
    z.slots = z.experts * z.slots_each
    z.piece = z.d // (z.ndp * z.nrow)
    z.chunk = min(512, z.ffh)
    return z


VM = pl.BlockSpec(memory_space=pltpu.VMEM)
ANY = pl.BlockSpec(memory_space=pl.ANY)


def write_results(z, given, wanted, *refs):
    r = types.SimpleNamespace(**dict(zip(given, refs[: len(given)], strict=True)))
    o = types.SimpleNamespace(**dict(zip(wanted, refs[len(given) :], strict=True)))
    o.gwi[...] = r.gwi[...].astype(F32)
    o.gwd[...] = r.gwd[...].astype(F32)

    @pl.when(pl.program_id(0) == 0)
    def _():
        for name in ("layer_out", "grad_tok", "grad_qkv", "grad_out"):
            getattr(o, name)[...] = getattr(r, name)[...]
        o.router[...] = r.small[: z.experts, :]
        o.rel[...] = r.late[1 : 1 + z.heads, : z.nbuck]
        o.gain_one[...] = r.late[0, :]
        o.gain_two[...] = r.small[z.experts, :]


def fast(mesh_shape, tokens, segments, routes, buckets, gain_attn, w_qkv, w_out, rel_table, gain_ffn, router, w_in,
         w_down, cotangent):
    z = sizes(mesh_shape, tokens, segments, rel_table, w_in, router)
    S = jax.ShapeDtypeStruct
    V = pltpu.VMEM
    sem = pltpu.SemaphoreType.DMA
    rb = jnp.concatenate([buckets[::-1], jnp.full((1,), -1, jnp.int32)])[None]
    stages = (z.ndp * z.nrow * z.ncol).bit_length()
    ins = {
        "tok": tokens[:, 0], "seg": segments, "routes": jnp.swapaxes(routes[:, 0], 1, 2), "rb": rb, "gain": gain_attn,
        "w_qkv": jnp.swapaxes(w_qkv, 0, 1), "w_out": w_out, "rel": rel_table.T, "gain_ffn": gain_ffn, "router": router.T, "cot": cotangent[:, 0],
        "w_in": w_in[0], "w_down": w_down[0],
    }
    outs = {
        "layer_out": S((z.micro, z.tok, z.d), BF16),
        "grad_tok": S((z.micro, z.tok, z.d), F32),
        "grad_qkv": S((3, z.piece, z.width), F32),
        "grad_out": S((z.width, z.piece), F32),
        "small": S((z.experts + 8, z.d), F32),
        "late": S((8, z.d), F32),
        "gwi": S((z.dr, z.ff), BF16),
        "gwd": S((z.ff, z.dr), BF16),
    }
    others, both = z.nrow - 1, z.nrow * z.piece
    scratch = {
        "nrm": V((z.micro, z.length, z.d), BF16),
        "qkv_t": V((z.micro, z.d, z.length), BF16),
        "lse": V((z.micro, 8, z.length), F32),
        "mix": V((z.micro, z.ncol, z.tok, z.width), BF16),
        "mown": V((z.micro, z.ncol, z.tok, z.width), BF16),
        "hidden": V((z.micro, z.tok, z.d), F32),
        "slots": V((z.micro, z.nrow, z.slots, 2 * z.d), BF16),
        "near": V((z.nrow, z.micro, 1, z.tok), jnp.int32),
        "near_rows": V((z.nrow, z.tok, 2 * z.d), BF16),
        "dense": V((z.d, z.d), BF16),
        "wo": V((z.ncol, z.d, z.width), BF16),
        "bias": V((z.heads, z.length, z.length), F32),
        "wi": V((z.d, z.ffh), BF16),
        "wd": V((z.nrow, z.ffh, z.dr), BF16),
        "arr": V((z.micro, z.nrow, z.slots, 2 * z.d), BF16),
        "own_part": V((z.micro, z.slots, 2 * z.d), F32),
        "psend": V((z.micro, others, z.slots, 2 * z.d), BF16),
        "precv": V((z.micro, others, z.slots, 2 * z.d), BF16),
        "back": V((z.micro, z.slots, 2 * z.d), BF16),
        "ret": V((z.micro, z.slots, 2 * z.d), BF16),
        "act": V((z.micro, z.nrow, z.slots, z.ffh), BF16),
        "gpre": V((z.micro, z.nrow, z.slots, z.ffh), BF16),
        "xt": V((z.d, z.micro * z.nrow * z.slots), BF16),
        "pc": V((z.micro, z.ncol, z.tok, z.d), BF16),
        "gh": V((z.micro, z.tok, z.d), F32),
        "gkeep": V((z.micro, z.heads, z.length, z.length), BF16),
        "gj_t": V((z.d, z.length), BF16),
        "gdf": V((z.d, z.d), F32),
        "pb": V((z.micro, z.ncol, z.tok, z.d), BF16),
        "pr": V((z.micro, 2, z.tok, z.d), BF16),
        "px": V((z.micro, z.tok, z.d), BF16),
        "xsum": V((z.micro, z.tok, z.d), BF16),
        "zs": V((z.ndp - 1, both, z.d), BF16),
        "zr": V((z.ndp - 1, both, z.d), BF16),
        "ys": V((others, z.piece, z.d), BF16),
        "yr": V((others, z.piece, z.d), BF16),
        "ebuf": V((stages, z.experts + 8, z.d), F32),
        "egot": V((stages - 1, z.experts + 8, z.d), F32),
        "lbuf": V((stages, 8, z.d), F32),
        "lgot": V((stages - 1, 8, z.d), F32),
        "send_sem": sem((200,)),
        "recv_sem": sem((200,)),
        "here_sem": sem((4,)),
    }
    run = pl.pallas_call(
        functools.partial(layer_kernel, z, [*ins, *outs, *scratch]),
        out_shape=list(outs.values()),
        in_specs=[VM] * (len(ins) - 2) + [ANY] * 2,
        out_specs=[VM] * 6 + [ANY] * 2,
        scratch_shapes=list(scratch.values()),
        compiler_params=pltpu.CompilerParams(collective_id=1, has_side_effects=True, vmem_limit_bytes=63 * 2**20),
        name="layer",
    )
    found = dict(zip(outs, run(*ins.values()), strict=True))
    steps = 6
    whole = lambda shape: pl.BlockSpec(shape, lambda i: (0,) * len(shape))
    cut_in, cut_down = (z.dr // steps, z.ff), (z.ff // steps, z.dr)
    shapes = {
        "layer_out": S((z.micro, z.tok, z.d), BF16),
        "grad_tok": S((z.micro, z.tok, z.d), F32),
        "gain_one": S((z.d,), F32),
        "grad_qkv": S((3, z.piece, z.width), F32),
        "grad_out": S((z.width, z.piece), F32),
        "rel": S((z.heads, z.nbuck), F32),
        "gain_two": S((z.d,), F32),
        "router": S((z.experts, z.d), F32),
        "gwi": S((z.dr, z.ff), F32),
        "gwd": S((z.ff, z.dr), F32),
    }
    by_rows = lambda shape: pl.BlockSpec(shape, lambda i: (i, 0))
    pick = lambda given: [
        by_rows(cut_in) if n == "gwi" else by_rows(cut_down) if n == "gwd" else whole(s.shape) for n, s in given.items()
    ]
    done = pl.pallas_call(
        functools.partial(write_results, z, list(outs), list(shapes)),
        grid=(steps,),
        out_shape=list(shapes.values()),
        in_specs=pick(outs),
        out_specs=pick(shapes),
        compiler_params=pltpu.CompilerParams(vmem_limit_bytes=40 * 2**20),
        name="results",
    )(*found.values())
    d = dict(zip(shapes, done, strict=True))
    return (
        d["layer_out"][:, None], d["grad_tok"][:, None], d["gain_one"], jnp.swapaxes(d["grad_qkv"], 0, 1), d["grad_out"],
        d["rel"].T, d["gain_two"], d["router"].T, d["gwi"][None], d["gwd"][None],
    )


def smooth_act(values):
    return jax.nn.gelu(values, approximate=True)


def plain_normalize(values, gain_vec):
    factor = lax.rsqrt(jnp.mean(values * values, axis=-1, keepdims=True) + EPSILON)
    return (values * factor * gain_vec, factor)


def plain_norm_back(grad_into, values, factor, gain_vec):
    scaled = grad_into * gain_vec
    inner = jnp.mean(scaled * values, axis=-1, keepdims=True)
    return (
        factor * (scaled - values * factor * factor * inner),
        jnp.sum(grad_into * values * factor, axis=0),
    )


def contract_rows(left, right, precision=None):
    return lax.dot_general(
        left,
        right,
        (((0,), (0,)), ((), ())),
        precision=precision,
        preferred_element_type=jnp.float32,
    )


def contract_cols(left, right, precision=None):
    return lax.dot_general(
        left,
        right,
        (((1,), (1,)), ((), ())),
        precision=precision,
        preferred_element_type=jnp.float32,
    )


def spread_rows(offsets, row_first, row_count, length):
    shifted = jnp.roll(offsets, row_first, axis=-1)
    span_width = 2 * length - 1
    tiled_rows = jnp.tile(shifted, (1, row_count))[:, : row_count * span_width]
    return tiled_rows.reshape(offsets.shape[0], row_count, span_width)[:, :, length - 1 :]


def plain_gather_offsets(grads, row_first, length):
    heads_here = grads.shape[0]
    row_count = grads.shape[1]
    span_width = 2 * length - 1
    widened = jnp.pad(grads, ((0, 0), (0, 0), (length - 1, 0)))
    flat_rows = jnp.pad(
        widened.reshape(heads_here, row_count * span_width), ((0, 0), (0, row_count))
    )
    folded = jnp.sum(flat_rows.reshape(heads_here, row_count, 2 * length), axis=1)
    return jnp.roll(folded, -row_first, axis=-1)


def score_block(query_part, key_rows, bias_part, marks_query, marks_keys):
    scores = (
        jnp.einsum("qhd,khd->hqk", query_part, key_rows, preferred_element_type=jnp.float32)
        + bias_part
    )
    same_doc = marks_query[:, None] == marks_keys[None, :]
    return jnp.where(same_doc[None], scores, MASKED)


def fetch_dense(w_qkv, w_out):
    return (
        lax.all_gather(w_qkv, ("dp", "row"), axis=0, tiled=True),
        lax.all_gather(w_out, ("dp", "row"), axis=1, tiled=True),
    )


def fetch_experts(w_in, w_down):
    grown_in, grown_down = (
        lax.all_gather(w_in, "row", axis=1, tiled=True),
        lax.all_gather(w_down, "row", axis=2, tiled=True),
    )
    return (grown_in[0], grown_down[0])


def plain_shards(
    tokens,
    segments,
    routes,
    buckets,
    gain_attn,
    w_qkv,
    w_out,
    rel_table,
    gain_ffn,
    router,
    w_in,
    w_down,
    cotangent,
):
    micro_count = tokens.shape[0]
    tok_rows = tokens.shape[2]
    model_width = tokens.shape[3]
    length = segments.shape[2]
    local_heads = rel_table.shape[1]
    head_size = w_out.shape[0] // local_heads
    local_width = local_heads * head_size
    experts_all = router.shape[1]
    hidden_units = w_in.shape[2]
    capacity = max(2, 2 * tok_rows // experts_all)
    query_block = min(512, length)
    block_starts = list(range(0, length, query_block))
    padded_ids = jnp.concatenate([buckets, jnp.full((1,), -1, jnp.int32)])
    offset_table = (
        padded_ids[:, None] == jnp.arange(rel_table.shape[0], dtype=jnp.int32)[None, :]
    ).astype(jnp.float32)
    offset_bias = jnp.dot(offset_table, rel_table, precision=HIGHEST).T
    block_bias = [
        spread_rows(offset_bias, row_start, query_block, length) for row_start in block_starts
    ]
    expert_ids = jnp.arange(experts_all, dtype=jnp.int32)
    slot_ids = jnp.arange(experts_all * capacity, dtype=jnp.int32)
    saved = []
    outputs = []
    for micro_index in range(micro_count):
        full_qkv, full_out = fetch_dense(w_qkv, w_out)
        full_in, full_down = fetch_experts(w_in, w_down)
        own_rows = tokens[micro_index, 0].astype(jnp.float32)
        whole_rows = lax.all_gather(tokens[micro_index, 0], "col", axis=0, tiled=True).astype(
            jnp.float32
        )
        normed_one = plain_normalize(whole_rows, gain_attn)[0].astype(jnp.bfloat16)
        joined = jnp.einsum(
            "td,dcf->tcf", normed_one, full_qkv, preferred_element_type=jnp.float32
        ).astype(jnp.bfloat16)
        queries = joined[:, 0].reshape(length, local_heads, head_size)
        key_rows = joined[:, 1].reshape(length, local_heads, head_size)
        value_rows = joined[:, 2].reshape(length, local_heads, head_size)
        marks = segments[micro_index, 0]
        mixed_parts = []
        log_sums = []
        for block_index, row_start in enumerate(block_starts):
            scores = score_block(queries, key_rows, block_bias[block_index], marks, marks)
            highest = jnp.max(scores, axis=-1, keepdims=True)
            log_sum = highest + jnp.log(jnp.sum(jnp.exp(scores - highest), axis=-1, keepdims=True))
            weights = jnp.exp(scores - log_sum).astype(jnp.bfloat16)
            mixed_parts.append(
                jnp.einsum(
                    "hqk,khd->qhd", weights, value_rows, preferred_element_type=jnp.float32
                ).astype(jnp.bfloat16)
            )
            log_sums.append(log_sum)
        mixed = mixed_parts[0].reshape(length, local_width)
        hidden = own_rows + lax.psum_scatter(
            jnp.dot(mixed, full_out, preferred_element_type=jnp.float32),
            "col",
            scatter_dimension=0,
            tiled=True,
        )
        normed_two, factor_two = plain_normalize(hidden, gain_ffn)
        chances = jax.nn.softmax(jnp.dot(normed_two, router, precision=HIGHEST), axis=-1)
        chosen = routes[micro_index, 0, :, 0]
        picked = chosen[:, None] == expert_ids[None, :]
        gate_value = jnp.sum(jnp.where(picked, chances, 0.0), axis=-1)
        picked_int = picked.astype(jnp.int32)
        ranks = jnp.sum((jnp.cumsum(picked_int, axis=0) - picked_int) * picked_int, axis=1)
        placement = ((chosen * capacity + ranks)[:, None] == slot_ids[None, :]).astype(jnp.bfloat16)
        outgoing = contract_rows(placement, normed_two.astype(jnp.bfloat16)).astype(jnp.bfloat16)
        outgoing = outgoing.reshape(experts_all, capacity, model_width)
        arrived = lax.all_to_all(outgoing, ("dp", "col"), split_axis=0, concat_axis=0, tiled=True)
        flat_in = arrived.reshape(-1, model_width)
        before = jnp.dot(flat_in, full_in, preferred_element_type=jnp.float32)
        active = smooth_act(before).astype(jnp.bfloat16)
        result = jnp.dot(active, full_down, preferred_element_type=jnp.float32).astype(jnp.bfloat16)
        sent_back = lax.all_to_all(
            result.reshape(arrived.shape), ("dp", "col"), split_axis=0, concat_axis=0, tiled=True
        )
        sent_back, arrived, before_all = (
            sent_back,
            arrived,
            before.reshape(arrived.shape[0], arrived.shape[1], hidden_units),
        )
        expert_out = jnp.dot(
            placement, sent_back.reshape(-1, model_width), preferred_element_type=jnp.float32
        )
        outputs.append((hidden + gate_value[:, None] * expert_out).astype(jnp.bfloat16))
        saved.append(
            (
                own_rows,
                normed_one,
                queries,
                key_rows,
                value_rows,
                marks,
                log_sums,
                mixed,
                hidden,
                normed_two,
                factor_two,
                chances,
                picked,
                gate_value,
                placement,
                expert_out,
                arrived,
                before_all,
            )
        )
    grad_qkv_sum = jnp.zeros((model_width, 3, local_width), jnp.float32)
    grad_out_sum = jnp.zeros((local_width, model_width), jnp.float32)
    grad_in_sum = jnp.zeros((model_width, hidden_units), jnp.float32)
    grad_down_sum = jnp.zeros((hidden_units, model_width), jnp.float32)
    grad_offsets = jnp.zeros((local_heads, 2 * length), jnp.float32)
    grad_gain_one = jnp.zeros((model_width,), jnp.float32)
    grad_gain_two = jnp.zeros((model_width,), jnp.float32)
    grad_router_sum = jnp.zeros(router.shape, jnp.float32)
    grads_input = []
    for micro_index in range(micro_count):
        (
            own_rows,
            normed_one,
            queries,
            key_rows,
            value_rows,
            marks,
            log_sums,
            mixed,
            hidden,
            normed_two,
            factor_two,
            chances,
            picked,
            gate_value,
            placement,
            expert_out,
            arrived,
            before_all,
        ) = saved[micro_index]
        full_qkv, full_out = fetch_dense(w_qkv, w_out)
        full_in, full_down = fetch_experts(w_in, w_down)
        upstream = cotangent[micro_index, 0].astype(jnp.float32)
        grad_gate = jnp.sum(upstream * expert_out, axis=-1)
        grad_result = (gate_value[:, None] * upstream).astype(jnp.bfloat16)
        to_slots = contract_rows(placement, grad_result).astype(jnp.bfloat16)
        to_slots = to_slots.reshape(experts_all, capacity, model_width)
        at_expert = lax.all_to_all(
            to_slots, ("dp", "col"), split_axis=0, concat_axis=0, tiled=True
        ).reshape(-1, model_width)
        flat_before = before_all.reshape(-1, hidden_units)
        act_value, act_pull = jax.vjp(smooth_act, flat_before)
        flat_active = act_value.astype(jnp.bfloat16)
        grad_down_sum = grad_down_sum + contract_rows(flat_active, at_expert)
        grad_active = contract_cols(at_expert, full_down)
        grad_before = act_pull(grad_active)[0].astype(jnp.bfloat16)
        grad_in_sum = grad_in_sum + contract_rows(arrived.reshape(-1, model_width), grad_before)
        grad_sent = (
            contract_cols(grad_before, full_in)
            .astype(jnp.bfloat16)
            .reshape(experts_all, capacity, model_width)
        )
        came_back = lax.all_to_all(
            grad_sent, ("dp", "col"), split_axis=0, concat_axis=0, tiled=True
        )
        grad_normed_two = jnp.dot(
            placement, came_back.reshape(-1, model_width), preferred_element_type=jnp.float32
        )
        grad_logits = (grad_gate * gate_value)[:, None] * (picked.astype(jnp.float32) - chances)
        grad_router_sum = grad_router_sum + contract_rows(normed_two, grad_logits, HIGHEST)
        grad_normed_two = grad_normed_two + contract_cols(grad_logits, router, HIGHEST)
        grad_norm_part, gain_part = plain_norm_back(grad_normed_two, hidden, factor_two, gain_ffn)
        grad_gain_two = grad_gain_two + gain_part
        grad_hidden = upstream + grad_norm_part
        piece = lax.all_gather(grad_hidden.astype(jnp.bfloat16), "col", axis=0, tiled=True)
        total_out = grad_out_sum
        total_out = total_out + contract_rows(mixed, piece)
        spread_grad = contract_cols(piece, full_out)
        grad_out_sum = total_out
        grad_mixed = spread_grad
        grad_mixed = grad_mixed.astype(jnp.bfloat16).reshape(length, local_heads, head_size)
        grad_keys = jnp.zeros((length, local_heads, head_size), jnp.float32)
        grad_values = jnp.zeros((length, local_heads, head_size), jnp.float32)
        query_grads = []
        for block_index, row_start in enumerate(block_starts):
            scores = score_block(queries, key_rows, block_bias[block_index], marks, marks)
            weights = jnp.exp(scores - log_sums[block_index])
            grad_values = jnp.einsum(
                "hqk,qhd->khd",
                weights.astype(jnp.bfloat16),
                grad_mixed,
                preferred_element_type=jnp.float32,
            )
            grad_weights = jnp.einsum(
                "qhd,khd->hqk", grad_mixed, value_rows, preferred_element_type=jnp.float32
            )
            grad_scores = (
                weights * (grad_weights - jnp.sum(weights * grad_weights, axis=-1, keepdims=True))
            ).astype(jnp.bfloat16)
            grad_offsets = grad_offsets + plain_gather_offsets(
                grad_scores.astype(jnp.float32), row_start, length
            )
            query_grads.append(
                jnp.einsum(
                    "hqk,khd->qhd", grad_scores, key_rows, preferred_element_type=jnp.float32
                )
            )
            grad_keys = jnp.einsum(
                "hqk,qhd->khd", grad_scores, queries, preferred_element_type=jnp.float32
            )
        grad_joined = jnp.stack([query_grads[0], grad_keys, grad_values], axis=1)
        grad_joined = grad_joined.reshape(length, 3, local_width).astype(jnp.bfloat16)
        grad_qkv_sum = grad_qkv_sum + jnp.einsum(
            "td,tcf->dcf", normed_one, grad_joined, preferred_element_type=jnp.float32
        )
        grad_normed_one = lax.psum_scatter(
            jnp.einsum(
                "tcf,dcf->td", grad_joined, full_qkv, preferred_element_type=jnp.float32
            ).astype(jnp.bfloat16),
            "col",
            scatter_dimension=0,
            tiled=True,
        ).astype(jnp.float32)
        factor_one = plain_normalize(own_rows, gain_attn)[1]
        grad_input_part, gain_part = plain_norm_back(grad_normed_one, own_rows, factor_one, gain_attn)
        grad_gain_one = grad_gain_one + gain_part
        grads_input.append(grad_hidden + grad_input_part)
    grad_rel_mine = jnp.dot(offset_table.T, grad_offsets.T, precision=HIGHEST)
    heads_all = local_heads * lax.axis_size("col")
    head_first = lax.axis_index("col") * local_heads
    rel_full = lax.dynamic_update_slice_in_dim(
        jnp.zeros((rel_table.shape[0], heads_all), jnp.float32), grad_rel_mine, head_first, 1
    )
    total_gain_one, total_gain_two, total_router, total_rel = lax.psum(
        (grad_gain_one, grad_gain_two, grad_router_sum, rel_full), ("dp", "row", "col")
    )
    rel_out = lax.dynamic_slice_in_dim(total_rel, head_first, local_heads, 1)
    dense_qkv, dense_out = (
        lax.psum_scatter(grad_qkv_sum, ("dp", "row"), scatter_dimension=0, tiled=True),
        lax.psum_scatter(grad_out_sum, ("dp", "row"), scatter_dimension=1, tiled=True),
    )
    expert_in, expert_down = (
        lax.psum_scatter(
            grad_in_sum[None].astype(jnp.bfloat16), "row", scatter_dimension=1, tiled=True
        ).astype(jnp.float32),
        lax.psum_scatter(
            grad_down_sum[None].astype(jnp.bfloat16), "row", scatter_dimension=2, tiled=True
        ).astype(jnp.float32),
    )
    layer_out = jnp.stack(outputs)[:, None]
    grad_tokens = jnp.stack(grads_input)[:, None]
    return (
        layer_out,
        grad_tokens,
        total_gain_one,
        dense_qkv,
        dense_out,
        rel_out,
        total_gain_two,
        total_router,
        expert_in,
        expert_down,
    )


def solution(mesh):
    shape = tuple(mesh.shape[a] for a in ("dp", "row", "col"))
    token_spec, expert_in, expert_down = P(None, ("dp", "row"), "col", None), P(("dp", "col"), "row", None), P(("dp", "col"), None, "row")
    qkv_spec, out_spec = P(("dp", "row"), None, "col"), P("col", ("dp", "row"))
    in_specs = (
        token_spec, P(None, ("dp", "row"), None), token_spec, P(), P(), qkv_spec, out_spec, P(None, "col"), P(), P(),
        expert_in, expert_down, token_spec,
    )
    out_specs = (token_spec, token_spec, P(), qkv_spec, out_spec, P(None, "col"), P(), P(), expert_in, expert_down)

    def run(*args):
        piece, each = args[5].shape[0] // (shape[0] * shape[1]), 2 * args[0].shape[2] // shape[2] // args[9].shape[1]
        whole_tiles = piece % 16 == 0 and each % 16 == 0 and shape[2] == 4 and args[0].shape[0] == 2
        body = functools.partial(fast, shape) if whole_tiles else plain_shards
        return jax.shard_map(body, mesh=mesh, in_specs=in_specs, out_specs=out_specs, check_vma=False)(*args)

    return run
```

```python
import functools
import types

import jax
import jax.numpy as jnp
from jax import lax
from jax.experimental import pallas as pl
from jax.experimental.pallas import tpu as pltpu
from jax.sharding import PartitionSpec as P

EPSILON = 1e-06
HIGHEST = lax.Precision.HIGHEST
MASKED = -1000000000.0
MESH = pl.DeviceIdType.MESH
F32 = jnp.float32
BF16 = jnp.bfloat16
NN = (((1,), (0,)), ((), ()))
NT = (((1,), (1,)), ((), ()))
TN = (((0,), (0,)), ((), ()))


def mm(left, right, dims=NN, precision=None):
    return lax.dot_general(left, right, dims, precision=precision, preferred_element_type=F32)


def rows(first, count):
    return pl.ds(pl.multiple_of(first, count), count)


class Links:
    def __init__(self, send_sem, recv_sem):
        self.send_sem, self.recv_sem, self.used, self.started = send_sem, recv_sem, 0, []

    def send(self, src, dst, device):
        k = self.used
        self.used += 1
        copy = pltpu.make_async_remote_copy(
            src_ref=src, dst_ref=dst, send_sem=self.send_sem.at[k], recv_sem=self.recv_sem.at[k],
            device_id=device, device_id_type=MESH,
        )
        copy.start()
        self.started.append(copy)
        return copy

    def finish(self):
        for copy in self.started:
            copy.wait_send()


class Place:
    def __init__(self, z):
        self.dp, self.row, self.col = lax.axis_index("dp"), lax.axis_index("row"), lax.axis_index("col")
        dp, row, col = self.dp, self.row, self.col
        self.dps = [lax.rem(dp + i, z.ndp) for i in range(z.ndp)]
        self.rws = [lax.rem(row + i, z.nrow) for i in range(z.nrow)]
        self.cls = [lax.rem(col + i, z.ncol) for i in range(z.ncol)]
        self.dps_back = [lax.rem(dp + z.ndp - i, z.ndp) for i in range(z.ndp)]
        self.rws_back = [lax.rem(row + z.nrow - i, z.nrow) for i in range(z.nrow)]
        self.cls_back = [lax.rem(col + z.ncol - i, z.ncol) for i in range(z.ncol)]
        self.across = lax.rem(col + 2, z.ncol)
        self.beside = col + 1 - 2 * lax.rem(col, 2)
        self.far = lax.rem(self.beside + 2, z.ncol)


def greet(devices):
    barrier = pltpu.get_barrier_semaphore()
    for device in devices:
        pl.semaphore_signal(barrier, inc=1, device_id=device, device_id_type=MESH)
    return lambda: pl.semaphore_wait(barrier, len(devices))


def norm_rows(values):
    return lax.rsqrt(jnp.mean(values * values, axis=-1, keepdims=True) + EPSILON)


def norm_back(grad_into, values, factor, gain_vec):
    scaled = grad_into * gain_vec
    inner = jnp.mean(scaled * values, axis=-1, keepdims=True)
    return (
        factor * (scaled - values * factor * factor * inner),
        jnp.sum(grad_into * values * factor, axis=0, keepdims=True),
    )


def column(line):
    return jnp.broadcast_to(line.astype(F32), (8, line.shape[1])).T[:, :1]


def offset_table(z, rb):
    ids = lax.broadcasted_iota(jnp.int32, (z.nbuck, 2 * z.length), 0)
    return (ids == rb[...]).astype(F32)


def make_bias(z, rb, rel, bias):
    offsets = mm(rel[...], offset_table(z, rb), NN, HIGHEST)
    for h in range(z.heads):
        spread = jnp.broadcast_to(offsets[h : h + 1, :], (z.length, 2 * z.length))
        turned = pltpu.roll(spread, z.length + 1, 1, stride=1, stride_axis=0)
        bias[h] = turned[:, : z.length]


def gather_offsets(values):
    count = values.shape[0] // 2
    while count >= 1:
        values = pltpu.roll(values[:count], count, 1) + values[count:]
        count //= 2
    return values


def routing(z, chosen):
    ids = lax.broadcasted_iota(jnp.int32, (z.tok, z.experts), 1).astype(F32)
    picked = chosen == ids
    before = (
        lax.broadcasted_iota(jnp.int32, (z.tok, z.tok), 0) > lax.broadcasted_iota(jnp.int32, (z.tok, z.tok), 1)
    ).astype(BF16)
    counts = mm(before, picked.astype(BF16))
    ranks = jnp.sum(jnp.where(picked, counts, 0.0), axis=1, keepdims=True)
    slot = chosen * z.slots_each + ranks
    placement = (slot == lax.broadcasted_iota(jnp.int32, (z.tok, z.slots), 1).astype(F32)).astype(BF16)
    return picked, placement


def softmax_rows(logits):
    top = jnp.exp(logits - jnp.max(logits, axis=-1, keepdims=True))
    return top / jnp.sum(top, axis=-1, keepdims=True)


def gelu_both(before):
    inner = 0.7978845608 * (before + 0.044715 * before * before * before)
    t = jnp.tanh(inner)
    half = 0.5 * (1.0 + t)
    slope = half + 0.5 * before * (1.0 - t * t) * (0.7978845608 * (1.0 + 3.0 * 0.044715 * before * before))
    return before * half, slope


def partner(index, step):
    return index + step - 2 * step * lax.rem(index // step, 2)


def reduce_all(z, me, links, buf, got, per_col=0):
    dp, row, col = me.dp, me.row, me.col
    for k in range(2):
        copy = links.send(buf.at[k], got.at[k], (dp, row, partner(col, 1 + k)))
        yield
        copy.wait_recv()
        term = got[k]
        if per_col:
            line = lax.broadcasted_iota(jnp.int32, term.shape, 0)
            term = jnp.where(line < term.shape[0] - per_col, term, 0.0)
        buf[k + 1] = buf[k] + term
    first = 2
    for k, size, mine, others in (
        (2, z.ndp, dp, [(d, row, col) for d in me.dps[1:]]), (3, z.nrow, row, [(dp, w, col) for w in me.rws[1:]])
    ):
        copies = [links.send(buf.at[k], got.at[first + mine], device) for device in others]
        got[first + mine] = buf[k]
        yield
        for copy in copies:
            copy.wait_recv()
        total = got[first]
        for i in range(1, size):
            total = total + got[first + i]
        buf[k + 1] = total
        first += size


def attention_forward(z, r, m):
    seg = r.seg[m]
    same = column(seg) == seg.astype(F32)
    parts = []
    for h in range(z.heads):
        q_t, k_t, v_t = (r.qkv_t[m, pl.ds((c + 1) * z.width + h * z.head, z.head), :] for c in range(3))
        scores = jnp.where(same, mm(k_t, q_t, TN) + r.bias[h], MASKED)
        highest = jnp.max(scores, axis=0, keepdims=True)
        raised = jnp.exp(scores - highest)
        total = jnp.sum(raised, axis=0, keepdims=True)
        r.lse[m, pl.ds(h, 1), :] = highest + jnp.log(total)
        probs = (raised * (1.0 / total)).astype(BF16)
        parts.append(mm(v_t, probs))
    mixed = jnp.concatenate(parts, axis=0).T.astype(BF16)
    for c in range(z.ncol):
        r.mix[m, c] = mixed[c * z.tok : (c + 1) * z.tok]


def attention_backward(z, r, m, grad_t, heads):
    seg = r.seg[m]
    same = column(seg) == seg.astype(F32)
    for h in heads:
        q_t, k_t, v_t = (r.qkv_t[m, pl.ds((c + 1) * z.width + h * z.head, z.head), :] for c in range(3))
        g_t = grad_t[h * z.head : (h + 1) * z.head, :]
        scores = jnp.where(same, mm(k_t, q_t, TN) + r.bias[h], MASKED)
        probs = jnp.exp(scores - r.lse[m, pl.ds(h, 1), :])
        grad_probs = mm(v_t, g_t, TN)
        delta = jnp.sum(probs * grad_probs, axis=0, keepdims=True)
        grads = (probs * (grad_probs - delta)).astype(BF16)
        r.gkeep[m, h] = grads
        for c, part in enumerate((mm(k_t, grads), mm(q_t, grads, NT), mm(g_t, probs.astype(BF16), NT))):
            r.gj_t[pl.ds((c + 1) * z.width + h * z.head, z.head), :] = part.astype(BF16)


def layer_kernel(z, names, *refs):
    r = types.SimpleNamespace(**dict(zip(names, refs, strict=True)))
    me = Place(z)
    dp, row, col = me.dp, me.row, me.col
    links = Links(r.send_sem, r.recv_sem)
    plane = [(i, j) for i in range(z.ndp) for j in range(z.ncol) if (i, j) != (0, 0)]
    arrived = greet([(me.dps[i], row, me.cls[j]) for i, j in plane] + [(dp, w, col) for w in me.rws[1:]])
    gain, gain_ffn = r.gain[...].reshape(1, z.d), r.gain_ffn[...].reshape(1, z.d)
    micros = range(z.micro)

    own = [
        pltpu.make_async_copy(r.w_in.at[:, rows(row * z.ffh, z.ffh)], r.wi.at[rows(row * z.dr, z.dr), :], r.here_sem.at[0]),
        pltpu.make_async_copy(r.w_down.at[rows(row * z.ffh, z.ffh), :], r.wd.at[row], r.here_sem.at[1]),
    ]
    for copy in own:
        copy.start()
    pid = dp * z.nrow + row
    piece = lambda p: r.dense.at[rows(p * z.piece, z.piece), :]
    r.dense[rows(pid * z.piece, z.piece), :] = jnp.concatenate(
        [r.w_out[...].astype(F32).T.astype(BF16)] + [r.w_qkv[c] for c in range(3)], axis=1
    )
    for m in micros:
        values = r.tok[m].astype(F32)
        r.nrm[m, rows(col * z.tok, z.tok), :] = (values * norm_rows(values) * gain).astype(BF16)
    arrived()

    dense_y = [links.send(piece(pid), piece(pid), (dp, w, col)) for w in me.rws[1:]]
    dense_z = [links.send(piece(pid), piece(pid), (d, row, col)) for d in me.dps[1:]]
    block = lambda m, c: r.nrm.at[m, rows(c * z.tok, z.tok), :]
    xs = [links.send(block(m, col), block(m, col), (dp, row, me.across)) for m in micros]
    cs = [links.send(block(m, col), block(m, col), (dp, row, me.beside)) for m in micros]
    routes = [links.send(r.routes, r.near.at[row], (dp, w, col)) for w in me.rws[1:]]
    experts = []
    for w in me.rws[1:]:
        experts.append(links.send(r.w_in.at[:, rows(w * z.ffh, z.ffh)], r.wi.at[rows(row * z.dr, z.dr), :], (dp, w, col)))
        experts.append(links.send(r.w_down.at[rows(w * z.ffh, z.ffh), :], r.wd.at[row], (dp, w, col)))
    for s, copy in enumerate(dense_y):
        copy.wait_recv()
        p = dp * z.nrow + me.rws_back[s + 1]
        dense_z += [links.send(piece(p), piece(p), (d, row, col)) for d in me.dps[1:]]
    make_bias(z, r.rb, r.rel, r.bias)
    fs = []
    for m in micros:
        xs[m].wait_recv()
        fs.append(links.send(block(m, me.across), block(m, me.across), (dp, row, me.beside)))
    for copy in dense_z + cs + fs:
        copy.wait_recv()

    r.wo[col] = r.dense[:, : z.width]
    wx = links.send(r.wo.at[col], r.wo.at[col], (dp, row, me.across))
    wc = links.send(r.wo.at[col], r.wo.at[col], (dp, row, me.beside))
    swaps = []
    for m in micros:
        r.qkv_t[m] = mm(r.nrm[m], r.dense[...]).astype(BF16).T
        attention_forward(z, r, m)
        swaps.append([links.send(r.mix.at[m, c], r.mown.at[m, col], (dp, row, c)) for c in me.cls[1:]])
        r.mown[m, col] = r.mix[m, col]
        if m == 0:
            wx.wait_recv()
            wf = links.send(r.wo.at[me.across], r.wo.at[me.across], (dp, row, me.beside))
    wc.wait_recv()
    wf.wait_recv()

    mine = dp * z.ncol + col
    each = z.slots_each
    group = z.ncol * each
    dispatch = []

    def spread(m, w, slots):
        r.slots[m, w] = slots
        copies = {}
        for i, j in plane[::-1]:
            e = me.dps[i] * z.ncol + me.cls[j]
            copies[i, j] = links.send(
                r.slots.at[m, w, rows(e * each, each), :], r.arr.at[m, w, rows(mine * each, each), :],
                (me.dps[i], row, me.cls[j]),
            )
        r.arr[m, w, rows(mine * each, each), :] = r.slots[m, w, rows(mine * each, each), :]
        return copies

    for m in micros:
        for copy in swaps[m]:
            copy.wait_recv()
        values = r.tok[m].astype(F32)
        for c in range(z.ncol):
            values = values + mm(r.mown[m, c], r.wo[c], NT)
        r.hidden[m] = values
        normed = values * norm_rows(values) * gain_ffn
        chances = softmax_rows(mm(normed, r.router[...], NT, HIGHEST))
        picked, placement = routing(z, column(r.routes[m]))
        gate = jnp.sum(jnp.where(picked, chances, 0.0), axis=-1, keepdims=True)
        sent = jnp.concatenate([normed.astype(BF16), (gate * r.cot[m].astype(F32)).astype(BF16)], axis=1)
        if m == z.micro - 1:
            r.near_rows[row] = sent
            crossing = [links.send(r.near_rows.at[row], r.near_rows.at[row], (dp, w, col)) for w in me.rws[1:]]
        dispatch.append(spread(m, row, mm(placement, sent, TN).astype(BF16)))

    forwards = []
    for m in micros[:-1]:
        copies = {}
        for i in range(z.ndp):
            for j in range(z.ncol):
                if (i, j) != (0, 0):
                    dispatch[m][i, j].wait_recv()
            part = r.arr.at[m, row, rows(me.dps_back[i] * group, group), :]
            for s, w in enumerate(me.rws[1:]):
                copies[i, s] = links.send(part, part, (dp, w, col))
        forwards.append(copies)

    for copy in routes + crossing:
        copy.wait_recv()
    cross = {}
    for s in range(z.nrow - 1):
        w = me.rws_back[s + 1]
        placement = routing(z, column(r.near[w, z.micro - 1]))[1]
        cross[s] = spread(z.micro - 1, w, mm(placement, r.near_rows[w], TN).astype(BF16))

    def expert(m, w, store):
        x = r.arr[m, w, :, : z.d]
        g = r.arr[m, w, :, z.d :]
        result = jnp.zeros((z.slots, z.d), F32)
        grad = jnp.zeros((z.slots, z.d), F32)
        for k in range(z.ffh // z.chunk):
            cut = pl.ds(k * z.chunk, z.chunk)
            w_one = r.wi[:, cut]
            w_two = jnp.concatenate([r.wd[p, cut, :] for p in range(z.nrow)], axis=1)
            value, slope = gelu_both(mm(x, w_one))
            value = value.astype(BF16)
            r.act[m, w, :, cut] = value
            result = result + mm(value, w_two)
            pre = (mm(g, w_two, NT) * slope).astype(BF16)
            r.gpre[m, w, :, cut] = pre
            grad = grad + mm(pre, w_one, NT)
        store(result, grad)

    for copy in own:
        copy.wait()
    for copy in experts:
        copy.wait_recv()
    partials = []
    order = [*range(1, z.ndp), 0]
    for m in micros:

        def store_own(result, grad, m=m):
            r.own_part[m, :, : z.d] = result
            r.own_part[m, :, z.d :] = grad

        if m == z.micro - 1:
            for copy in dispatch[m].values():
                copy.wait_recv()
        expert(m, row, store_own)
        for copies in (forwards[m],) if m < z.micro - 1 else cross.values():
            for copy in copies.values():
                copy.wait_recv()
        copies = {}
        for s, w in enumerate(me.rws[1:]):

            def store(result, grad, m=m, s=s):
                r.psend[m, s, :, : z.d] = result.astype(BF16)
                r.psend[m, s, :, z.d :] = grad.astype(BF16)

            expert(m, w, store)
            for i in order:
                spot = rows(me.dps[i] * group, group)
                copies[i, s] = links.send(r.psend.at[m, s, spot, :], r.precv.at[m, s, spot, :], (dp, w, col))
        partials.append(copies)

    def go_home(m):
        home = []
        for i in order:
            spot = rows(me.dps[i] * group, group)
            total = r.own_part[m, spot, :]
            for s in range(z.nrow - 1):
                partials[m][i, s].wait_recv()
                total = total + r.precv[m, s, spot, :].astype(F32)
            r.back[m, spot, :] = total.astype(BF16)
            for j in range(z.ncol):
                if (i, j) != (0, 0):
                    e = me.dps[i] * z.ncol + me.cls[j]
                    home.append(
                        links.send(
                            r.back.at[m, rows(e * each, each), :], r.ret.at[m, rows(mine * each, each), :],
                            (me.dps[i], row, me.cls[j]),
                        )
                    )
        r.ret[m, rows(mine * each, each), :] = r.back[m, rows(mine * each, each), :]
        return home

    returns = [go_home(m) for m in micros[:-1]]

    blocks = [(m, w) for m in micros for w in range(z.nrow)]
    for b, (m, w) in enumerate(blocks):
        r.xt[:, b * z.slots : (b + 1) * z.slots] = r.arr[m, w, :, : z.d].T
    for k in range(z.ffh // z.chunk):
        cut = pl.ds(k * z.chunk, z.chunk)
        pre = jnp.concatenate([r.gpre[m, w, :, cut] for m, w in blocks], axis=0)
        value = jnp.concatenate([r.act[m, w, :, cut] for m, w in blocks], axis=0)
        g = jnp.concatenate([r.arr[m, w, :, z.d :] for m, w in blocks], axis=0)
        r.wi[:, cut] = mm(r.xt[...], pre).astype(BF16)
        grad_down = mm(value, g, TN).astype(BF16)
        for p in range(z.nrow):
            r.wd[p, cut, :] = grad_down[:, p * z.dr : (p + 1) * z.dr]

    def token_back(m):
        for copy in returns[m]:
            copy.wait_recv()
        values = r.hidden[m]
        factor = norm_rows(values)
        normed = values * factor * gain_ffn
        chances = softmax_rows(mm(normed, r.router[...], NT, HIGHEST))
        picked, placement = routing(z, column(r.routes[m]))
        gate = jnp.sum(jnp.where(picked, chances, 0.0), axis=-1, keepdims=True)
        came = mm(placement, r.ret[m])
        returned, grad_sent = came[:, : z.d], came[:, z.d :]
        r.layer_out[m] = (values + gate * returned).astype(BF16)
        upstream = r.cot[m].astype(F32)
        grad_gate = jnp.sum(upstream * returned, axis=-1, keepdims=True)
        grad_logits = grad_gate * gate * (picked.astype(F32) - chances)
        grad_normed = grad_sent + mm(grad_logits, r.router[...], NN, HIGHEST)
        part, gain_part = norm_back(grad_normed, values, factor, gain_ffn)
        grad_hidden = upstream + part
        r.gh[m] = grad_hidden
        r.pc[m, col] = grad_hidden.astype(BF16)
        across = links.send(r.pc.at[m, col], r.pc.at[m, col], (dp, row, me.across))
        beside = links.send(r.pc.at[m, col], r.pc.at[m, col], (dp, row, me.beside))
        return across, beside, mm(grad_logits, normed, TN, HIGHEST), gain_part

    step = lambda run: next(run, None)
    wire = []

    def all_rows(m, sends):
        across, beside = sends
        across.wait_recv()
        passed = links.send(r.pc.at[m, me.across], r.pc.at[m, me.across], (dp, row, me.beside))
        beside.wait_recv()
        passed.wait_recv()
        return r.pc[m].reshape(z.length, z.d)

    def into_heads(branch):
        return mm(branch, r.dense[:, : z.width]).astype(BF16).T

    def first_norm_rows(m, gj):
        partial = mm(gj, r.dense[...], NT).astype(BF16)
        for c in range(z.ncol):
            r.pb[m, c] = partial[c * z.tok : (c + 1) * z.tok]
        wire.append([links.send(r.pb.at[m, me.far], r.pr.at[m, 1], (dp, row, me.beside)),
                     links.send(r.pb.at[m, me.beside], r.pr.at[m, 0], (dp, row, me.beside))])

    def across_chips(m):
        wire[m][0].wait_recv()
        r.xsum[m] = (r.pb[m, me.across].astype(F32) + r.pr[m, 1].astype(F32)).astype(BF16)
        wire[m].append(links.send(r.xsum.at[m], r.px.at[m], (dp, row, me.across)))

    both = z.nrow * z.piece

    def reduce_over_dp(total, out, got):
        sends = []
        for i, d in enumerate(me.dps[1:]):
            out[i] = total[rows(d * both, both), :].astype(BF16)
            sends.append(links.send(out.at[i], got.at[i], (d, row, col)))
        return sends

    def sum_here(w, total, got):
        spot = rows((dp * z.nrow + w) * z.piece, z.piece)
        value = total[spot, :]
        for i in range(z.ndp - 1):
            value = value + got[i, rows(w * z.piece, z.piece), :].astype(F32)
        return value

    across, beside, router_t, gain_two = token_back(0)
    pcs = [(across, beside)]
    returns.append(go_home(1))
    kept = [
        pltpu.make_async_copy(r.wi.at[rows(row * z.dr, z.dr), :], r.gwi.at[:, rows(row * z.ffh, z.ffh)], r.here_sem.at[2]),
        pltpu.make_async_copy(r.wd.at[row], r.gwd.at[rows(row * z.ffh, z.ffh), :], r.here_sem.at[3]),
    ]
    for copy in kept:
        copy.start()
    swapped = []

    def swap_grads(first, last, parts):
        for w in me.rws[1:]:
            for k in range(first, last):
                n = z.dr // parts
                swapped.append(links.send(
                    r.wi.at[rows(w * z.dr + k * n, n), :], r.gwi.at[pl.ds(k * n, n), rows(row * z.ffh, z.ffh)], (dp, w, col)
                ))
                n = z.ffh // parts
                swapped.append(links.send(
                    r.wd.at[w, pl.ds(k * n, n), :], r.gwd.at[rows(row * z.ffh + k * n, n), :], (dp, w, col)
                ))

    swap_grads(0, 4, 4)
    branch = all_rows(0, pcs[0])
    grad_t = into_heads(branch)
    r.gj_t[: z.width, :] = jnp.zeros((z.width, z.length), BF16)
    attention_backward(z, r, 0, grad_t, [0])
    across, beside, router_part, gain_part = token_back(1)
    pcs.append((across, beside))
    r.ebuf[0] = jnp.concatenate([router_t + router_part, gain_two + gain_part, jnp.zeros((7, z.d), F32)], axis=0)
    early = reduce_all(z, me, links, r.ebuf, r.egot)
    step(early)
    attention_backward(z, r, 0, grad_t, range(1, z.heads))
    gj = r.gj_t[...].T
    first_norm_rows(0, gj)
    r.gdq[...] = mm(r.nrm[0], gj, TN)[:, z.width :]
    out_part = mm(branch, r.mix[0].reshape(z.length, z.width), TN)
    step(early)
    across_chips(0)
    branch = all_rows(1, pcs[1])
    r.gdo[...] = out_part + mm(branch, r.mix[1].reshape(z.length, z.width), TN)
    out_sent = reduce_over_dp(r.gdo, r.zo, r.zo_got)
    grad_t = into_heads(branch)
    step(early)
    attention_backward(z, r, 1, grad_t, range(z.heads))
    gj = r.gj_t[...].T
    r.gdq[...] = r.gdq[...] + mm(r.nrm[1], gj, TN)[:, z.width :]
    qkv_sent = reduce_over_dp(r.gdq, r.zq, r.zq_got)
    first_norm_rows(1, gj)
    step(early)
    across_chips(1)
    offsets = []
    for h in range(z.heads):
        total = r.gkeep[0, h].astype(F32)
        for m in range(1, z.micro):
            total = total + r.gkeep[m, h].astype(F32)
        offsets.append(gather_offsets(jnp.concatenate([total, jnp.zeros((z.length, z.length), F32)], axis=1)))
    grad_rel = mm(jnp.concatenate(offsets, axis=0), offset_table(z, r.rb), NT, HIGHEST)
    gain_one = jnp.zeros((1, z.d), F32)
    for m in micros:
        wire[m][1].wait_recv()
        wire[m][2].wait_recv()
        grad_normed = r.pb[m, col].astype(F32) + r.pr[m, 0].astype(F32) + r.px[m].astype(F32)
        values = r.tok[m].astype(F32)
        part, gain_part = norm_back(grad_normed, values, norm_rows(values), gain)
        gain_one = gain_one + gain_part
        r.grad_tok[m] = r.gh[m] + part
    r.lbuf[0, pl.ds(0, 1), :] = gain_one
    r.lbuf[0, pl.ds(1, 7), :] = jnp.zeros((7, z.d), F32)
    r.lbuf[0, pl.ds(1, z.heads), : z.nbuck] = grad_rel
    final = reduce_all(z, me, links, r.lbuf, r.lgot, 7)
    for _ in range(3):
        step(final)
    for copy in out_sent:
        copy.wait_recv()
    ysent = []
    for s, w in enumerate(me.rws[1:]):
        r.yo[s] = sum_here(w, r.gdo, r.zo_got).astype(BF16)
        ysent.append(links.send(r.yo.at[s], r.yo_got.at[s], (dp, w, col)))
    for copy in qkv_sent:
        copy.wait_recv()
    for s, w in enumerate(me.rws[1:]):
        r.yq[s] = sum_here(w, r.gdq, r.zq_got).astype(BF16)
        ysent.append(links.send(r.yq.at[s], r.yq_got.at[s], (dp, w, col)))
    step(final)
    out_sum = sum_here(row, r.gdo, r.zo_got)
    qkv_sum = sum_here(row, r.gdq, r.zq_got)
    for copy in ysent:
        copy.wait_recv()
    for s in range(z.nrow - 1):
        out_sum = out_sum + r.yo_got[s].astype(F32)
        qkv_sum = qkv_sum + r.yq_got[s].astype(F32)
    r.grad_out[...] = out_sum.T
    for c in range(3):
        r.grad_qkv[c] = qkv_sum[:, c * z.width : (c + 1) * z.width]
    for run in (early, final):
        for _ in run:
            pass
    r.small[...] = r.ebuf[4]
    r.late[...] = r.lbuf[4]
    for copy in kept:
        copy.wait()
    for copy in swapped:
        copy.wait_recv()
    links.finish()


def sizes(mesh_shape, tokens, segments, rel_table, w_in, router):
    z = types.SimpleNamespace()
    z.ndp, z.nrow, z.ncol = mesh_shape
    z.micro, z.tok, z.d = tokens.shape[0], tokens.shape[2], tokens.shape[3]
    z.length = segments.shape[2]
    z.nbuck, z.heads = rel_table.shape
    z.width = z.d // z.ncol
    z.head = z.width // z.heads
    z.ff = w_in.shape[2]
    z.ffh, z.dr = z.ff // z.nrow, z.d // z.nrow
    z.experts = router.shape[1]
    z.slots_each = max(2, 2 * z.tok // z.experts)
    z.slots = z.experts * z.slots_each
    z.piece = z.d // (z.ndp * z.nrow)
    z.chunk = min(512, z.ffh)
    return z


VM = pl.BlockSpec(memory_space=pltpu.VMEM)
ANY = pl.BlockSpec(memory_space=pl.ANY)


def write_results(z, given, wanted, *refs):
    r = types.SimpleNamespace(**dict(zip(given, refs[: len(given)], strict=True)))
    o = types.SimpleNamespace(**dict(zip(wanted, refs[len(given) :], strict=True)))
    o.gwi[...] = r.gwi[...].astype(F32)
    o.gwd[...] = r.gwd[...].astype(F32)

    @pl.when(pl.program_id(0) == 0)
    def _():
        for name in ("layer_out", "grad_tok", "grad_qkv", "grad_out"):
            getattr(o, name)[...] = getattr(r, name)[...]
        o.router[...] = r.small[: z.experts, :]
        o.rel[...] = r.late[1 : 1 + z.heads, : z.nbuck]
        o.gain_one[...] = r.late[0, :]
        o.gain_two[...] = r.small[z.experts, :]


def fast(mesh_shape, tokens, segments, routes, buckets, gain_attn, w_qkv, w_out, rel_table, gain_ffn, router, w_in,
         w_down, cotangent):
    z = sizes(mesh_shape, tokens, segments, rel_table, w_in, router)
    S = jax.ShapeDtypeStruct
    V = pltpu.VMEM
    sem = pltpu.SemaphoreType.DMA
    rb = jnp.concatenate([buckets[::-1], jnp.full((1,), -1, jnp.int32)])[None]
    ins = {
        "tok": tokens[:, 0], "seg": segments, "routes": jnp.swapaxes(routes[:, 0], 1, 2), "rb": rb, "gain": gain_attn,
        "w_qkv": jnp.swapaxes(w_qkv, 0, 1), "w_out": w_out, "rel": rel_table.T, "gain_ffn": gain_ffn, "router": router.T, "cot": cotangent[:, 0],
        "w_in": w_in[0], "w_down": w_down[0],
    }
    outs = {
        "layer_out": S((z.micro, z.tok, z.d), BF16),
        "grad_tok": S((z.micro, z.tok, z.d), F32),
        "grad_qkv": S((3, z.piece, z.width), F32),
        "grad_out": S((z.width, z.piece), F32),
        "small": S((z.experts + 8, z.d), F32),
        "late": S((8, z.d), F32),
        "gwi": S((z.dr, z.ff), BF16),
        "gwd": S((z.ff, z.dr), BF16),
    }
    others, both = z.nrow - 1, z.nrow * z.piece
    scratch = {
        "nrm": V((z.micro, z.length, z.d), BF16),
        "qkv_t": V((z.micro, z.d, z.length), BF16),
        "lse": V((z.micro, 8, z.length), F32),
        "mix": V((z.micro, z.ncol, z.tok, z.width), BF16),
        "mown": V((z.micro, z.ncol, z.tok, z.width), BF16),
        "hidden": V((z.micro, z.tok, z.d), F32),
        "slots": V((z.micro, z.nrow, z.slots, 2 * z.d), BF16),
        "near": V((z.nrow, z.micro, 1, z.tok), jnp.int32),
        "near_rows": V((z.nrow, z.tok, 2 * z.d), BF16),
        "dense": V((z.d, z.d), BF16),
        "wo": V((z.ncol, z.d, z.width), BF16),
        "bias": V((z.heads, z.length, z.length), F32),
        "wi": V((z.d, z.ffh), BF16),
        "wd": V((z.nrow, z.ffh, z.dr), BF16),
        "arr": V((z.micro, z.nrow, z.slots, 2 * z.d), BF16),
        "own_part": V((z.micro, z.slots, 2 * z.d), F32),
        "psend": V((z.micro, others, z.slots, 2 * z.d), BF16),
        "precv": V((z.micro, others, z.slots, 2 * z.d), BF16),
        "back": V((z.micro, z.slots, 2 * z.d), BF16),
        "ret": V((z.micro, z.slots, 2 * z.d), BF16),
        "act": V((z.micro, z.nrow, z.slots, z.ffh), BF16),
        "gpre": V((z.micro, z.nrow, z.slots, z.ffh), BF16),
        "xt": V((z.d, z.micro * z.nrow * z.slots), BF16),
        "pc": V((z.micro, z.ncol, z.tok, z.d), BF16),
        "gh": V((z.micro, z.tok, z.d), F32),
        "gkeep": V((z.micro, z.heads, z.length, z.length), BF16),
        "gj_t": V((z.d, z.length), BF16),
        "gdo": V((z.d, z.width), F32),
        "gdq": V((z.d, 3 * z.width), F32),
        "pb": V((z.micro, z.ncol, z.tok, z.d), BF16),
        "pr": V((z.micro, 2, z.tok, z.d), BF16),
        "px": V((z.micro, z.tok, z.d), BF16),
        "xsum": V((z.micro, z.tok, z.d), BF16),
        "zo": V((z.ndp - 1, both, z.width), BF16),
        "zo_got": V((z.ndp - 1, both, z.width), BF16),
        "zq": V((z.ndp - 1, both, 3 * z.width), BF16),
        "zq_got": V((z.ndp - 1, both, 3 * z.width), BF16),
        "yo": V((others, z.piece, z.width), BF16),
        "yo_got": V((others, z.piece, z.width), BF16),
        "yq": V((others, z.piece, 3 * z.width), BF16),
        "yq_got": V((others, z.piece, 3 * z.width), BF16),
        "ebuf": V((5, z.experts + 8, z.d), F32),
        "egot": V((2 + z.ndp + z.nrow, z.experts + 8, z.d), F32),
        "lbuf": V((5, 8, z.d), F32),
        "lgot": V((2 + z.ndp + z.nrow, 8, z.d), F32),
        "send_sem": sem((200,)),
        "recv_sem": sem((200,)),
        "here_sem": sem((4,)),
    }
    run = pl.pallas_call(
        functools.partial(layer_kernel, z, [*ins, *outs, *scratch]),
        out_shape=list(outs.values()),
        in_specs=[VM] * (len(ins) - 2) + [ANY] * 2,
        out_specs=[VM] * 6 + [ANY] * 2,
        scratch_shapes=list(scratch.values()),
        compiler_params=pltpu.CompilerParams(collective_id=1, has_side_effects=True, vmem_limit_bytes=63 * 2**20),
        name="layer",
    )
    found = dict(zip(outs, run(*ins.values()), strict=True))
    steps = 6
    whole = lambda shape: pl.BlockSpec(shape, lambda i: (0,) * len(shape))
    cut_in, cut_down = (z.dr // steps, z.ff), (z.ff // steps, z.dr)
    shapes = {
        "layer_out": S((z.micro, z.tok, z.d), BF16),
        "grad_tok": S((z.micro, z.tok, z.d), F32),
        "gain_one": S((z.d,), F32),
        "grad_qkv": S((3, z.piece, z.width), F32),
        "grad_out": S((z.width, z.piece), F32),
        "rel": S((z.heads, z.nbuck), F32),
        "gain_two": S((z.d,), F32),
        "router": S((z.experts, z.d), F32),
        "gwi": S((z.dr, z.ff), F32),
        "gwd": S((z.ff, z.dr), F32),
    }
    by_rows = lambda shape: pl.BlockSpec(shape, lambda i: (i, 0))
    pick = lambda given: [
        by_rows(cut_in) if n == "gwi" else by_rows(cut_down) if n == "gwd" else whole(s.shape) for n, s in given.items()
    ]
    done = pl.pallas_call(
        functools.partial(write_results, z, list(outs), list(shapes)),
        grid=(steps,),
        out_shape=list(shapes.values()),
        in_specs=pick(outs),
        out_specs=pick(shapes),
        compiler_params=pltpu.CompilerParams(vmem_limit_bytes=62 * 2**20),
        name="results",
    )(*found.values())
    d = dict(zip(shapes, done, strict=True))
    return (
        d["layer_out"][:, None], d["grad_tok"][:, None], d["gain_one"], jnp.swapaxes(d["grad_qkv"], 0, 1), d["grad_out"],
        d["rel"].T, d["gain_two"], d["router"].T, d["gwi"][None], d["gwd"][None],
    )


def smooth_act(values):
    return jax.nn.gelu(values, approximate=True)


def plain_normalize(values, gain_vec):
    factor = lax.rsqrt(jnp.mean(values * values, axis=-1, keepdims=True) + EPSILON)
    return (values * factor * gain_vec, factor)


def plain_norm_back(grad_into, values, factor, gain_vec):
    scaled = grad_into * gain_vec
    inner = jnp.mean(scaled * values, axis=-1, keepdims=True)
    return (
        factor * (scaled - values * factor * factor * inner),
        jnp.sum(grad_into * values * factor, axis=0),
    )


def contract_rows(left, right, precision=None):
    return lax.dot_general(
        left,
        right,
        (((0,), (0,)), ((), ())),
        precision=precision,
        preferred_element_type=jnp.float32,
    )


def contract_cols(left, right, precision=None):
    return lax.dot_general(
        left,
        right,
        (((1,), (1,)), ((), ())),
        precision=precision,
        preferred_element_type=jnp.float32,
    )


def spread_rows(offsets, row_first, row_count, length):
    shifted = jnp.roll(offsets, row_first, axis=-1)
    span_width = 2 * length - 1
    tiled_rows = jnp.tile(shifted, (1, row_count))[:, : row_count * span_width]
    return tiled_rows.reshape(offsets.shape[0], row_count, span_width)[:, :, length - 1 :]


def plain_gather_offsets(grads, row_first, length):
    heads_here = grads.shape[0]
    row_count = grads.shape[1]
    span_width = 2 * length - 1
    widened = jnp.pad(grads, ((0, 0), (0, 0), (length - 1, 0)))
    flat_rows = jnp.pad(
        widened.reshape(heads_here, row_count * span_width), ((0, 0), (0, row_count))
    )
    folded = jnp.sum(flat_rows.reshape(heads_here, row_count, 2 * length), axis=1)
    return jnp.roll(folded, -row_first, axis=-1)


def score_block(query_part, key_rows, bias_part, marks_query, marks_keys):
    scores = (
        jnp.einsum("qhd,khd->hqk", query_part, key_rows, preferred_element_type=jnp.float32)
        + bias_part
    )
    same_doc = marks_query[:, None] == marks_keys[None, :]
    return jnp.where(same_doc[None], scores, MASKED)


def fetch_dense(w_qkv, w_out):
    return (
        lax.all_gather(w_qkv, ("dp", "row"), axis=0, tiled=True),
        lax.all_gather(w_out, ("dp", "row"), axis=1, tiled=True),
    )


def fetch_experts(w_in, w_down):
    grown_in, grown_down = (
        lax.all_gather(w_in, "row", axis=1, tiled=True),
        lax.all_gather(w_down, "row", axis=2, tiled=True),
    )
    return (grown_in[0], grown_down[0])


def plain_shards(
    tokens,
    segments,
    routes,
    buckets,
    gain_attn,
    w_qkv,
    w_out,
    rel_table,
    gain_ffn,
    router,
    w_in,
    w_down,
    cotangent,
):
    micro_count = tokens.shape[0]
    tok_rows = tokens.shape[2]
    model_width = tokens.shape[3]
    length = segments.shape[2]
    local_heads = rel_table.shape[1]
    head_size = w_out.shape[0] // local_heads
    local_width = local_heads * head_size
    experts_all = router.shape[1]
    hidden_units = w_in.shape[2]
    capacity = max(2, 2 * tok_rows // experts_all)
    query_block = min(512, length)
    block_starts = list(range(0, length, query_block))
    padded_ids = jnp.concatenate([buckets, jnp.full((1,), -1, jnp.int32)])
    offset_table = (
        padded_ids[:, None] == jnp.arange(rel_table.shape[0], dtype=jnp.int32)[None, :]
    ).astype(jnp.float32)
    offset_bias = jnp.dot(offset_table, rel_table, precision=HIGHEST).T
    block_bias = [
        spread_rows(offset_bias, row_start, query_block, length) for row_start in block_starts
    ]
    expert_ids = jnp.arange(experts_all, dtype=jnp.int32)
    slot_ids = jnp.arange(experts_all * capacity, dtype=jnp.int32)
    saved = []
    outputs = []
    for micro_index in range(micro_count):
        full_qkv, full_out = fetch_dense(w_qkv, w_out)
        full_in, full_down = fetch_experts(w_in, w_down)
        own_rows = tokens[micro_index, 0].astype(jnp.float32)
        whole_rows = lax.all_gather(tokens[micro_index, 0], "col", axis=0, tiled=True).astype(
            jnp.float32
        )
        normed_one = plain_normalize(whole_rows, gain_attn)[0].astype(jnp.bfloat16)
        joined = jnp.einsum(
            "td,dcf->tcf", normed_one, full_qkv, preferred_element_type=jnp.float32
        ).astype(jnp.bfloat16)
        queries = joined[:, 0].reshape(length, local_heads, head_size)
        key_rows = joined[:, 1].reshape(length, local_heads, head_size)
        value_rows = joined[:, 2].reshape(length, local_heads, head_size)
        marks = segments[micro_index, 0]
        mixed_parts = []
        log_sums = []
        for block_index, row_start in enumerate(block_starts):
            scores = score_block(queries, key_rows, block_bias[block_index], marks, marks)
            highest = jnp.max(scores, axis=-1, keepdims=True)
            log_sum = highest + jnp.log(jnp.sum(jnp.exp(scores - highest), axis=-1, keepdims=True))
            weights = jnp.exp(scores - log_sum).astype(jnp.bfloat16)
            mixed_parts.append(
                jnp.einsum(
                    "hqk,khd->qhd", weights, value_rows, preferred_element_type=jnp.float32
                ).astype(jnp.bfloat16)
            )
            log_sums.append(log_sum)
        mixed = mixed_parts[0].reshape(length, local_width)
        hidden = own_rows + lax.psum_scatter(
            jnp.dot(mixed, full_out, preferred_element_type=jnp.float32),
            "col",
            scatter_dimension=0,
            tiled=True,
        )
        normed_two, factor_two = plain_normalize(hidden, gain_ffn)
        chances = jax.nn.softmax(jnp.dot(normed_two, router, precision=HIGHEST), axis=-1)
        chosen = routes[micro_index, 0, :, 0]
        picked = chosen[:, None] == expert_ids[None, :]
        gate_value = jnp.sum(jnp.where(picked, chances, 0.0), axis=-1)
        picked_int = picked.astype(jnp.int32)
        ranks = jnp.sum((jnp.cumsum(picked_int, axis=0) - picked_int) * picked_int, axis=1)
        placement = ((chosen * capacity + ranks)[:, None] == slot_ids[None, :]).astype(jnp.bfloat16)
        outgoing = contract_rows(placement, normed_two.astype(jnp.bfloat16)).astype(jnp.bfloat16)
        outgoing = outgoing.reshape(experts_all, capacity, model_width)
        arrived = lax.all_to_all(outgoing, ("dp", "col"), split_axis=0, concat_axis=0, tiled=True)
        flat_in = arrived.reshape(-1, model_width)
        before = jnp.dot(flat_in, full_in, preferred_element_type=jnp.float32)
        active = smooth_act(before).astype(jnp.bfloat16)
        result = jnp.dot(active, full_down, preferred_element_type=jnp.float32).astype(jnp.bfloat16)
        sent_back = lax.all_to_all(
            result.reshape(arrived.shape), ("dp", "col"), split_axis=0, concat_axis=0, tiled=True
        )
        sent_back, arrived, before_all = (
            sent_back,
            arrived,
            before.reshape(arrived.shape[0], arrived.shape[1], hidden_units),
        )
        expert_out = jnp.dot(
            placement, sent_back.reshape(-1, model_width), preferred_element_type=jnp.float32
        )
        outputs.append((hidden + gate_value[:, None] * expert_out).astype(jnp.bfloat16))
        saved.append(
            (
                own_rows,
                normed_one,
                queries,
                key_rows,
                value_rows,
                marks,
                log_sums,
                mixed,
                hidden,
                normed_two,
                factor_two,
                chances,
                picked,
                gate_value,
                placement,
                expert_out,
                arrived,
                before_all,
            )
        )
    grad_qkv_sum = jnp.zeros((model_width, 3, local_width), jnp.float32)
    grad_out_sum = jnp.zeros((local_width, model_width), jnp.float32)
    grad_in_sum = jnp.zeros((model_width, hidden_units), jnp.float32)
    grad_down_sum = jnp.zeros((hidden_units, model_width), jnp.float32)
    grad_offsets = jnp.zeros((local_heads, 2 * length), jnp.float32)
    grad_gain_one = jnp.zeros((model_width,), jnp.float32)
    grad_gain_two = jnp.zeros((model_width,), jnp.float32)
    grad_router_sum = jnp.zeros(router.shape, jnp.float32)
    grads_input = []
    for micro_index in range(micro_count):
        (
            own_rows,
            normed_one,
            queries,
            key_rows,
            value_rows,
            marks,
            log_sums,
            mixed,
            hidden,
            normed_two,
            factor_two,
            chances,
            picked,
            gate_value,
            placement,
            expert_out,
            arrived,
            before_all,
        ) = saved[micro_index]
        full_qkv, full_out = fetch_dense(w_qkv, w_out)
        full_in, full_down = fetch_experts(w_in, w_down)
        upstream = cotangent[micro_index, 0].astype(jnp.float32)
        grad_gate = jnp.sum(upstream * expert_out, axis=-1)
        grad_result = (gate_value[:, None] * upstream).astype(jnp.bfloat16)
        to_slots = contract_rows(placement, grad_result).astype(jnp.bfloat16)
        to_slots = to_slots.reshape(experts_all, capacity, model_width)
        at_expert = lax.all_to_all(
            to_slots, ("dp", "col"), split_axis=0, concat_axis=0, tiled=True
        ).reshape(-1, model_width)
        flat_before = before_all.reshape(-1, hidden_units)
        act_value, act_pull = jax.vjp(smooth_act, flat_before)
        flat_active = act_value.astype(jnp.bfloat16)
        grad_down_sum = grad_down_sum + contract_rows(flat_active, at_expert)
        grad_active = contract_cols(at_expert, full_down)
        grad_before = act_pull(grad_active)[0].astype(jnp.bfloat16)
        grad_in_sum = grad_in_sum + contract_rows(arrived.reshape(-1, model_width), grad_before)
        grad_sent = (
            contract_cols(grad_before, full_in)
            .astype(jnp.bfloat16)
            .reshape(experts_all, capacity, model_width)
        )
        came_back = lax.all_to_all(
            grad_sent, ("dp", "col"), split_axis=0, concat_axis=0, tiled=True
        )
        grad_normed_two = jnp.dot(
            placement, came_back.reshape(-1, model_width), preferred_element_type=jnp.float32
        )
        grad_logits = (grad_gate * gate_value)[:, None] * (picked.astype(jnp.float32) - chances)
        grad_router_sum = grad_router_sum + contract_rows(normed_two, grad_logits, HIGHEST)
        grad_normed_two = grad_normed_two + contract_cols(grad_logits, router, HIGHEST)
        grad_norm_part, gain_part = plain_norm_back(grad_normed_two, hidden, factor_two, gain_ffn)
        grad_gain_two = grad_gain_two + gain_part
        grad_hidden = upstream + grad_norm_part
        piece = lax.all_gather(grad_hidden.astype(jnp.bfloat16), "col", axis=0, tiled=True)
        total_out = grad_out_sum
        total_out = total_out + contract_rows(mixed, piece)
        spread_grad = contract_cols(piece, full_out)
        grad_out_sum = total_out
        grad_mixed = spread_grad
        grad_mixed = grad_mixed.astype(jnp.bfloat16).reshape(length, local_heads, head_size)
        grad_keys = jnp.zeros((length, local_heads, head_size), jnp.float32)
        grad_values = jnp.zeros((length, local_heads, head_size), jnp.float32)
        query_grads = []
        for block_index, row_start in enumerate(block_starts):
            scores = score_block(queries, key_rows, block_bias[block_index], marks, marks)
            weights = jnp.exp(scores - log_sums[block_index])
            grad_values = jnp.einsum(
                "hqk,qhd->khd",
                weights.astype(jnp.bfloat16),
                grad_mixed,
                preferred_element_type=jnp.float32,
            )
            grad_weights = jnp.einsum(
                "qhd,khd->hqk", grad_mixed, value_rows, preferred_element_type=jnp.float32
            )
            grad_scores = (
                weights * (grad_weights - jnp.sum(weights * grad_weights, axis=-1, keepdims=True))
            ).astype(jnp.bfloat16)
            grad_offsets = grad_offsets + plain_gather_offsets(
                grad_scores.astype(jnp.float32), row_start, length
            )
            query_grads.append(
                jnp.einsum(
                    "hqk,khd->qhd", grad_scores, key_rows, preferred_element_type=jnp.float32
                )
            )
            grad_keys = jnp.einsum(
                "hqk,qhd->khd", grad_scores, queries, preferred_element_type=jnp.float32
            )
        grad_joined = jnp.stack([query_grads[0], grad_keys, grad_values], axis=1)
        grad_joined = grad_joined.reshape(length, 3, local_width).astype(jnp.bfloat16)
        grad_qkv_sum = grad_qkv_sum + jnp.einsum(
            "td,tcf->dcf", normed_one, grad_joined, preferred_element_type=jnp.float32
        )
        grad_normed_one = lax.psum_scatter(
            jnp.einsum(
                "tcf,dcf->td", grad_joined, full_qkv, preferred_element_type=jnp.float32
            ).astype(jnp.bfloat16),
            "col",
            scatter_dimension=0,
            tiled=True,
        ).astype(jnp.float32)
        factor_one = plain_normalize(own_rows, gain_attn)[1]
        grad_input_part, gain_part = plain_norm_back(grad_normed_one, own_rows, factor_one, gain_attn)
        grad_gain_one = grad_gain_one + gain_part
        grads_input.append(grad_hidden + grad_input_part)
    grad_rel_mine = jnp.dot(offset_table.T, grad_offsets.T, precision=HIGHEST)
    heads_all = local_heads * lax.axis_size("col")
    head_first = lax.axis_index("col") * local_heads
    rel_full = lax.dynamic_update_slice_in_dim(
        jnp.zeros((rel_table.shape[0], heads_all), jnp.float32), grad_rel_mine, head_first, 1
    )
    total_gain_one, total_gain_two, total_router, total_rel = lax.psum(
        (grad_gain_one, grad_gain_two, grad_router_sum, rel_full), ("dp", "row", "col")
    )
    rel_out = lax.dynamic_slice_in_dim(total_rel, head_first, local_heads, 1)
    dense_qkv, dense_out = (
        lax.psum_scatter(grad_qkv_sum, ("dp", "row"), scatter_dimension=0, tiled=True),
        lax.psum_scatter(grad_out_sum, ("dp", "row"), scatter_dimension=1, tiled=True),
    )
    expert_in, expert_down = (
        lax.psum_scatter(
            grad_in_sum[None].astype(jnp.bfloat16), "row", scatter_dimension=1, tiled=True
        ).astype(jnp.float32),
        lax.psum_scatter(
            grad_down_sum[None].astype(jnp.bfloat16), "row", scatter_dimension=2, tiled=True
        ).astype(jnp.float32),
    )
    layer_out = jnp.stack(outputs)[:, None]
    grad_tokens = jnp.stack(grads_input)[:, None]
    return (
        layer_out,
        grad_tokens,
        total_gain_one,
        dense_qkv,
        dense_out,
        rel_out,
        total_gain_two,
        total_router,
        expert_in,
        expert_down,
    )


def solution(mesh):
    shape = tuple(mesh.shape[a] for a in ("dp", "row", "col"))
    token_spec, expert_in, expert_down = P(None, ("dp", "row"), "col", None), P(("dp", "col"), "row", None), P(("dp", "col"), None, "row")
    qkv_spec, out_spec = P(("dp", "row"), None, "col"), P("col", ("dp", "row"))
    in_specs = (
        token_spec, P(None, ("dp", "row"), None), token_spec, P(), P(), qkv_spec, out_spec, P(None, "col"), P(), P(),
        expert_in, expert_down, token_spec,
    )
    out_specs = (token_spec, token_spec, P(), qkv_spec, out_spec, P(None, "col"), P(), P(), expert_in, expert_down)

    def run(*args):
        piece, each = args[5].shape[0] // (shape[0] * shape[1]), 2 * args[0].shape[2] // shape[2] // args[9].shape[1]
        whole_tiles = piece % 16 == 0 and each % 16 == 0 and shape[2] == 4 and args[0].shape[0] == 2
        body = functools.partial(fast, shape) if whole_tiles else plain_shards
        return jax.shard_map(body, mesh=mesh, in_specs=in_specs, out_specs=out_specs, check_vma=False)(*args)

    return run
```

```python
import functools
import types

import jax
import jax.numpy as jnp
from jax import lax
from jax.experimental import pallas as pl
from jax.experimental.pallas import tpu as pltpu
from jax.sharding import PartitionSpec as P

EPSILON = 1e-06
HIGHEST = lax.Precision.HIGHEST
MASKED = -1000000000.0
MESH = pl.DeviceIdType.MESH
F32 = jnp.float32
BF16 = jnp.bfloat16
NN = (((1,), (0,)), ((), ()))
NT = (((1,), (1,)), ((), ()))
TN = (((0,), (0,)), ((), ()))


def mm(left, right, dims=NN, precision=None):
    return lax.dot_general(left, right, dims, precision=precision, preferred_element_type=F32)


def rows(first, count):
    return pl.ds(pl.multiple_of(first, count), count)


class Links:
    def __init__(self, send_sem, recv_sem):
        self.send_sem, self.recv_sem, self.used, self.started = send_sem, recv_sem, 0, []

    def send(self, src, dst, device):
        k = self.used
        self.used += 1
        copy = pltpu.make_async_remote_copy(
            src_ref=src, dst_ref=dst, send_sem=self.send_sem.at[k], recv_sem=self.recv_sem.at[k],
            device_id=device, device_id_type=MESH,
        )
        copy.start()
        self.started.append(copy)
        return copy

    def finish(self):
        for copy in self.started:
            copy.wait_send()


class Place:
    def __init__(self, z):
        self.dp, self.row, self.col = lax.axis_index("dp"), lax.axis_index("row"), lax.axis_index("col")
        dp, row, col = self.dp, self.row, self.col
        self.dps = [lax.rem(dp + i, z.ndp) for i in range(z.ndp)]
        self.rws = [lax.rem(row + i, z.nrow) for i in range(z.nrow)]
        self.cls = [lax.rem(col + i, z.ncol) for i in range(z.ncol)]
        self.dps_back = [lax.rem(dp + z.ndp - i, z.ndp) for i in range(z.ndp)]
        self.rws_back = [lax.rem(row + z.nrow - i, z.nrow) for i in range(z.nrow)]
        self.cls_back = [lax.rem(col + z.ncol - i, z.ncol) for i in range(z.ncol)]
        self.across = lax.rem(col + 2, z.ncol)
        self.beside = col + 1 - 2 * lax.rem(col, 2)
        self.far = lax.rem(self.beside + 2, z.ncol)


def greet(devices):
    barrier = pltpu.get_barrier_semaphore()
    for device in devices:
        pl.semaphore_signal(barrier, inc=1, device_id=device, device_id_type=MESH)
    return lambda: pl.semaphore_wait(barrier, len(devices))


def norm_rows(values):
    return lax.rsqrt(jnp.mean(values * values, axis=-1, keepdims=True) + EPSILON)


def norm_back(grad_into, values, factor, gain_vec):
    scaled = grad_into * gain_vec
    inner = jnp.mean(scaled * values, axis=-1, keepdims=True)
    return (
        factor * (scaled - values * factor * factor * inner),
        jnp.sum(grad_into * values * factor, axis=0, keepdims=True),
    )


def column(line):
    return jnp.broadcast_to(line.astype(F32), (8, line.shape[1])).T[:, :1]


def offset_table(z, rb):
    ids = lax.broadcasted_iota(jnp.int32, (z.nbuck, 2 * z.length), 0)
    return (ids == rb[...]).astype(F32)


def make_bias(z, rb, rel, bias):
    offsets = mm(rel[...], offset_table(z, rb), NN, HIGHEST)
    for h in range(z.heads):
        spread = jnp.broadcast_to(offsets[h : h + 1, :], (z.length, 2 * z.length))
        turned = pltpu.roll(spread, z.length + 1, 1, stride=1, stride_axis=0)
        bias[h] = turned[:, : z.length]


def gather_offsets(values):
    count = values.shape[0] // 2
    while count >= 1:
        values = pltpu.roll(values[:count], count, 1) + values[count:]
        count //= 2
    return values


def routing(z, chosen):
    ids = lax.broadcasted_iota(jnp.int32, (z.tok, z.experts), 1).astype(F32)
    picked = chosen == ids
    before = (
        lax.broadcasted_iota(jnp.int32, (z.tok, z.tok), 0) > lax.broadcasted_iota(jnp.int32, (z.tok, z.tok), 1)
    ).astype(BF16)
    counts = mm(before, picked.astype(BF16))
    ranks = jnp.sum(jnp.where(picked, counts, 0.0), axis=1, keepdims=True)
    slot = chosen * z.slots_each + ranks
    placement = (slot == lax.broadcasted_iota(jnp.int32, (z.tok, z.slots), 1).astype(F32)).astype(BF16)
    return picked, placement


def softmax_rows(logits):
    top = jnp.exp(logits - jnp.max(logits, axis=-1, keepdims=True))
    return top / jnp.sum(top, axis=-1, keepdims=True)


def gelu_both(before):
    inner = 0.7978845608 * (before + 0.044715 * before * before * before)
    t = jnp.tanh(inner)
    half = 0.5 * (1.0 + t)
    slope = half + 0.5 * before * (1.0 - t * t) * (0.7978845608 * (1.0 + 3.0 * 0.044715 * before * before))
    return before * half, slope


def partner(index, step):
    return index + step - 2 * step * lax.rem(index // step, 2)


def reduce_all(z, me, links, part, term, got, out, per_col=0):
    dp, row, col = me.dp, me.row, me.col
    split = len(out.shape) == 3
    stages = (
        (z.ncol, col, [(dp, row, c) for c in me.cls[1:]]),
        (z.ndp, dp, [(d, row, col) for d in me.dps[1:]]),
        (z.nrow, row, [(dp, w, col) for w in me.rws[1:]]),
    )
    for k, (size, mine, others) in enumerate(stages):
        if k == 0:
            copies = [links.send(part(c), got.at[0, col], device) for c, device in zip(me.cls[1:], others)]
            got[0, col] = part(col)[...]
        else:
            term[k - 1] = total
            copies = [links.send(term.at[k - 1], got.at[k, mine], device) for device in others]
            got[k, mine] = total
        yield
        for copy in copies:
            copy.wait_recv()
        total = jnp.zeros(got.shape[2:], F32)
        for i in range(size):
            value = got[k, i]
            if k == 0 and per_col:
                line = lax.broadcasted_iota(jnp.int32, value.shape, 0)
                value = jnp.where((line < value.shape[0] - per_col) | (i == col), value, 0.0)
            total = total + value
    if split:
        out[col] = total
        copies = [links.send(out.at[col], out.at[col], device) for device in stages[0][2]]
        yield
        for copy in copies:
            copy.wait_recv()
    else:
        out[...] = total


def attention_forward(z, r, m):
    seg = r.seg[m]
    same = column(seg) == seg.astype(F32)
    parts = []
    for h in range(z.heads):
        q_t, k_t, v_t = (r.qkv_t[m, pl.ds(c * z.width + h * z.head, z.head), :] for c in range(3))
        scores = jnp.where(same, mm(k_t, q_t, TN) + r.bias[h], MASKED)
        highest = jnp.max(scores, axis=0, keepdims=True)
        raised = jnp.exp(scores - highest)
        total = jnp.sum(raised, axis=0, keepdims=True)
        probs = (raised * (1.0 / total)).astype(BF16)
        r.pairs[m, h] = probs
        parts.append(mm(v_t, probs))
    mixed = jnp.concatenate(parts, axis=0).T.astype(BF16)
    for c in range(z.ncol):
        r.mix[m, c] = mixed[c * z.tok : (c + 1) * z.tok]


def attention_backward(z, r, m, h, grad_t):
    q_t, k_t, v_t = (r.qkv_t[m, pl.ds(c * z.width + h * z.head, z.head), :] for c in range(3))
    g_t = grad_t[h * z.head : (h + 1) * z.head, :]
    probs = r.pairs[m, h]
    wide = probs.astype(F32)
    grad_probs = mm(v_t, g_t, TN)
    delta = jnp.sum(wide * grad_probs, axis=0, keepdims=True)
    grads = (wide * (grad_probs - delta)).astype(BF16)
    r.pairs[m, h] = grads
    parts = [mm(k_t, grads), mm(q_t, grads, NT), mm(g_t, probs, NT)]
    for c, part in enumerate(parts):
        r.gj_t[pl.ds(c * z.width + h * z.head, z.head), :] = part.astype(BF16)
    return mm(r.nrm_t[m], jnp.concatenate(parts, axis=0).T.astype(BF16))


def layer_kernel(z, names, *refs):
    r = types.SimpleNamespace(**dict(zip(names, refs, strict=True)))
    me = Place(z)
    dp, row, col = me.dp, me.row, me.col
    links = Links(r.send_sem, r.recv_sem)
    plane = [(i, j) for i in range(z.ndp) for j in range(z.ncol) if (i, j) != (0, 0)]
    arrived = greet([(me.dps[i], row, me.cls[j]) for i, j in plane] + [(dp, w, col) for w in me.rws[1:]])
    gain, gain_ffn = r.gain[...].reshape(1, z.d), r.gain_ffn[...].reshape(1, z.d)
    micros = range(z.micro)

    own = [
        pltpu.make_async_copy(r.w_in.at[:, rows(row * z.ffh, z.ffh)], r.wi.at[rows(row * z.dr, z.dr), :], r.here_sem.at[0]),
        pltpu.make_async_copy(r.w_down.at[rows(row * z.ffh, z.ffh), :], r.wd.at[row], r.here_sem.at[1]),
    ]
    for copy in own:
        copy.start()
    pid = dp * z.nrow + row
    piece = lambda p: r.dq.at[rows(p * z.piece, z.piece), :]
    out_piece = lambda c, p: r.wo.at[c, rows(p * z.piece, z.piece), :]
    r.dq[rows(pid * z.piece, z.piece), :] = jnp.concatenate([r.w_qkv[c] for c in range(3)], axis=1)
    r.wo[col, rows(pid * z.piece, z.piece), :] = r.w_out[...].astype(F32).T.astype(BF16)
    for m in micros:
        values = r.tok[m].astype(F32)
        r.nrm[m, rows(col * z.tok, z.tok), :] = (values * norm_rows(values) * gain).astype(BF16)
    arrived()

    dense_y = [links.send(piece(pid), piece(pid), (dp, w, col)) for w in me.rws[1:]]
    out_y = [links.send(out_piece(col, pid), out_piece(col, pid), (dp, w, col)) for w in me.rws[1:]]
    dense_z = [links.send(piece(pid), piece(pid), (d, row, col)) for d in me.dps[1:]]
    routes = [links.send(r.routes, r.near.at[row], (dp, w, col)) for w in me.rws[1:]]
    experts = []
    for w in me.rws[1:]:
        experts.append(links.send(r.w_in.at[:, rows(w * z.ffh, z.ffh)], r.wi.at[rows(row * z.dr, z.dr), :], (dp, w, col)))
        experts.append(links.send(r.w_down.at[rows(w * z.ffh, z.ffh), :], r.wd.at[row], (dp, w, col)))
    block = lambda m, c: r.nrm.at[m, rows(c * z.tok, z.tok), :]
    xs = [links.send(block(m, col), block(m, col), (dp, row, me.across)) for m in micros]
    cs = [links.send(block(m, col), block(m, col), (dp, row, me.beside)) for m in micros]
    out_x, out_c = {}, []

    def share(i, s):
        p = me.dps_back[i] * z.nrow + me.rws_back[s]
        out_x[i, s] = links.send(out_piece(col, p), out_piece(col, p), (dp, row, me.across))
        out_c.append(links.send(out_piece(col, p), out_piece(col, p), (dp, row, me.beside)))

    share(0, 0)
    for s, copy in enumerate(dense_y):
        copy.wait_recv()
        p = dp * z.nrow + me.rws_back[s + 1]
        dense_z += [links.send(piece(p), piece(p), (d, row, col)) for d in me.dps[1:]]
    out_z = {(i, 0): links.send(out_piece(col, pid), out_piece(col, pid), (me.dps[i], row, col)) for i in range(1, z.ndp)}
    for s, copy in enumerate(out_y):
        copy.wait_recv()
        p = dp * z.nrow + me.rws_back[s + 1]
        for i in range(1, z.ndp):
            out_z[i, s + 1] = links.send(out_piece(col, p), out_piece(col, p), (me.dps[i], row, col))
        share(0, s + 1)
    make_bias(z, r.rb, r.rel, r.bias)
    fs = []
    for m in micros:
        xs[m].wait_recv()
        fs.append(links.send(block(m, me.across), block(m, me.across), (dp, row, me.beside)))
    for copy in dense_z + cs + fs:
        copy.wait_recv()

    swaps = []
    for m in micros:
        r.qkv_t[m] = mm(r.nrm[m], r.dq[...]).astype(BF16).T
        if m == 0:
            for i in range(1, z.ndp):
                out_z[i, 0].wait_recv()
                share(i, 0)
        attention_forward(z, r, m)
        swaps.append([links.send(r.mix.at[m, c], r.mown.at[m, col], (dp, row, c)) for c in me.cls[1:]])
        r.mown[m, col] = r.mix[m, col]
        if m == 0:
            for s in range(1, z.nrow):
                for i in range(1, z.ndp):
                    out_z[i, s].wait_recv()
                    share(i, s)
        r.nrm_t[m] = r.nrm[m].T
    for (i, s), copy in out_x.items():
        copy.wait_recv()
        p = me.dps_back[i] * z.nrow + me.rws_back[s]
        out_c.append(links.send(out_piece(me.across, p), out_piece(me.across, p), (dp, row, me.beside)))
    for copy in out_c:
        copy.wait_recv()

    mine = dp * z.ncol + col
    each = z.slots_each
    group = z.ncol * each
    dispatch = []

    def spread(m, w, slots):
        r.slots[m, w] = slots
        copies = {}
        for i, j in plane:
            e = me.dps[i] * z.ncol + me.cls[j]
            copies[i, j] = links.send(
                r.slots.at[m, w, rows(e * each, each), :], r.arr.at[m, w, rows(mine * each, each), :],
                (me.dps[i], row, me.cls[j]),
            )
        r.arr[m, w, rows(mine * each, each), :] = r.slots[m, w, rows(mine * each, each), :]
        return copies

    for m in micros:
        for copy in swaps[m]:
            copy.wait_recv()
        values = r.tok[m].astype(F32)
        for c in range(z.ncol):
            values = values + mm(r.mown[m, c], r.wo[c], NT)
        r.hidden[m] = values
        normed = values * norm_rows(values) * gain_ffn
        chances = softmax_rows(mm(normed, r.router[...], NT, HIGHEST))
        picked, placement = routing(z, column(r.routes[m]))
        gate = jnp.sum(jnp.where(picked, chances, 0.0), axis=-1, keepdims=True)
        r.normed[m], r.chances[m], r.gate[m], r.place[m] = normed, chances, gate, placement
        sent = jnp.concatenate([normed.astype(BF16), (gate * r.cot[m].astype(F32)).astype(BF16)], axis=1)
        if m == z.micro - 1:
            r.near_rows[row] = sent
            crossing = [links.send(r.near_rows.at[row], r.near_rows.at[row], (dp, w, col)) for w in me.rws[1:]]
        dispatch.append(spread(m, row, mm(placement, sent, TN).astype(BF16)))

    forwards = []
    for m in micros[:-1]:
        copies = {}
        for i in range(z.ndp):
            for j in range(z.ncol):
                if (i, j) != (0, 0):
                    dispatch[m][i, j].wait_recv()
            part = r.arr.at[m, row, rows(me.dps_back[i] * group, group), :]
            for s, w in enumerate(me.rws[1:]):
                copies[i, s] = links.send(part, part, (dp, w, col))
        forwards.append(copies)

    for copy in routes + crossing:
        copy.wait_recv()
    cross = {}
    for s in range(z.nrow - 1):
        w = me.rws_back[s + 1]
        placement = routing(z, column(r.near[w, z.micro - 1]))[1]
        cross[s] = spread(z.micro - 1, w, mm(placement, r.near_rows[w], TN).astype(BF16))

    spots = [rows(d * group, group) for d in me.dps]
    halves = [(0, z.ndp - 1), tuple(range(z.ndp - 2, 0, -1))]

    def expert(m, w, picks, store):
        x = jnp.concatenate([r.arr[m, w, spots[i], : z.d] for i in picks], axis=0)
        g = jnp.concatenate([r.arr[m, w, spots[i], z.d :] for i in picks], axis=0)
        result = jnp.zeros(x.shape, F32)
        grad = jnp.zeros(x.shape, F32)
        for k in range(z.ffh // z.chunk):
            cut = pl.ds(k * z.chunk, z.chunk)
            w_one = r.wi[:, cut]
            w_two = jnp.concatenate([r.wd[p, cut, :] for p in range(z.nrow)], axis=1)
            value, slope = gelu_both(mm(x, w_one))
            value = value.astype(BF16)
            result = result + mm(value, w_two)
            pre = (mm(g, w_two, NT) * slope).astype(BF16)
            grad = grad + mm(pre, w_one, NT)
            for n, i in enumerate(picks):
                r.act[m, w, spots[i], cut] = value[n * group : (n + 1) * group]
                r.gpre[m, w, spots[i], cut] = pre[n * group : (n + 1) * group]
        for n, i in enumerate(picks):
            store(i, jnp.concatenate([result[n * group : (n + 1) * group], grad[n * group : (n + 1) * group]], axis=1))

    for copy in own:
        copy.wait()
    for copy in experts:
        copy.wait_recv()
    def go_home(m):
        home = []
        for i in order:
            spot = spots[i]
            total = r.own_part[m, spot, :]
            for s in range(z.nrow - 1):
                partials[m][i, s].wait_recv()
                total = total + r.precv[m, s, spot, :].astype(F32)
            r.back[m, spot, :] = total.astype(BF16)
            for j in range(z.ncol):
                if (i, j) != (0, 0):
                    e = me.dps[i] * z.ncol + me.cls[j]
                    home.append(
                        links.send(
                            r.back.at[m, rows(e * each, each), :], r.ret.at[m, rows(mine * each, each), :],
                            (me.dps[i], row, me.cls[j]),
                        )
                    )
        r.ret[m, rows(mine * each, each), :] = r.back[m, rows(mine * each, each), :]
        return home

    returns = []
    waited = set()
    partials = []
    order = [*range(z.ndp - 1, 0, -1), 0]
    for m in micros:

        def store_own(i, value, m=m):
            r.own_part[m, spots[i], :] = value

        if m == z.micro - 1:
            for copy in dispatch[m].values():
                copy.wait_recv()
        expert(m, row, range(z.ndp), store_own)
        copies = {}
        for s, w in enumerate(me.rws[1:]):
            for picks in halves:
                back = [(z.ndp - i) % z.ndp for i in picks]
                if m < z.micro - 1:
                    for i in back:
                        for k in range(z.nrow - 1):
                            if (i, k) not in waited:
                                forwards[m][i, k].wait_recv()
                                waited.add((i, k))
                else:
                    for k in range(z.nrow - 1):
                        for i, j in plane:
                            if i in back and (i, j, k) not in waited:
                                cross[k][i, j].wait_recv()
                                waited.add((i, j, k))

                def store(i, value, m=m, s=s, w=w):
                    r.psend[m, s, spots[i], :] = value.astype(BF16)
                    copies[i, s] = links.send(r.psend.at[m, s, spots[i], :], r.precv.at[m, s, spots[i], :], (dp, w, col))

                expert(m, w, picks, store)
                if m == z.micro - 1 and s == 0 and picks is halves[0]:
                    returns.append(go_home(0))
        partials.append(copies)

    blocks = [(m, w) for m in micros for w in range(z.nrow)]
    for b, (m, w) in enumerate(blocks):
        r.xt[:, b * z.slots : (b + 1) * z.slots] = r.arr[m, w, :, : z.d].T
    for k in range(z.ffh // z.chunk):
        cut = pl.ds(k * z.chunk, z.chunk)
        pre = jnp.concatenate([r.gpre[m, w, :, cut] for m, w in blocks], axis=0)
        value = jnp.concatenate([r.act[m, w, :, cut] for m, w in blocks], axis=0)
        g = jnp.concatenate([r.arr[m, w, :, z.d :] for m, w in blocks], axis=0)
        r.wi[:, cut] = mm(r.xt[...], pre).astype(BF16)
        grad_down = mm(value, g, TN).astype(BF16)
        for p in range(z.nrow):
            r.wd[p, cut, :] = grad_down[:, p * z.dr : (p + 1) * z.dr]

    kept = [
        pltpu.make_async_copy(r.wi.at[rows(row * z.dr, z.dr), :], r.gwi.at[:, rows(row * z.ffh, z.ffh)], r.here_sem.at[2]),
        pltpu.make_async_copy(r.wd.at[row], r.gwd.at[rows(row * z.ffh, z.ffh), :], r.here_sem.at[3]),
    ]
    for copy in kept:
        copy.start()
    swapped = []

    def swap_grads(first, last, parts):
        for w in me.rws[1:]:
            for k in range(first, last):
                n = z.dr // parts
                swapped.append(links.send(
                    r.wi.at[rows(w * z.dr + k * n, n), :], r.gwi.at[pl.ds(k * n, n), rows(row * z.ffh, z.ffh)], (dp, w, col)
                ))
                n = z.ffh // parts
                swapped.append(links.send(
                    r.wd.at[w, pl.ds(k * n, n), :], r.gwd.at[rows(row * z.ffh + k * n, n), :], (dp, w, col)
                ))

    swap_grads(0, 8, 8)

    def token_back(m):
        for copy in returns[m]:
            copy.wait_recv()
        values = r.hidden[m]
        factor = norm_rows(values)
        normed, chances, gate = r.normed[m], r.chances[m], r.gate[m]
        picked = column(r.routes[m]) == lax.broadcasted_iota(jnp.int32, (z.tok, z.experts), 1).astype(F32)
        came = mm(r.place[m], r.ret[m])
        returned, grad_sent = came[:, : z.d], came[:, z.d :]
        r.layer_out[m] = (values + gate * returned).astype(BF16)
        upstream = r.cot[m].astype(F32)
        grad_gate = jnp.sum(upstream * returned, axis=-1, keepdims=True)
        grad_logits = grad_gate * gate * (picked.astype(F32) - chances)
        grad_normed = grad_sent + mm(grad_logits, r.router[...], NN, HIGHEST)
        part, gain_part = norm_back(grad_normed, values, factor, gain_ffn)
        grad_hidden = upstream + part
        r.gh[m] = grad_hidden
        branch = grad_hidden.astype(BF16)
        for c in me.cls:
            r.gms[m, c] = mm(branch, r.wo[c]).astype(BF16)
        heads_in = [links.send(r.gms.at[m, c], r.gm.at[m, col], (dp, row, c)) for c in me.cls[1:]]
        r.gm[m, col] = r.gms[m, col]
        r.pc[m, col] = branch
        across = links.send(r.pc.at[m, col], r.pc.at[m, col], (dp, row, me.across))
        beside = links.send(r.pc.at[m, col], r.pc.at[m, col], (dp, row, me.beside))
        return heads_in, (across, beside), mm(grad_logits, normed, TN, HIGHEST), gain_part

    step = lambda run: next(run, None)
    wire = []

    def all_rows(m, sends):
        across, beside = sends
        across.wait_recv()
        passed = links.send(r.pc.at[m, me.across], r.pc.at[m, me.across], (dp, row, me.beside))
        beside.wait_recv()
        passed.wait_recv()
        return r.pc[m].reshape(z.length, z.d)

    def into_heads(m, copies):
        for copy in copies:
            copy.wait_recv()
        return r.gm[m].reshape(z.length, z.width).T

    def first_norm_rows(m, gj):
        partial = mm(gj, r.dq[...], NT).astype(BF16)
        for c in range(z.ncol):
            r.pb[m, c] = partial[c * z.tok : (c + 1) * z.tok]
        wire.append([links.send(r.pb.at[m, me.far], r.pr.at[m, 1], (dp, row, me.beside)),
                     links.send(r.pb.at[m, me.beside], r.pr.at[m, 0], (dp, row, me.beside))])

    def across_chips(m):
        wire[m][0].wait_recv()
        r.xsum[m] = (r.pb[m, me.across].astype(F32) + r.pr[m, 1].astype(F32)).astype(BF16)
        wire[m].append(links.send(r.xsum.at[m], r.px.at[m], (dp, row, me.across)))

    both = z.nrow * z.piece

    def reduce_over_dp(total, out, got):
        sends = []
        for i, d in enumerate(me.dps[1:]):
            out[i] = total[rows(d * both, both), :].astype(BF16)
            sends.append(links.send(out.at[i], got.at[i], (d, row, col)))
        return sends

    def sum_here(w, total, got):
        spot = rows((dp * z.nrow + w) * z.piece, z.piece)
        value = total[spot, :]
        for i in range(z.ndp - 1):
            value = value + got[i, rows(w * z.piece, z.piece), :].astype(F32)
        return value

    heads_in, sends_zero, router_t, gain_two = token_back(0)
    returns.append(go_home(1))
    grad_t = into_heads(0, heads_in)
    r.gdq[0] = attention_backward(z, r, 0, 0, grad_t)
    for h in range(1, z.heads):
        r.gdq[h] = attention_backward(z, r, 0, h, grad_t)
    first_norm_rows(0, r.gj_t[...].T)
    heads_in, sends_one, router_part, gain_part = token_back(1)
    across_chips(0)
    r.gdo[...] = mm(all_rows(0, sends_zero), r.mix[0].reshape(z.length, z.width), TN)
    sums = jnp.concatenate([router_t + router_part, gain_two + gain_part], axis=0)
    sums = jnp.concatenate([sums, jnp.zeros((z.small - z.experts - 1, z.d), F32)], axis=0)
    for c in range(z.ncol):
        r.ebuf[c] = sums[c * z.small // z.ncol : (c + 1) * z.small // z.ncol]
    early = reduce_all(z, me, links, lambda c: r.ebuf.at[c], r.eterm, r.egot, r.eout)
    step(early)
    grad_t = into_heads(1, heads_in)
    qkv_sent = []
    for h in range(z.heads):
        r.gdq[h] = r.gdq[h] + attention_backward(z, r, 1, h, grad_t)
        qkv_sent.append(reduce_over_dp(r.gdq.at[h], r.zq.at[h], r.zq_got.at[h]))
        if h == 0:
            step(early)
            r.gdo[...] = r.gdo[...] + mm(all_rows(1, sends_one), r.mix[1].reshape(z.length, z.width), TN)
            out_sent = reduce_over_dp(r.gdo, r.zo, r.zo_got)
    first_norm_rows(1, r.gj_t[...].T)
    step(early)
    across_chips(1)

    offsets = []
    for h in range(z.heads):
        total = r.pairs[0, h].astype(F32)
        for m in range(1, z.micro):
            total = total + r.pairs[m, h].astype(F32)
        offsets.append(gather_offsets(jnp.concatenate([total, jnp.zeros((z.length, z.length), F32)], axis=1)))
    grad_rel = mm(jnp.concatenate(offsets, axis=0), offset_table(z, r.rb), NT, HIGHEST)
    gain_one = jnp.zeros((1, z.d), F32)
    for m in micros:
        wire[m][1].wait_recv()
        wire[m][2].wait_recv()
        grad_normed = r.pb[m, col].astype(F32) + r.pr[m, 0].astype(F32) + r.px[m].astype(F32)
        values = r.tok[m].astype(F32)
        part, gain_part = norm_back(grad_normed, values, norm_rows(values), gain)
        gain_one = gain_one + gain_part
        r.grad_tok[m] = r.gh[m] + part
    lines = z.d // 128
    r.lbuf[...] = jnp.zeros(r.lbuf.shape, F32)
    for k in range(lines):
        r.lbuf[pl.ds(k, 1), :] = gain_one[:, k * 128 : (k + 1) * 128]
    r.lbuf[pl.ds(lines, 1), :] = jnp.concatenate(
        [grad_rel[h : h + 1, :] for h in range(z.heads)] + [jnp.zeros((1, 128 - z.heads * z.nbuck), F32)], axis=1
    )
    final = reduce_all(z, me, links, lambda c: r.lbuf, r.lterm, r.lgot, r.late, 8 - lines)
    for _ in range(2):
        step(final)
    ysent = []
    for h in range(z.heads):
        for copy in qkv_sent[h]:
            copy.wait_recv()
        for s, w in enumerate(me.rws[1:]):
            r.yq[h, s] = sum_here(w, r.gdq.at[h], r.zq_got.at[h]).astype(BF16)
            ysent.append(links.send(r.yq.at[h, s], r.yq_got.at[h, s], (dp, w, col)))
    for copy in out_sent:
        copy.wait_recv()
    for s, w in enumerate(me.rws[1:]):
        r.yo[s] = sum_here(w, r.gdo, r.zo_got).astype(BF16)
        ysent.append(links.send(r.yo.at[s], r.yo_got.at[s], (dp, w, col)))
    step(final)
    step(early)
    out_sum = sum_here(row, r.gdo, r.zo_got)
    qkv_sum = [sum_here(row, r.gdq.at[h], r.zq_got.at[h]) for h in range(z.heads)]
    for copy in ysent:
        copy.wait_recv()
    for s in range(z.nrow - 1):
        out_sum = out_sum + r.yo_got[s].astype(F32)
        qkv_sum = [total + r.yq_got[h, s].astype(F32) for h, total in enumerate(qkv_sum)]
    r.grad_out[...] = out_sum.T
    for c in range(3):
        r.grad_qkv[c] = jnp.concatenate([total[:, c * z.head : (c + 1) * z.head] for total in qkv_sum], axis=1)
    for run in (early, final):
        for _ in run:
            pass
    for c in range(z.ncol):
        r.small[pl.ds(c * z.small // z.ncol, z.small // z.ncol), :] = r.eout[c]
    for copy in kept:
        copy.wait()
    for copy in swapped:
        copy.wait_recv()
    links.finish()


def sizes(mesh_shape, tokens, segments, rel_table, w_in, router):
    z = types.SimpleNamespace()
    z.ndp, z.nrow, z.ncol = mesh_shape
    z.micro, z.tok, z.d = tokens.shape[0], tokens.shape[2], tokens.shape[3]
    z.length = segments.shape[2]
    z.nbuck, z.heads = rel_table.shape
    z.width = z.d // z.ncol
    z.head = z.width // z.heads
    z.ff = w_in.shape[2]
    z.ffh, z.dr = z.ff // z.nrow, z.d // z.nrow
    z.experts = router.shape[1]
    z.slots_each = max(2, 2 * z.tok // z.experts)
    z.slots = z.experts * z.slots_each
    z.piece = z.d // (z.ndp * z.nrow)
    z.chunk = min(512, z.ffh)
    z.small = -(-(z.experts + 1) // (8 * z.ncol)) * 8 * z.ncol
    return z


VM = pl.BlockSpec(memory_space=pltpu.VMEM)
ANY = pl.BlockSpec(memory_space=pl.ANY)


def write_results(z, given, wanted, *refs):
    r = types.SimpleNamespace(**dict(zip(given, refs[: len(given)], strict=True)))
    o = types.SimpleNamespace(**dict(zip(wanted, refs[len(given) :], strict=True)))
    o.gwi[...] = r.gwi[...].astype(F32)
    o.gwd[...] = r.gwd[...].astype(F32)

    @pl.when(pl.program_id(0) == 0)
    def _():
        for name in ("layer_out", "grad_tok", "grad_qkv", "grad_out"):
            getattr(o, name)[...] = getattr(r, name)[...]
        o.router[...] = r.small[: z.experts, :]
        lines = z.d // 128
        for h in range(z.heads):
            o.rel[pl.ds(h, 1), :] = r.late[lines : lines + 1, h * z.nbuck : (h + 1) * z.nbuck]
        for k in range(lines):
            o.gain_one[pl.ds(k * 128, 128)] = r.late[k, :]
        o.gain_two[...] = r.small[z.experts, :]


def fast(mesh_shape, tokens, segments, routes, buckets, gain_attn, w_qkv, w_out, rel_table, gain_ffn, router, w_in,
         w_down, cotangent):
    z = sizes(mesh_shape, tokens, segments, rel_table, w_in, router)
    S = jax.ShapeDtypeStruct
    V = pltpu.VMEM
    sem = pltpu.SemaphoreType.DMA
    rb = jnp.concatenate([buckets[::-1], jnp.full((1,), -1, jnp.int32)])[None]
    ins = {
        "tok": tokens[:, 0], "seg": segments, "routes": jnp.swapaxes(routes[:, 0], 1, 2), "rb": rb, "gain": gain_attn,
        "w_qkv": jnp.swapaxes(w_qkv, 0, 1), "w_out": w_out, "rel": rel_table.T, "gain_ffn": gain_ffn, "router": router.T, "cot": cotangent[:, 0],
        "w_in": w_in[0], "w_down": w_down[0],
    }
    outs = {
        "layer_out": S((z.micro, z.tok, z.d), BF16),
        "grad_tok": S((z.micro, z.tok, z.d), F32),
        "grad_qkv": S((3, z.piece, z.width), F32),
        "grad_out": S((z.width, z.piece), F32),
        "small": S((z.small, z.d), F32),
        "late": S((8, 128), F32),
        "gwi": S((z.dr, z.ff), BF16),
        "gwd": S((z.ff, z.dr), BF16),
    }
    others, both = z.nrow - 1, z.nrow * z.piece
    most = max(mesh_shape)
    scratch = {
        "nrm": V((z.micro, z.length, z.d), BF16),
        "nrm_t": V((z.micro, z.d, z.length), BF16),
        "qkv_t": V((z.micro, 3 * z.width, z.length), BF16),
        "normed": V((z.micro, z.tok, z.d), F32),
        "chances": V((z.micro, z.tok, z.experts), F32),
        "gate": V((z.micro, z.tok, 1), F32),
        "place": V((z.micro, z.tok, z.slots), BF16),
        "mix": V((z.micro, z.ncol, z.tok, z.width), BF16),
        "mown": V((z.micro, z.ncol, z.tok, z.width), BF16),
        "hidden": V((z.micro, z.tok, z.d), F32),
        "slots": V((z.micro, z.nrow, z.slots, 2 * z.d), BF16),
        "near": V((z.nrow, z.micro, 1, z.tok), jnp.int32),
        "near_rows": V((z.nrow, z.tok, 2 * z.d), BF16),
        "dq": V((z.d, 3 * z.width), BF16),
        "wo": V((z.ncol, z.d, z.width), BF16),
        "bias": V((z.heads, z.length, z.length), F32),
        "wi": V((z.d, z.ffh), BF16),
        "wd": V((z.nrow, z.ffh, z.dr), BF16),
        "arr": V((z.micro, z.nrow, z.slots, 2 * z.d), BF16),
        "own_part": V((z.micro, z.slots, 2 * z.d), F32),
        "psend": V((z.micro, others, z.slots, 2 * z.d), BF16),
        "precv": V((z.micro, others, z.slots, 2 * z.d), BF16),
        "back": V((z.micro, z.slots, 2 * z.d), BF16),
        "ret": V((z.micro, z.slots, 2 * z.d), BF16),
        "act": V((z.micro, z.nrow, z.slots, z.ffh), BF16),
        "gpre": V((z.micro, z.nrow, z.slots, z.ffh), BF16),
        "xt": V((z.d, z.micro * z.nrow * z.slots), BF16),
        "pc": V((z.micro, z.ncol, z.tok, z.d), BF16),
        "gh": V((z.micro, z.tok, z.d), F32),
        "gms": V((z.micro, z.ncol, z.tok, z.width), BF16),
        "gm": V((z.micro, z.ncol, z.tok, z.width), BF16),
        "pairs": V((z.micro, z.heads, z.length, z.length), BF16),
        "gj_t": V((3 * z.width, z.length), BF16),
        "gdo": V((z.d, z.width), F32),
        "gdq": V((z.heads, z.d, z.width), F32),
        "pb": V((z.micro, z.ncol, z.tok, z.d), BF16),
        "pr": V((z.micro, 2, z.tok, z.d), BF16),
        "px": V((z.micro, z.tok, z.d), BF16),
        "xsum": V((z.micro, z.tok, z.d), BF16),
        "zo": V((z.ndp - 1, both, z.width), BF16),
        "zo_got": V((z.ndp - 1, both, z.width), BF16),
        "zq": V((z.heads, z.ndp - 1, both, z.width), BF16),
        "zq_got": V((z.heads, z.ndp - 1, both, z.width), BF16),
        "yo": V((others, z.piece, z.width), BF16),
        "yo_got": V((others, z.piece, z.width), BF16),
        "yq": V((z.heads, others, z.piece, z.width), BF16),
        "yq_got": V((z.heads, others, z.piece, z.width), BF16),
        "ebuf": V((z.ncol, z.small // z.ncol, z.d), F32),
        "eterm": V((2, z.small // z.ncol, z.d), F32),
        "egot": V((3, most, z.small // z.ncol, z.d), F32),
        "eout": V((z.ncol, z.small // z.ncol, z.d), F32),
        "lbuf": V((8, 128), F32),
        "lterm": V((2, 8, 128), F32),
        "lgot": V((3, most, 8, 128), F32),
        "send_sem": sem((320,)),
        "recv_sem": sem((320,)),
        "here_sem": sem((4,)),
    }
    run = pl.pallas_call(
        functools.partial(layer_kernel, z, [*ins, *outs, *scratch]),
        out_shape=list(outs.values()),
        in_specs=[VM] * (len(ins) - 2) + [ANY] * 2,
        out_specs=[VM] * 6 + [ANY] * 2,
        scratch_shapes=list(scratch.values()),
        compiler_params=pltpu.CompilerParams(collective_id=1, has_side_effects=True, vmem_limit_bytes=63 * 2**20),
        name="layer",
    )
    found = dict(zip(outs, run(*ins.values()), strict=True))
    steps = 2
    whole = lambda shape: pl.BlockSpec(shape, lambda i: (0,) * len(shape))
    cut_in, cut_down = (z.dr // steps, z.ff), (z.ff // steps, z.dr)
    shapes = {
        "layer_out": S((z.micro, z.tok, z.d), BF16),
        "grad_tok": S((z.micro, z.tok, z.d), F32),
        "gain_one": S((z.d,), F32),
        "grad_qkv": S((3, z.piece, z.width), F32),
        "grad_out": S((z.width, z.piece), F32),
        "rel": S((z.heads, z.nbuck), F32),
        "gain_two": S((z.d,), F32),
        "router": S((z.experts, z.d), F32),
        "gwi": S((z.dr, z.ff), F32),
        "gwd": S((z.ff, z.dr), F32),
    }
    by_rows = lambda shape: pl.BlockSpec(shape, lambda i: (i, 0))
    pick = lambda given: [
        by_rows(cut_in) if n == "gwi" else by_rows(cut_down) if n == "gwd" else whole(s.shape) for n, s in given.items()
    ]
    done = pl.pallas_call(
        functools.partial(write_results, z, list(outs), list(shapes)),
        grid=(steps,),
        out_shape=list(shapes.values()),
        in_specs=pick(outs),
        out_specs=pick(shapes),
        compiler_params=pltpu.CompilerParams(vmem_limit_bytes=62 * 2**20),
        name="results",
    )(*found.values())
    d = dict(zip(shapes, done, strict=True))
    return (
        d["layer_out"][:, None], d["grad_tok"][:, None], d["gain_one"], jnp.swapaxes(d["grad_qkv"], 0, 1), d["grad_out"],
        d["rel"].T, d["gain_two"], d["router"].T, d["gwi"][None], d["gwd"][None],
    )


def smooth_act(values):
    return jax.nn.gelu(values, approximate=True)


def plain_normalize(values, gain_vec):
    factor = lax.rsqrt(jnp.mean(values * values, axis=-1, keepdims=True) + EPSILON)
    return (values * factor * gain_vec, factor)


def plain_norm_back(grad_into, values, factor, gain_vec):
    scaled = grad_into * gain_vec
    inner = jnp.mean(scaled * values, axis=-1, keepdims=True)
    return (
        factor * (scaled - values * factor * factor * inner),
        jnp.sum(grad_into * values * factor, axis=0),
    )


def contract_rows(left, right, precision=None):
    return lax.dot_general(
        left,
        right,
        (((0,), (0,)), ((), ())),
        precision=precision,
        preferred_element_type=jnp.float32,
    )


def contract_cols(left, right, precision=None):
    return lax.dot_general(
        left,
        right,
        (((1,), (1,)), ((), ())),
        precision=precision,
        preferred_element_type=jnp.float32,
    )


def spread_rows(offsets, row_first, row_count, length):
    shifted = jnp.roll(offsets, row_first, axis=-1)
    span_width = 2 * length - 1
    tiled_rows = jnp.tile(shifted, (1, row_count))[:, : row_count * span_width]
    return tiled_rows.reshape(offsets.shape[0], row_count, span_width)[:, :, length - 1 :]


def plain_gather_offsets(grads, row_first, length):
    heads_here = grads.shape[0]
    row_count = grads.shape[1]
    span_width = 2 * length - 1
    widened = jnp.pad(grads, ((0, 0), (0, 0), (length - 1, 0)))
    flat_rows = jnp.pad(
        widened.reshape(heads_here, row_count * span_width), ((0, 0), (0, row_count))
    )
    folded = jnp.sum(flat_rows.reshape(heads_here, row_count, 2 * length), axis=1)
    return jnp.roll(folded, -row_first, axis=-1)


def score_block(query_part, key_rows, bias_part, marks_query, marks_keys):
    scores = (
        jnp.einsum("qhd,khd->hqk", query_part, key_rows, preferred_element_type=jnp.float32)
        + bias_part
    )
    same_doc = marks_query[:, None] == marks_keys[None, :]
    return jnp.where(same_doc[None], scores, MASKED)


def fetch_dense(w_qkv, w_out):
    return (
        lax.all_gather(w_qkv, ("dp", "row"), axis=0, tiled=True),
        lax.all_gather(w_out, ("dp", "row"), axis=1, tiled=True),
    )


def fetch_experts(w_in, w_down):
    grown_in, grown_down = (
        lax.all_gather(w_in, "row", axis=1, tiled=True),
        lax.all_gather(w_down, "row", axis=2, tiled=True),
    )
    return (grown_in[0], grown_down[0])


def plain_shards(
    tokens,
    segments,
    routes,
    buckets,
    gain_attn,
    w_qkv,
    w_out,
    rel_table,
    gain_ffn,
    router,
    w_in,
    w_down,
    cotangent,
):
    micro_count = tokens.shape[0]
    tok_rows = tokens.shape[2]
    model_width = tokens.shape[3]
    length = segments.shape[2]
    local_heads = rel_table.shape[1]
    head_size = w_out.shape[0] // local_heads
    local_width = local_heads * head_size
    experts_all = router.shape[1]
    hidden_units = w_in.shape[2]
    capacity = max(2, 2 * tok_rows // experts_all)
    query_block = min(512, length)
    block_starts = list(range(0, length, query_block))
    padded_ids = jnp.concatenate([buckets, jnp.full((1,), -1, jnp.int32)])
    offset_table = (
        padded_ids[:, None] == jnp.arange(rel_table.shape[0], dtype=jnp.int32)[None, :]
    ).astype(jnp.float32)
    offset_bias = jnp.dot(offset_table, rel_table, precision=HIGHEST).T
    block_bias = [
        spread_rows(offset_bias, row_start, query_block, length) for row_start in block_starts
    ]
    expert_ids = jnp.arange(experts_all, dtype=jnp.int32)
    slot_ids = jnp.arange(experts_all * capacity, dtype=jnp.int32)
    saved = []
    outputs = []
    for micro_index in range(micro_count):
        full_qkv, full_out = fetch_dense(w_qkv, w_out)
        full_in, full_down = fetch_experts(w_in, w_down)
        own_rows = tokens[micro_index, 0].astype(jnp.float32)
        whole_rows = lax.all_gather(tokens[micro_index, 0], "col", axis=0, tiled=True).astype(
            jnp.float32
        )
        normed_one = plain_normalize(whole_rows, gain_attn)[0].astype(jnp.bfloat16)
        joined = jnp.einsum(
            "td,dcf->tcf", normed_one, full_qkv, preferred_element_type=jnp.float32
        ).astype(jnp.bfloat16)
        queries = joined[:, 0].reshape(length, local_heads, head_size)
        key_rows = joined[:, 1].reshape(length, local_heads, head_size)
        value_rows = joined[:, 2].reshape(length, local_heads, head_size)
        marks = segments[micro_index, 0]
        mixed_parts = []
        log_sums = []
        for block_index, row_start in enumerate(block_starts):
            scores = score_block(queries, key_rows, block_bias[block_index], marks, marks)
            highest = jnp.max(scores, axis=-1, keepdims=True)
            log_sum = highest + jnp.log(jnp.sum(jnp.exp(scores - highest), axis=-1, keepdims=True))
            weights = jnp.exp(scores - log_sum).astype(jnp.bfloat16)
            mixed_parts.append(
                jnp.einsum(
                    "hqk,khd->qhd", weights, value_rows, preferred_element_type=jnp.float32
                ).astype(jnp.bfloat16)
            )
            log_sums.append(log_sum)
        mixed = mixed_parts[0].reshape(length, local_width)
        hidden = own_rows + lax.psum_scatter(
            jnp.dot(mixed, full_out, preferred_element_type=jnp.float32),
            "col",
            scatter_dimension=0,
            tiled=True,
        )
        normed_two, factor_two = plain_normalize(hidden, gain_ffn)
        chances = jax.nn.softmax(jnp.dot(normed_two, router, precision=HIGHEST), axis=-1)
        chosen = routes[micro_index, 0, :, 0]
        picked = chosen[:, None] == expert_ids[None, :]
        gate_value = jnp.sum(jnp.where(picked, chances, 0.0), axis=-1)
        picked_int = picked.astype(jnp.int32)
        ranks = jnp.sum((jnp.cumsum(picked_int, axis=0) - picked_int) * picked_int, axis=1)
        placement = ((chosen * capacity + ranks)[:, None] == slot_ids[None, :]).astype(jnp.bfloat16)
        outgoing = contract_rows(placement, normed_two.astype(jnp.bfloat16)).astype(jnp.bfloat16)
        outgoing = outgoing.reshape(experts_all, capacity, model_width)
        arrived = lax.all_to_all(outgoing, ("dp", "col"), split_axis=0, concat_axis=0, tiled=True)
        flat_in = arrived.reshape(-1, model_width)
        before = jnp.dot(flat_in, full_in, preferred_element_type=jnp.float32)
        active = smooth_act(before).astype(jnp.bfloat16)
        result = jnp.dot(active, full_down, preferred_element_type=jnp.float32).astype(jnp.bfloat16)
        sent_back = lax.all_to_all(
            result.reshape(arrived.shape), ("dp", "col"), split_axis=0, concat_axis=0, tiled=True
        )
        sent_back, arrived, before_all = (
            sent_back,
            arrived,
            before.reshape(arrived.shape[0], arrived.shape[1], hidden_units),
        )
        expert_out = jnp.dot(
            placement, sent_back.reshape(-1, model_width), preferred_element_type=jnp.float32
        )
        outputs.append((hidden + gate_value[:, None] * expert_out).astype(jnp.bfloat16))
        saved.append(
            (
                own_rows,
                normed_one,
                queries,
                key_rows,
                value_rows,
                marks,
                log_sums,
                mixed,
                hidden,
                normed_two,
                factor_two,
                chances,
                picked,
                gate_value,
                placement,
                expert_out,
                arrived,
                before_all,
            )
        )
    grad_qkv_sum = jnp.zeros((model_width, 3, local_width), jnp.float32)
    grad_out_sum = jnp.zeros((local_width, model_width), jnp.float32)
    grad_in_sum = jnp.zeros((model_width, hidden_units), jnp.float32)
    grad_down_sum = jnp.zeros((hidden_units, model_width), jnp.float32)
    grad_offsets = jnp.zeros((local_heads, 2 * length), jnp.float32)
    grad_gain_one = jnp.zeros((model_width,), jnp.float32)
    grad_gain_two = jnp.zeros((model_width,), jnp.float32)
    grad_router_sum = jnp.zeros(router.shape, jnp.float32)
    grads_input = []
    for micro_index in range(micro_count):
        (
            own_rows,
            normed_one,
            queries,
            key_rows,
            value_rows,
            marks,
            log_sums,
            mixed,
            hidden,
            normed_two,
            factor_two,
            chances,
            picked,
            gate_value,
            placement,
            expert_out,
            arrived,
            before_all,
        ) = saved[micro_index]
        full_qkv, full_out = fetch_dense(w_qkv, w_out)
        full_in, full_down = fetch_experts(w_in, w_down)
        upstream = cotangent[micro_index, 0].astype(jnp.float32)
        grad_gate = jnp.sum(upstream * expert_out, axis=-1)
        grad_result = (gate_value[:, None] * upstream).astype(jnp.bfloat16)
        to_slots = contract_rows(placement, grad_result).astype(jnp.bfloat16)
        to_slots = to_slots.reshape(experts_all, capacity, model_width)
        at_expert = lax.all_to_all(
            to_slots, ("dp", "col"), split_axis=0, concat_axis=0, tiled=True
        ).reshape(-1, model_width)
        flat_before = before_all.reshape(-1, hidden_units)
        act_value, act_pull = jax.vjp(smooth_act, flat_before)
        flat_active = act_value.astype(jnp.bfloat16)
        grad_down_sum = grad_down_sum + contract_rows(flat_active, at_expert)
        grad_active = contract_cols(at_expert, full_down)
        grad_before = act_pull(grad_active)[0].astype(jnp.bfloat16)
        grad_in_sum = grad_in_sum + contract_rows(arrived.reshape(-1, model_width), grad_before)
        grad_sent = (
            contract_cols(grad_before, full_in)
            .astype(jnp.bfloat16)
            .reshape(experts_all, capacity, model_width)
        )
        came_back = lax.all_to_all(
            grad_sent, ("dp", "col"), split_axis=0, concat_axis=0, tiled=True
        )
        grad_normed_two = jnp.dot(
            placement, came_back.reshape(-1, model_width), preferred_element_type=jnp.float32
        )
        grad_logits = (grad_gate * gate_value)[:, None] * (picked.astype(jnp.float32) - chances)
        grad_router_sum = grad_router_sum + contract_rows(normed_two, grad_logits, HIGHEST)
        grad_normed_two = grad_normed_two + contract_cols(grad_logits, router, HIGHEST)
        grad_norm_part, gain_part = plain_norm_back(grad_normed_two, hidden, factor_two, gain_ffn)
        grad_gain_two = grad_gain_two + gain_part
        grad_hidden = upstream + grad_norm_part
        piece = lax.all_gather(grad_hidden.astype(jnp.bfloat16), "col", axis=0, tiled=True)
        total_out = grad_out_sum
        total_out = total_out + contract_rows(mixed, piece)
        spread_grad = contract_cols(piece, full_out)
        grad_out_sum = total_out
        grad_mixed = spread_grad
        grad_mixed = grad_mixed.astype(jnp.bfloat16).reshape(length, local_heads, head_size)
        grad_keys = jnp.zeros((length, local_heads, head_size), jnp.float32)
        grad_values = jnp.zeros((length, local_heads, head_size), jnp.float32)
        query_grads = []
        for block_index, row_start in enumerate(block_starts):
            scores = score_block(queries, key_rows, block_bias[block_index], marks, marks)
            weights = jnp.exp(scores - log_sums[block_index])
            grad_values = jnp.einsum(
                "hqk,qhd->khd",
                weights.astype(jnp.bfloat16),
                grad_mixed,
                preferred_element_type=jnp.float32,
            )
            grad_weights = jnp.einsum(
                "qhd,khd->hqk", grad_mixed, value_rows, preferred_element_type=jnp.float32
            )
            grad_scores = (
                weights * (grad_weights - jnp.sum(weights * grad_weights, axis=-1, keepdims=True))
            ).astype(jnp.bfloat16)
            grad_offsets = grad_offsets + plain_gather_offsets(
                grad_scores.astype(jnp.float32), row_start, length
            )
            query_grads.append(
                jnp.einsum(
                    "hqk,khd->qhd", grad_scores, key_rows, preferred_element_type=jnp.float32
                )
            )
            grad_keys = jnp.einsum(
                "hqk,qhd->khd", grad_scores, queries, preferred_element_type=jnp.float32
            )
        grad_joined = jnp.stack([query_grads[0], grad_keys, grad_values], axis=1)
        grad_joined = grad_joined.reshape(length, 3, local_width).astype(jnp.bfloat16)
        grad_qkv_sum = grad_qkv_sum + jnp.einsum(
            "td,tcf->dcf", normed_one, grad_joined, preferred_element_type=jnp.float32
        )
        grad_normed_one = lax.psum_scatter(
            jnp.einsum(
                "tcf,dcf->td", grad_joined, full_qkv, preferred_element_type=jnp.float32
            ).astype(jnp.bfloat16),
            "col",
            scatter_dimension=0,
            tiled=True,
        ).astype(jnp.float32)
        factor_one = plain_normalize(own_rows, gain_attn)[1]
        grad_input_part, gain_part = plain_norm_back(grad_normed_one, own_rows, factor_one, gain_attn)
        grad_gain_one = grad_gain_one + gain_part
        grads_input.append(grad_hidden + grad_input_part)
    grad_rel_mine = jnp.dot(offset_table.T, grad_offsets.T, precision=HIGHEST)
    heads_all = local_heads * lax.axis_size("col")
    head_first = lax.axis_index("col") * local_heads
    rel_full = lax.dynamic_update_slice_in_dim(
        jnp.zeros((rel_table.shape[0], heads_all), jnp.float32), grad_rel_mine, head_first, 1
    )
    total_gain_one, total_gain_two, total_router, total_rel = lax.psum(
        (grad_gain_one, grad_gain_two, grad_router_sum, rel_full), ("dp", "row", "col")
    )
    rel_out = lax.dynamic_slice_in_dim(total_rel, head_first, local_heads, 1)
    dense_qkv, dense_out = (
        lax.psum_scatter(grad_qkv_sum, ("dp", "row"), scatter_dimension=0, tiled=True),
        lax.psum_scatter(grad_out_sum, ("dp", "row"), scatter_dimension=1, tiled=True),
    )
    expert_in, expert_down = (
        lax.psum_scatter(
            grad_in_sum[None].astype(jnp.bfloat16), "row", scatter_dimension=1, tiled=True
        ).astype(jnp.float32),
        lax.psum_scatter(
            grad_down_sum[None].astype(jnp.bfloat16), "row", scatter_dimension=2, tiled=True
        ).astype(jnp.float32),
    )
    layer_out = jnp.stack(outputs)[:, None]
    grad_tokens = jnp.stack(grads_input)[:, None]
    return (
        layer_out,
        grad_tokens,
        total_gain_one,
        dense_qkv,
        dense_out,
        rel_out,
        total_gain_two,
        total_router,
        expert_in,
        expert_down,
    )


def solution(mesh):
    shape = tuple(mesh.shape[a] for a in ("dp", "row", "col"))
    token_spec, expert_in, expert_down = P(None, ("dp", "row"), "col", None), P(("dp", "col"), "row", None), P(("dp", "col"), None, "row")
    qkv_spec, out_spec = P(("dp", "row"), None, "col"), P("col", ("dp", "row"))
    in_specs = (
        token_spec, P(None, ("dp", "row"), None), token_spec, P(), P(), qkv_spec, out_spec, P(None, "col"), P(), P(),
        expert_in, expert_down, token_spec,
    )
    out_specs = (token_spec, token_spec, P(), qkv_spec, out_spec, P(None, "col"), P(), P(), expert_in, expert_down)

    def run(*args):
        piece, each = args[5].shape[0] // (shape[0] * shape[1]), 2 * args[0].shape[2] // shape[2] // args[9].shape[1]
        whole_tiles = piece % 16 == 0 and each % 16 == 0 and shape[2] == 4 and args[0].shape[0] == 2
        body = functools.partial(fast, shape) if whole_tiles else plain_shards
        return jax.shard_map(body, mesh=mesh, in_specs=in_specs, out_specs=out_specs, check_vma=False)(*args)

    return run
```

```python
import functools
import types

import jax
import jax.numpy as jnp
from jax import lax
from jax.experimental import pallas as pl
from jax.experimental.pallas import tpu as pltpu
from jax.sharding import PartitionSpec as P

EPSILON = 1e-06
HIGHEST = lax.Precision.HIGHEST
MASKED = -1000000000.0
MESH = pl.DeviceIdType.MESH
F32 = jnp.float32
BF16 = jnp.bfloat16
NN = (((1,), (0,)), ((), ()))
NT = (((1,), (1,)), ((), ()))
TN = (((0,), (0,)), ((), ()))


def mm(left, right, dims=NN, precision=None):
    return lax.dot_general(left, right, dims, precision=precision, preferred_element_type=F32)


def rows(first, count):
    return pl.ds(pl.multiple_of(first, count), count)


class Links:
    def __init__(self, send_sem, recv_sem):
        self.send_sem, self.recv_sem, self.used, self.started = send_sem, recv_sem, 0, []

    def send(self, src, dst, device):
        k = self.used
        self.used += 1
        copy = pltpu.make_async_remote_copy(
            src_ref=src, dst_ref=dst, send_sem=self.send_sem.at[k], recv_sem=self.recv_sem.at[k],
            device_id=device, device_id_type=MESH,
        )
        copy.start()
        self.started.append(copy)
        return copy

    def finish(self):
        for copy in self.started:
            copy.wait_send()


class Place:
    def __init__(self, z):
        self.dp, self.row, self.col = lax.axis_index("dp"), lax.axis_index("row"), lax.axis_index("col")
        dp, row, col = self.dp, self.row, self.col
        self.dps = [lax.rem(dp + i, z.ndp) for i in range(z.ndp)]
        self.rws = [lax.rem(row + i, z.nrow) for i in range(z.nrow)]
        self.cls = [lax.rem(col + i, z.ncol) for i in range(z.ncol)]
        self.dps_back = [lax.rem(dp + z.ndp - i, z.ndp) for i in range(z.ndp)]
        self.rws_back = [lax.rem(row + z.nrow - i, z.nrow) for i in range(z.nrow)]
        self.cls_back = [lax.rem(col + z.ncol - i, z.ncol) for i in range(z.ncol)]
        self.across = lax.rem(col + 2, z.ncol)
        self.beside = col + 1 - 2 * lax.rem(col, 2)
        self.far = lax.rem(self.beside + 2, z.ncol)


def greet(devices):
    barrier = pltpu.get_barrier_semaphore()
    for device in devices:
        pl.semaphore_signal(barrier, inc=1, device_id=device, device_id_type=MESH)
    return lambda: pl.semaphore_wait(barrier, len(devices))


def norm_rows(values):
    return lax.rsqrt(jnp.mean(values * values, axis=-1, keepdims=True) + EPSILON)


def norm_back(grad_into, values, factor, gain_vec):
    scaled = grad_into * gain_vec
    inner = jnp.mean(scaled * values, axis=-1, keepdims=True)
    return (
        factor * (scaled - values * factor * factor * inner),
        jnp.sum(grad_into * values * factor, axis=0, keepdims=True),
    )


def column(line):
    return jnp.broadcast_to(line.astype(F32), (8, line.shape[1])).T[:, :1]


def offset_table(z, rb):
    ids = lax.broadcasted_iota(jnp.int32, (z.nbuck, 2 * z.length), 0)
    return (ids == rb[...]).astype(F32)


def backwards(values):
    ids = lax.broadcasted_iota(jnp.int32, (128, 128), 0) + lax.broadcasted_iota(jnp.int32, (128, 128), 1)
    turn = (ids == 127).astype(F32)
    blocks = values.shape[1] // 128
    return jnp.concatenate(
        [mm(values[:, k * 128 : (k + 1) * 128], turn, NN, HIGHEST) for k in range(blocks - 1, -1, -1)], axis=1
    )


def make_bias(z, rb, rel, bias):
    offsets = backwards(mm(rel[...], offset_table(z, rb), NN, HIGHEST))
    for h in range(z.heads):
        spread = jnp.broadcast_to(offsets[h : h + 1, :], (z.length, 2 * z.length))
        turned = pltpu.roll(spread, z.length, 1, stride=1, stride_axis=0)
        bias[h] = turned[:, : z.length]


def gather_offsets(values):
    count = values.shape[0] // 2
    while count >= 1:
        values = pltpu.roll(values[:count], count, 1) + values[count:]
        count //= 2
    return values


def routing(z, chosen):
    ids = lax.broadcasted_iota(jnp.int32, (z.tok, z.experts), 1).astype(F32)
    picked = chosen == ids
    before = (
        lax.broadcasted_iota(jnp.int32, (z.tok, z.tok), 0) > lax.broadcasted_iota(jnp.int32, (z.tok, z.tok), 1)
    ).astype(BF16)
    counts = mm(before, picked.astype(BF16))
    ranks = jnp.sum(jnp.where(picked, counts, 0.0), axis=1, keepdims=True)
    slot = chosen * z.slots_each + ranks
    placement = (slot == lax.broadcasted_iota(jnp.int32, (z.tok, z.slots), 1).astype(F32)).astype(BF16)
    return picked, placement


def softmax_rows(logits):
    top = jnp.exp(logits - jnp.max(logits, axis=-1, keepdims=True))
    return top / jnp.sum(top, axis=-1, keepdims=True)


def gelu_both(before):
    inner = 0.7978845608 * (before + 0.044715 * before * before * before)
    t = jnp.tanh(inner)
    half = 0.5 * (1.0 + t)
    slope = half + 0.5 * before * (1.0 - t * t) * (0.7978845608 * (1.0 + 3.0 * 0.044715 * before * before))
    return before * half, slope


def partner(index, step):
    return index + step - 2 * step * lax.rem(index // step, 2)


def reduce_all(z, me, links, part, term, got, out, per_col=0):
    dp, row, col = me.dp, me.row, me.col
    split = len(out.shape) == 3
    stages = (
        (z.ncol, col, [(dp, row, c) for c in me.cls[1:]]),
        (z.ndp, dp, [(d, row, col) for d in me.dps[1:]]),
        (z.nrow, row, [(dp, w, col) for w in me.rws[1:]]),
    )
    for k, (size, mine, others) in enumerate(stages):
        if k == 0:
            copies = [links.send(part(c), got.at[0, col], device) for c, device in zip(me.cls[1:], others)]
            got[0, col] = part(col)[...]
        else:
            term[k - 1] = total
            copies = [links.send(term.at[k - 1], got.at[k, mine], device) for device in others]
            got[k, mine] = total
        yield
        for copy in copies:
            copy.wait_recv()
        total = jnp.zeros(got.shape[2:], F32)
        for i in range(size):
            value = got[k, i]
            if k == 0 and per_col:
                line = lax.broadcasted_iota(jnp.int32, value.shape, 0)
                value = jnp.where((line < value.shape[0] - per_col) | (i == col), value, 0.0)
            total = total + value
    if split:
        out[col] = total
        copies = [links.send(out.at[col], out.at[col], device) for device in stages[0][2]]
        yield
        for copy in copies:
            copy.wait_recv()
    else:
        out[...] = total


def attention_forward(z, r, m):
    seg = r.seg[m]
    same = column(seg) == seg.astype(F32)
    parts = []
    for h in range(z.heads):
        q_t, k_t, v_t = (r.qkv_t[m, pl.ds(c * z.width + h * z.head, z.head), :] for c in range(3))
        scores = jnp.where(same, mm(k_t, q_t, TN) + r.bias[h], MASKED)
        highest = jnp.max(scores, axis=0, keepdims=True)
        raised = jnp.exp(scores - highest)
        total = jnp.sum(raised, axis=0, keepdims=True)
        probs = (raised * (1.0 / total)).astype(BF16)
        r.pairs[m, h] = probs
        parts.append(mm(v_t, probs))
    mixed = jnp.concatenate(parts, axis=0).T.astype(BF16)
    for c in range(z.ncol):
        r.mix[m, c] = mixed[c * z.tok : (c + 1) * z.tok]


def attention_backward(z, r, m, h, grad_t):
    q_t, k_t, v_t = (r.qkv_t[m, pl.ds(c * z.width + h * z.head, z.head), :] for c in range(3))
    g_t = grad_t[h * z.head : (h + 1) * z.head, :]
    probs = r.pairs[m, h]
    wide = probs.astype(F32)
    grad_probs = mm(v_t, g_t, TN)
    delta = jnp.sum(wide * grad_probs, axis=0, keepdims=True)
    grads = (wide * (grad_probs - delta)).astype(BF16)
    r.pairs[m, h] = grads
    parts = [mm(k_t, grads), mm(q_t, grads, NT), mm(g_t, probs, NT)]
    for c, part in enumerate(parts):
        r.gj_t[pl.ds(c * z.width + h * z.head, z.head), :] = part.astype(BF16)
    return mm(r.nrm_t[m], jnp.concatenate(parts, axis=0).T.astype(BF16))


def layer_kernel(z, names, *refs):
    r = types.SimpleNamespace(**dict(zip(names, refs, strict=True)))
    me = Place(z)
    dp, row, col = me.dp, me.row, me.col
    links = Links(r.send_sem, r.recv_sem)
    plane = [(i, j) for i in range(z.ndp) for j in range(z.ncol) if (i, j) != (0, 0)]
    arrived = greet([(me.dps[i], row, me.cls[j]) for i, j in plane] + [(dp, w, col) for w in me.rws[1:]])
    gain, gain_ffn = r.gain[...].reshape(1, z.d), r.gain_ffn[...].reshape(1, z.d)
    micros = range(z.micro)

    own = [
        pltpu.make_async_copy(r.w_in.at[:, rows(row * z.ffh, z.ffh)], r.wi.at[rows(row * z.dr, z.dr), :], r.here_sem.at[0]),
        pltpu.make_async_copy(r.w_down.at[rows(row * z.ffh, z.ffh), :], r.wd.at[row], r.here_sem.at[1]),
    ]
    for copy in own:
        copy.start()
    pid = dp * z.nrow + row
    piece = lambda p: r.dq.at[rows(p * z.piece, z.piece), :]
    out_piece = lambda c, p: r.wo.at[c, rows(p * z.piece, z.piece), :]
    r.dq[rows(pid * z.piece, z.piece), :] = jnp.concatenate([r.w_qkv[c] for c in range(3)], axis=1)
    r.wo[col, rows(pid * z.piece, z.piece), :] = r.w_out[...].astype(F32).T.astype(BF16)
    for m in micros:
        values = r.tok[m].astype(F32)
        r.nrm[m, rows(col * z.tok, z.tok), :] = (values * norm_rows(values) * gain).astype(BF16)
    arrived()

    dense_y = [links.send(piece(pid), piece(pid), (dp, w, col)) for w in me.rws[1:]]
    out_y = [links.send(out_piece(col, pid), out_piece(col, pid), (dp, w, col)) for w in me.rws[1:]]
    dense_z = [links.send(piece(pid), piece(pid), (d, row, col)) for d in me.dps[1:]]
    routes = [links.send(r.routes, r.near.at[row], (dp, w, col)) for w in me.rws[1:]]
    experts = []
    for w in me.rws[1:]:
        experts.append(links.send(r.w_in.at[:, rows(w * z.ffh, z.ffh)], r.wi.at[rows(row * z.dr, z.dr), :], (dp, w, col)))
        experts.append(links.send(r.w_down.at[rows(w * z.ffh, z.ffh), :], r.wd.at[row], (dp, w, col)))
    block = lambda m, c: r.nrm.at[m, rows(c * z.tok, z.tok), :]
    xs = [links.send(block(m, col), block(m, col), (dp, row, me.across)) for m in micros]
    cs = [links.send(block(m, col), block(m, col), (dp, row, me.beside)) for m in micros]
    out_x, out_c = {}, []

    def share(i, s):
        p = me.dps_back[i] * z.nrow + me.rws_back[s]
        out_x[i, s] = links.send(out_piece(col, p), out_piece(col, p), (dp, row, me.across))
        out_c.append(links.send(out_piece(col, p), out_piece(col, p), (dp, row, me.beside)))

    share(0, 0)
    for s, copy in enumerate(dense_y):
        copy.wait_recv()
        p = dp * z.nrow + me.rws_back[s + 1]
        dense_z += [links.send(piece(p), piece(p), (d, row, col)) for d in me.dps[1:]]
    out_z = {(i, 0): links.send(out_piece(col, pid), out_piece(col, pid), (me.dps[i], row, col)) for i in range(1, z.ndp)}
    for s, copy in enumerate(out_y):
        copy.wait_recv()
        p = dp * z.nrow + me.rws_back[s + 1]
        for i in range(1, z.ndp):
            out_z[i, s + 1] = links.send(out_piece(col, p), out_piece(col, p), (me.dps[i], row, col))
        share(0, s + 1)
    make_bias(z, r.rb, r.rel, r.bias)
    fs = []
    for m in micros:
        xs[m].wait_recv()
        fs.append(links.send(block(m, me.across), block(m, me.across), (dp, row, me.beside)))
    for copy in dense_z + cs + fs:
        copy.wait_recv()

    swaps = []
    for m in micros:
        r.qkv_t[m] = mm(r.nrm[m], r.dq[...]).astype(BF16).T
        if m == 0:
            for i in range(1, z.ndp):
                out_z[i, 0].wait_recv()
                share(i, 0)
        attention_forward(z, r, m)
        swaps.append([links.send(r.mix.at[m, c], r.mown.at[m, col], (dp, row, c)) for c in me.cls[1:]])
        r.mown[m, col] = r.mix[m, col]
        if m == 0:
            for s in range(1, z.nrow):
                for i in range(1, z.ndp):
                    out_z[i, s].wait_recv()
                    share(i, s)
        r.nrm_t[m] = r.nrm[m].T
    for (i, s), copy in out_x.items():
        copy.wait_recv()
        p = me.dps_back[i] * z.nrow + me.rws_back[s]
        out_c.append(links.send(out_piece(me.across, p), out_piece(me.across, p), (dp, row, me.beside)))
    for copy in out_c:
        copy.wait_recv()

    mine = dp * z.ncol + col
    each = z.slots_each
    group = z.ncol * each
    dispatch = []

    def spread(m, w, slots):
        r.slots[m, w] = slots
        copies = {}
        for i, j in plane:
            e = me.dps[i] * z.ncol + me.cls[j]
            copies[i, j] = links.send(
                r.slots.at[m, w, rows(e * each, each), :], r.arr.at[m, w, rows(mine * each, each), :],
                (me.dps[i], row, me.cls[j]),
            )
        r.arr[m, w, rows(mine * each, each), :] = r.slots[m, w, rows(mine * each, each), :]
        return copies

    for m in micros:
        for copy in swaps[m]:
            copy.wait_recv()
        values = r.tok[m].astype(F32)
        for c in range(z.ncol):
            values = values + mm(r.mown[m, c], r.wo[c], NT)
        r.hidden[m] = values
        normed = values * norm_rows(values) * gain_ffn
        chances = softmax_rows(mm(normed, r.router[...], NT, HIGHEST))
        picked, placement = routing(z, column(r.routes[m]))
        gate = jnp.sum(jnp.where(picked, chances, 0.0), axis=-1, keepdims=True)
        r.normed[m], r.chances[m], r.gate[m], r.place[m] = normed, chances, gate, placement
        sent = jnp.concatenate([normed.astype(BF16), (gate * r.cot[m].astype(F32)).astype(BF16)], axis=1)
        if m == z.micro - 1:
            r.near_rows[row] = sent
            crossing = [links.send(r.near_rows.at[row], r.near_rows.at[row], (dp, w, col)) for w in me.rws[1:]]
        dispatch.append(spread(m, row, mm(placement, sent, TN).astype(BF16)))

    forwards = []
    for m in micros[:-1]:
        copies = {}
        for i in range(z.ndp):
            for j in range(z.ncol):
                if (i, j) != (0, 0):
                    dispatch[m][i, j].wait_recv()
            part = r.arr.at[m, row, rows(me.dps_back[i] * group, group), :]
            for s, w in enumerate(me.rws[1:]):
                copies[i, s] = links.send(part, part, (dp, w, col))
        forwards.append(copies)

    for copy in routes + crossing:
        copy.wait_recv()
    cross = {}
    for s in range(z.nrow - 1):
        w = me.rws_back[s + 1]
        placement = routing(z, column(r.near[w, z.micro - 1]))[1]
        cross[s] = spread(z.micro - 1, w, mm(placement, r.near_rows[w], TN).astype(BF16))

    spots = [rows(d * group, group) for d in me.dps]
    halves = [(0, z.ndp - 1), tuple(range(z.ndp - 2, 0, -1))]

    def expert(m, w, picks, store):
        x = jnp.concatenate([r.arr[m, w, spots[i], : z.d] for i in picks], axis=0)
        g = jnp.concatenate([r.arr[m, w, spots[i], z.d :] for i in picks], axis=0)
        result = jnp.zeros(x.shape, F32)
        grad = jnp.zeros(x.shape, F32)
        for k in range(z.ffh // z.chunk):
            cut = pl.ds(k * z.chunk, z.chunk)
            w_one = r.wi[:, cut]
            w_two = jnp.concatenate([r.wd[p, cut, :] for p in range(z.nrow)], axis=1)
            value, slope = gelu_both(mm(x, w_one))
            value = value.astype(BF16)
            result = result + mm(value, w_two)
            pre = (mm(g, w_two, NT) * slope).astype(BF16)
            grad = grad + mm(pre, w_one, NT)
            for n, i in enumerate(picks):
                r.act[m, w, spots[i], cut] = value[n * group : (n + 1) * group]
                r.gpre[m, w, spots[i], cut] = pre[n * group : (n + 1) * group]
        for n, i in enumerate(picks):
            store(i, jnp.concatenate([result[n * group : (n + 1) * group], grad[n * group : (n + 1) * group]], axis=1))

    for copy in own:
        copy.wait()
    for copy in experts:
        copy.wait_recv()
    def go_home(m):
        home = []
        for i in order:
            spot = spots[i]
            total = r.own_part[m, spot, :]
            for s in range(z.nrow - 1):
                partials[m][i, s].wait_recv()
                total = total + r.precv[m, s, spot, :].astype(F32)
            r.back[m, spot, :] = total.astype(BF16)
            for j in range(z.ncol):
                if (i, j) != (0, 0):
                    e = me.dps[i] * z.ncol + me.cls[j]
                    home.append(
                        links.send(
                            r.back.at[m, rows(e * each, each), :], r.ret.at[m, rows(mine * each, each), :],
                            (me.dps[i], row, me.cls[j]),
                        )
                    )
        r.ret[m, rows(mine * each, each), :] = r.back[m, rows(mine * each, each), :]
        return home

    returns = []
    waited = set()
    partials = []
    order = [*range(z.ndp - 1, 0, -1), 0]
    for m in micros:

        def store_own(i, value, m=m):
            r.own_part[m, spots[i], :] = value

        if m == z.micro - 1:
            for copy in dispatch[m].values():
                copy.wait_recv()
        expert(m, row, range(z.ndp), store_own)
        copies = {}
        for s, w in enumerate(me.rws[1:]):
            for picks in halves:
                back = [(z.ndp - i) % z.ndp for i in picks]
                if m < z.micro - 1:
                    for i in back:
                        for k in range(z.nrow - 1):
                            if (i, k) not in waited:
                                forwards[m][i, k].wait_recv()
                                waited.add((i, k))
                else:
                    for k in range(z.nrow - 1):
                        for i, j in plane:
                            if i in back and (i, j, k) not in waited:
                                cross[k][i, j].wait_recv()
                                waited.add((i, j, k))

                def store(i, value, m=m, s=s, w=w):
                    r.psend[m, s, spots[i], :] = value.astype(BF16)
                    copies[i, s] = links.send(r.psend.at[m, s, spots[i], :], r.precv.at[m, s, spots[i], :], (dp, w, col))

                expert(m, w, picks, store)
                if m == z.micro - 1 and s == 0 and picks is halves[0]:
                    returns.append(go_home(0))
        partials.append(copies)

    blocks = [(m, w) for m in micros for w in range(z.nrow)]
    for b, (m, w) in enumerate(blocks):
        r.xt[:, b * z.slots : (b + 1) * z.slots] = r.arr[m, w, :, : z.d].T
    for k in range(z.ffh // z.chunk):
        cut = pl.ds(k * z.chunk, z.chunk)
        pre = jnp.concatenate([r.gpre[m, w, :, cut] for m, w in blocks], axis=0)
        value = jnp.concatenate([r.act[m, w, :, cut] for m, w in blocks], axis=0)
        g = jnp.concatenate([r.arr[m, w, :, z.d :] for m, w in blocks], axis=0)
        r.wi[:, cut] = mm(r.xt[...], pre).astype(BF16)
        grad_down = mm(value, g, TN).astype(BF16)
        for p in range(z.nrow):
            r.wd[p, cut, :] = grad_down[:, p * z.dr : (p + 1) * z.dr]

    kept = [
        pltpu.make_async_copy(r.wi.at[rows(row * z.dr, z.dr), :], r.gwi.at[:, rows(row * z.ffh, z.ffh)], r.here_sem.at[2]),
        pltpu.make_async_copy(r.wd.at[row], r.gwd.at[rows(row * z.ffh, z.ffh), :], r.here_sem.at[3]),
    ]
    for copy in kept:
        copy.start()
    swapped = []

    def swap_grads(first, last, parts):
        for w in me.rws[1:]:
            for k in range(first, last):
                n = z.dr // parts
                swapped.append(links.send(
                    r.wi.at[rows(w * z.dr + k * n, n), :], r.gwi.at[pl.ds(k * n, n), rows(row * z.ffh, z.ffh)], (dp, w, col)
                ))
                n = z.ffh // parts
                swapped.append(links.send(
                    r.wd.at[w, pl.ds(k * n, n), :], r.gwd.at[rows(row * z.ffh + k * n, n), :], (dp, w, col)
                ))

    swap_grads(0, 8, 8)

    def token_back(m):
        for copy in returns[m]:
            copy.wait_recv()
        values = r.hidden[m]
        factor = norm_rows(values)
        normed, chances, gate = r.normed[m], r.chances[m], r.gate[m]
        picked = column(r.routes[m]) == lax.broadcasted_iota(jnp.int32, (z.tok, z.experts), 1).astype(F32)
        came = mm(r.place[m], r.ret[m])
        returned, grad_sent = came[:, : z.d], came[:, z.d :]
        r.layer_out[m] = (values + gate * returned).astype(BF16)
        upstream = r.cot[m].astype(F32)
        grad_gate = jnp.sum(upstream * returned, axis=-1, keepdims=True)
        grad_logits = grad_gate * gate * (picked.astype(F32) - chances)
        grad_normed = grad_sent + mm(grad_logits, r.router[...], NN, HIGHEST)
        part, gain_part = norm_back(grad_normed, values, factor, gain_ffn)
        grad_hidden = upstream + part
        r.gh[m] = grad_hidden
        branch = grad_hidden.astype(BF16)
        for c in me.cls:
            r.gms[m, c] = mm(branch, r.wo[c]).astype(BF16)
        heads_in = [links.send(r.gms.at[m, c], r.gm.at[m, col], (dp, row, c)) for c in me.cls[1:]]
        r.gm[m, col] = r.gms[m, col]
        r.pc[m, col] = branch
        across = links.send(r.pc.at[m, col], r.pc.at[m, col], (dp, row, me.across))
        beside = links.send(r.pc.at[m, col], r.pc.at[m, col], (dp, row, me.beside))
        return heads_in, (across, beside), mm(grad_logits, normed, TN, HIGHEST), gain_part

    step = lambda run: next(run, None)
    wire = []

    def all_rows(m, sends):
        across, beside = sends
        across.wait_recv()
        passed = links.send(r.pc.at[m, me.across], r.pc.at[m, me.across], (dp, row, me.beside))
        beside.wait_recv()
        passed.wait_recv()
        return r.pc[m].reshape(z.length, z.d)

    def into_heads(m, copies):
        for copy in copies:
            copy.wait_recv()
        return r.gm[m].reshape(z.length, z.width).T

    def first_norm_rows(m, gj):
        partial = mm(gj, r.dq[...], NT).astype(BF16)
        for c in range(z.ncol):
            r.pb[m, c] = partial[c * z.tok : (c + 1) * z.tok]
        wire.append([links.send(r.pb.at[m, me.far], r.pr.at[m, 1], (dp, row, me.beside)),
                     links.send(r.pb.at[m, me.beside], r.pr.at[m, 0], (dp, row, me.beside))])

    def across_chips(m):
        wire[m][0].wait_recv()
        r.xsum[m] = (r.pb[m, me.across].astype(F32) + r.pr[m, 1].astype(F32)).astype(BF16)
        wire[m].append(links.send(r.xsum.at[m], r.px.at[m], (dp, row, me.across)))

    both = z.nrow * z.piece

    def reduce_over_dp(total, out, got):
        sends = []
        for i, d in enumerate(me.dps[1:]):
            out[i] = total[rows(d * both, both), :].astype(BF16)
            sends.append(links.send(out.at[i], got.at[i], (d, row, col)))
        return sends

    def sum_here(w, total, got):
        spot = rows((dp * z.nrow + w) * z.piece, z.piece)
        value = total[spot, :]
        for i in range(z.ndp - 1):
            value = value + got[i, rows(w * z.piece, z.piece), :].astype(F32)
        return value

    heads_in, sends_zero, router_t, gain_two = token_back(0)
    returns.append(go_home(1))
    grad_t = into_heads(0, heads_in)
    r.gdq[0] = attention_backward(z, r, 0, 0, grad_t)
    for h in range(1, z.heads):
        r.gdq[h] = attention_backward(z, r, 0, h, grad_t)
    first_norm_rows(0, r.gj_t[...].T)
    heads_in, sends_one, router_part, gain_part = token_back(1)
    across_chips(0)
    r.gdo[...] = mm(all_rows(0, sends_zero), r.mix[0].reshape(z.length, z.width), TN)
    sums = jnp.concatenate([router_t + router_part, gain_two + gain_part], axis=0)
    sums = jnp.concatenate([sums, jnp.zeros((z.small - z.experts - 1, z.d), F32)], axis=0)
    for c in range(z.ncol):
        r.ebuf[c] = sums[c * z.small // z.ncol : (c + 1) * z.small // z.ncol]
    early = reduce_all(z, me, links, lambda c: r.ebuf.at[c], r.eterm, r.egot, r.eout)
    step(early)
    grad_t = into_heads(1, heads_in)
    qkv_sent = []
    for h in range(z.heads):
        r.gdq[h] = r.gdq[h] + attention_backward(z, r, 1, h, grad_t)
        qkv_sent.append(reduce_over_dp(r.gdq.at[h], r.zq.at[h], r.zq_got.at[h]))
        if h == 0:
            step(early)
            r.gdo[...] = r.gdo[...] + mm(all_rows(1, sends_one), r.mix[1].reshape(z.length, z.width), TN)
            out_sent = reduce_over_dp(r.gdo, r.zo, r.zo_got)
    first_norm_rows(1, r.gj_t[...].T)
    step(early)
    across_chips(1)

    offsets = []
    for h in range(z.heads):
        total = r.pairs[0, h].astype(F32)
        for m in range(1, z.micro):
            total = total + r.pairs[m, h].astype(F32)
        offsets.append(gather_offsets(jnp.concatenate([total, jnp.zeros((z.length, z.length), F32)], axis=1)))
    offsets = backwards(pltpu.roll(jnp.concatenate(offsets, axis=0), 1, 1))
    grad_rel = mm(offsets, offset_table(z, r.rb), NT, HIGHEST)
    gain_one = jnp.zeros((1, z.d), F32)
    for m in micros:
        wire[m][1].wait_recv()
        wire[m][2].wait_recv()
        grad_normed = r.pb[m, col].astype(F32) + r.pr[m, 0].astype(F32) + r.px[m].astype(F32)
        values = r.tok[m].astype(F32)
        part, gain_part = norm_back(grad_normed, values, norm_rows(values), gain)
        gain_one = gain_one + gain_part
        r.grad_tok[m] = r.gh[m] + part
    lines = z.d // 128
    r.lbuf[...] = jnp.zeros(r.lbuf.shape, F32)
    for k in range(lines):
        r.lbuf[pl.ds(k, 1), :] = gain_one[:, k * 128 : (k + 1) * 128]
    r.lbuf[pl.ds(lines, 1), :] = jnp.concatenate(
        [grad_rel[h : h + 1, :] for h in range(z.heads)] + [jnp.zeros((1, 128 - z.heads * z.nbuck), F32)], axis=1
    )
    final = reduce_all(z, me, links, lambda c: r.lbuf, r.lterm, r.lgot, r.late, 8 - lines)
    for _ in range(2):
        step(final)
    ysent = []
    for h in range(z.heads):
        for copy in qkv_sent[h]:
            copy.wait_recv()
        for s, w in enumerate(me.rws[1:]):
            r.yq[h, s] = sum_here(w, r.gdq.at[h], r.zq_got.at[h]).astype(BF16)
            ysent.append(links.send(r.yq.at[h, s], r.yq_got.at[h, s], (dp, w, col)))
    step(final)
    for copy in out_sent:
        copy.wait_recv()
    for s, w in enumerate(me.rws[1:]):
        r.yo[s] = sum_here(w, r.gdo, r.zo_got).astype(BF16)
        ysent.append(links.send(r.yo.at[s], r.yo_got.at[s], (dp, w, col)))
    step(early)
    out_sum = sum_here(row, r.gdo, r.zo_got)
    qkv_sum = [sum_here(row, r.gdq.at[h], r.zq_got.at[h]) for h in range(z.heads)]
    for copy in ysent:
        copy.wait_recv()
    for s in range(z.nrow - 1):
        out_sum = out_sum + r.yo_got[s].astype(F32)
        qkv_sum = [total + r.yq_got[h, s].astype(F32) for h, total in enumerate(qkv_sum)]
    r.grad_out[...] = out_sum.T
    for c in range(3):
        r.grad_qkv[c] = jnp.concatenate([total[:, c * z.head : (c + 1) * z.head] for total in qkv_sum], axis=1)
    for run in (early, final):
        for _ in run:
            pass
    for c in range(z.ncol):
        r.small[pl.ds(c * z.small // z.ncol, z.small // z.ncol), :] = r.eout[c]
    for copy in kept:
        copy.wait()
    for copy in swapped:
        copy.wait_recv()
    links.finish()


def sizes(mesh_shape, tokens, segments, rel_table, w_in, router):
    z = types.SimpleNamespace()
    z.ndp, z.nrow, z.ncol = mesh_shape
    z.micro, z.tok, z.d = tokens.shape[0], tokens.shape[2], tokens.shape[3]
    z.length = segments.shape[2]
    z.nbuck, z.heads = rel_table.shape
    z.width = z.d // z.ncol
    z.head = z.width // z.heads
    z.ff = w_in.shape[2]
    z.ffh, z.dr = z.ff // z.nrow, z.d // z.nrow
    z.experts = router.shape[1]
    z.slots_each = max(2, 2 * z.tok // z.experts)
    z.slots = z.experts * z.slots_each
    z.piece = z.d // (z.ndp * z.nrow)
    z.chunk = min(512, z.ffh)
    z.small = -(-(z.experts + 1) // (8 * z.ncol)) * 8 * z.ncol
    return z


VM = pl.BlockSpec(memory_space=pltpu.VMEM)
ANY = pl.BlockSpec(memory_space=pl.ANY)


def write_results(z, given, wanted, *refs):
    r = types.SimpleNamespace(**dict(zip(given, refs[: len(given)], strict=True)))
    o = types.SimpleNamespace(**dict(zip(wanted, refs[len(given) :], strict=True)))
    o.gwi[...] = r.gwi[...].astype(F32)
    o.gwd[...] = r.gwd[...].astype(F32)

    @pl.when(pl.program_id(0) == 0)
    def _():
        for name in ("layer_out", "grad_tok", "grad_qkv", "grad_out"):
            getattr(o, name)[...] = getattr(r, name)[...]
        o.router[...] = r.small[: z.experts, :]
        lines = z.d // 128
        for h in range(z.heads):
            o.rel[pl.ds(h, 1), :] = r.late[lines : lines + 1, h * z.nbuck : (h + 1) * z.nbuck]
        for k in range(lines):
            o.gain_one[pl.ds(k * 128, 128)] = r.late[k, :]
        o.gain_two[...] = r.small[z.experts, :]


def fast(mesh_shape, tokens, segments, routes, buckets, gain_attn, w_qkv, w_out, rel_table, gain_ffn, router, w_in,
         w_down, cotangent):
    z = sizes(mesh_shape, tokens, segments, rel_table, w_in, router)
    S = jax.ShapeDtypeStruct
    V = pltpu.VMEM
    sem = pltpu.SemaphoreType.DMA
    rb = jnp.pad(buckets, (0, 1), constant_values=-1)[None]
    ins = {
        "tok": tokens[:, 0], "seg": segments, "routes": jnp.swapaxes(routes[:, 0], 1, 2), "rb": rb, "gain": gain_attn,
        "w_qkv": jnp.swapaxes(w_qkv, 0, 1), "w_out": w_out, "rel": rel_table.T, "gain_ffn": gain_ffn, "router": router.T, "cot": cotangent[:, 0],
        "w_in": w_in[0], "w_down": w_down[0],
    }
    outs = {
        "layer_out": S((z.micro, z.tok, z.d), BF16),
        "grad_tok": S((z.micro, z.tok, z.d), F32),
        "grad_qkv": S((3, z.piece, z.width), F32),
        "grad_out": S((z.width, z.piece), F32),
        "small": S((z.small, z.d), F32),
        "late": S((8, 128), F32),
        "gwi": S((z.dr, z.ff), BF16),
        "gwd": S((z.ff, z.dr), BF16),
    }
    others, both = z.nrow - 1, z.nrow * z.piece
    most = max(mesh_shape)
    scratch = {
        "nrm": V((z.micro, z.length, z.d), BF16),
        "nrm_t": V((z.micro, z.d, z.length), BF16),
        "qkv_t": V((z.micro, 3 * z.width, z.length), BF16),
        "normed": V((z.micro, z.tok, z.d), F32),
        "chances": V((z.micro, z.tok, z.experts), F32),
        "gate": V((z.micro, z.tok, 1), F32),
        "place": V((z.micro, z.tok, z.slots), BF16),
        "mix": V((z.micro, z.ncol, z.tok, z.width), BF16),
        "mown": V((z.micro, z.ncol, z.tok, z.width), BF16),
        "hidden": V((z.micro, z.tok, z.d), F32),
        "slots": V((z.micro, z.nrow, z.slots, 2 * z.d), BF16),
        "near": V((z.nrow, z.micro, 1, z.tok), jnp.int32),
        "near_rows": V((z.nrow, z.tok, 2 * z.d), BF16),
        "dq": V((z.d, 3 * z.width), BF16),
        "wo": V((z.ncol, z.d, z.width), BF16),
        "bias": V((z.heads, z.length, z.length), F32),
        "wi": V((z.d, z.ffh), BF16),
        "wd": V((z.nrow, z.ffh, z.dr), BF16),
        "arr": V((z.micro, z.nrow, z.slots, 2 * z.d), BF16),
        "own_part": V((z.micro, z.slots, 2 * z.d), F32),
        "psend": V((z.micro, others, z.slots, 2 * z.d), BF16),
        "precv": V((z.micro, others, z.slots, 2 * z.d), BF16),
        "back": V((z.micro, z.slots, 2 * z.d), BF16),
        "ret": V((z.micro, z.slots, 2 * z.d), BF16),
        "act": V((z.micro, z.nrow, z.slots, z.ffh), BF16),
        "gpre": V((z.micro, z.nrow, z.slots, z.ffh), BF16),
        "xt": V((z.d, z.micro * z.nrow * z.slots), BF16),
        "pc": V((z.micro, z.ncol, z.tok, z.d), BF16),
        "gh": V((z.micro, z.tok, z.d), F32),
        "gms": V((z.micro, z.ncol, z.tok, z.width), BF16),
        "gm": V((z.micro, z.ncol, z.tok, z.width), BF16),
        "pairs": V((z.micro, z.heads, z.length, z.length), BF16),
        "gj_t": V((3 * z.width, z.length), BF16),
        "gdo": V((z.d, z.width), F32),
        "gdq": V((z.heads, z.d, z.width), F32),
        "pb": V((z.micro, z.ncol, z.tok, z.d), BF16),
        "pr": V((z.micro, 2, z.tok, z.d), BF16),
        "px": V((z.micro, z.tok, z.d), BF16),
        "xsum": V((z.micro, z.tok, z.d), BF16),
        "zo": V((z.ndp - 1, both, z.width), BF16),
        "zo_got": V((z.ndp - 1, both, z.width), BF16),
        "zq": V((z.heads, z.ndp - 1, both, z.width), BF16),
        "zq_got": V((z.heads, z.ndp - 1, both, z.width), BF16),
        "yo": V((others, z.piece, z.width), BF16),
        "yo_got": V((others, z.piece, z.width), BF16),
        "yq": V((z.heads, others, z.piece, z.width), BF16),
        "yq_got": V((z.heads, others, z.piece, z.width), BF16),
        "ebuf": V((z.ncol, z.small // z.ncol, z.d), F32),
        "eterm": V((2, z.small // z.ncol, z.d), F32),
        "egot": V((3, most, z.small // z.ncol, z.d), F32),
        "eout": V((z.ncol, z.small // z.ncol, z.d), F32),
        "lbuf": V((8, 128), F32),
        "lterm": V((2, 8, 128), F32),
        "lgot": V((3, most, 8, 128), F32),
        "send_sem": sem((320,)),
        "recv_sem": sem((320,)),
        "here_sem": sem((4,)),
    }
    run = pl.pallas_call(
        functools.partial(layer_kernel, z, [*ins, *outs, *scratch]),
        out_shape=list(outs.values()),
        in_specs=[VM] * (len(ins) - 2) + [ANY] * 2,
        out_specs=[VM] * 6 + [ANY] * 2,
        scratch_shapes=list(scratch.values()),
        compiler_params=pltpu.CompilerParams(collective_id=1, has_side_effects=True, vmem_limit_bytes=63 * 2**20),
        name="layer",
    )
    found = dict(zip(outs, run(*ins.values()), strict=True))
    steps = 2
    whole = lambda shape: pl.BlockSpec(shape, lambda i: (0,) * len(shape))
    cut_in, cut_down = (z.dr // steps, z.ff), (z.ff // steps, z.dr)
    shapes = {
        "layer_out": S((z.micro, z.tok, z.d), BF16),
        "grad_tok": S((z.micro, z.tok, z.d), F32),
        "gain_one": S((z.d,), F32),
        "grad_qkv": S((3, z.piece, z.width), F32),
        "grad_out": S((z.width, z.piece), F32),
        "rel": S((z.heads, z.nbuck), F32),
        "gain_two": S((z.d,), F32),
        "router": S((z.experts, z.d), F32),
        "gwi": S((z.dr, z.ff), F32),
        "gwd": S((z.ff, z.dr), F32),
    }
    by_rows = lambda shape: pl.BlockSpec(shape, lambda i: (i, 0))
    pick = lambda given: [
        by_rows(cut_in) if n == "gwi" else by_rows(cut_down) if n == "gwd" else whole(s.shape) for n, s in given.items()
    ]
    done = pl.pallas_call(
        functools.partial(write_results, z, list(outs), list(shapes)),
        grid=(steps,),
        out_shape=list(shapes.values()),
        in_specs=pick(outs),
        out_specs=pick(shapes),
        compiler_params=pltpu.CompilerParams(vmem_limit_bytes=62 * 2**20),
        name="results",
    )(*found.values())
    d = dict(zip(shapes, done, strict=True))
    return (
        d["layer_out"][:, None], d["grad_tok"][:, None], d["gain_one"], jnp.swapaxes(d["grad_qkv"], 0, 1), d["grad_out"],
        d["rel"].T, d["gain_two"], d["router"].T, d["gwi"][None], d["gwd"][None],
    )


def smooth_act(values):
    return jax.nn.gelu(values, approximate=True)


def plain_normalize(values, gain_vec):
    factor = lax.rsqrt(jnp.mean(values * values, axis=-1, keepdims=True) + EPSILON)
    return (values * factor * gain_vec, factor)


def plain_norm_back(grad_into, values, factor, gain_vec):
    scaled = grad_into * gain_vec
    inner = jnp.mean(scaled * values, axis=-1, keepdims=True)
    return (
        factor * (scaled - values * factor * factor * inner),
        jnp.sum(grad_into * values * factor, axis=0),
    )


def contract_rows(left, right, precision=None):
    return lax.dot_general(
        left,
        right,
        (((0,), (0,)), ((), ())),
        precision=precision,
        preferred_element_type=jnp.float32,
    )


def contract_cols(left, right, precision=None):
    return lax.dot_general(
        left,
        right,
        (((1,), (1,)), ((), ())),
        precision=precision,
        preferred_element_type=jnp.float32,
    )


def spread_rows(offsets, row_first, row_count, length):
    shifted = jnp.roll(offsets, row_first, axis=-1)
    span_width = 2 * length - 1
    tiled_rows = jnp.tile(shifted, (1, row_count))[:, : row_count * span_width]
    return tiled_rows.reshape(offsets.shape[0], row_count, span_width)[:, :, length - 1 :]


def plain_gather_offsets(grads, row_first, length):
    heads_here = grads.shape[0]
    row_count = grads.shape[1]
    span_width = 2 * length - 1
    widened = jnp.pad(grads, ((0, 0), (0, 0), (length - 1, 0)))
    flat_rows = jnp.pad(
        widened.reshape(heads_here, row_count * span_width), ((0, 0), (0, row_count))
    )
    folded = jnp.sum(flat_rows.reshape(heads_here, row_count, 2 * length), axis=1)
    return jnp.roll(folded, -row_first, axis=-1)


def score_block(query_part, key_rows, bias_part, marks_query, marks_keys):
    scores = (
        jnp.einsum("qhd,khd->hqk", query_part, key_rows, preferred_element_type=jnp.float32)
        + bias_part
    )
    same_doc = marks_query[:, None] == marks_keys[None, :]
    return jnp.where(same_doc[None], scores, MASKED)


def fetch_dense(w_qkv, w_out):
    return (
        lax.all_gather(w_qkv, ("dp", "row"), axis=0, tiled=True),
        lax.all_gather(w_out, ("dp", "row"), axis=1, tiled=True),
    )


def fetch_experts(w_in, w_down):
    grown_in, grown_down = (
        lax.all_gather(w_in, "row", axis=1, tiled=True),
        lax.all_gather(w_down, "row", axis=2, tiled=True),
    )
    return (grown_in[0], grown_down[0])


def plain_shards(
    tokens,
    segments,
    routes,
    buckets,
    gain_attn,
    w_qkv,
    w_out,
    rel_table,
    gain_ffn,
    router,
    w_in,
    w_down,
    cotangent,
):
    micro_count = tokens.shape[0]
    tok_rows = tokens.shape[2]
    model_width = tokens.shape[3]
    length = segments.shape[2]
    local_heads = rel_table.shape[1]
    head_size = w_out.shape[0] // local_heads
    local_width = local_heads * head_size
    experts_all = router.shape[1]
    hidden_units = w_in.shape[2]
    capacity = max(2, 2 * tok_rows // experts_all)
    query_block = min(512, length)
    block_starts = list(range(0, length, query_block))
    padded_ids = jnp.concatenate([buckets, jnp.full((1,), -1, jnp.int32)])
    offset_table = (
        padded_ids[:, None] == jnp.arange(rel_table.shape[0], dtype=jnp.int32)[None, :]
    ).astype(jnp.float32)
    offset_bias = jnp.dot(offset_table, rel_table, precision=HIGHEST).T
    block_bias = [
        spread_rows(offset_bias, row_start, query_block, length) for row_start in block_starts
    ]
    expert_ids = jnp.arange(experts_all, dtype=jnp.int32)
    slot_ids = jnp.arange(experts_all * capacity, dtype=jnp.int32)
    saved = []
    outputs = []
    for micro_index in range(micro_count):
        full_qkv, full_out = fetch_dense(w_qkv, w_out)
        full_in, full_down = fetch_experts(w_in, w_down)
        own_rows = tokens[micro_index, 0].astype(jnp.float32)
        whole_rows = lax.all_gather(tokens[micro_index, 0], "col", axis=0, tiled=True).astype(
            jnp.float32
        )
        normed_one = plain_normalize(whole_rows, gain_attn)[0].astype(jnp.bfloat16)
        joined = jnp.einsum(
            "td,dcf->tcf", normed_one, full_qkv, preferred_element_type=jnp.float32
        ).astype(jnp.bfloat16)
        queries = joined[:, 0].reshape(length, local_heads, head_size)
        key_rows = joined[:, 1].reshape(length, local_heads, head_size)
        value_rows = joined[:, 2].reshape(length, local_heads, head_size)
        marks = segments[micro_index, 0]
        mixed_parts = []
        log_sums = []
        for block_index, row_start in enumerate(block_starts):
            scores = score_block(queries, key_rows, block_bias[block_index], marks, marks)
            highest = jnp.max(scores, axis=-1, keepdims=True)
            log_sum = highest + jnp.log(jnp.sum(jnp.exp(scores - highest), axis=-1, keepdims=True))
            weights = jnp.exp(scores - log_sum).astype(jnp.bfloat16)
            mixed_parts.append(
                jnp.einsum(
                    "hqk,khd->qhd", weights, value_rows, preferred_element_type=jnp.float32
                ).astype(jnp.bfloat16)
            )
            log_sums.append(log_sum)
        mixed = mixed_parts[0].reshape(length, local_width)
        hidden = own_rows + lax.psum_scatter(
            jnp.dot(mixed, full_out, preferred_element_type=jnp.float32),
            "col",
            scatter_dimension=0,
            tiled=True,
        )
        normed_two, factor_two = plain_normalize(hidden, gain_ffn)
        chances = jax.nn.softmax(jnp.dot(normed_two, router, precision=HIGHEST), axis=-1)
        chosen = routes[micro_index, 0, :, 0]
        picked = chosen[:, None] == expert_ids[None, :]
        gate_value = jnp.sum(jnp.where(picked, chances, 0.0), axis=-1)
        picked_int = picked.astype(jnp.int32)
        ranks = jnp.sum((jnp.cumsum(picked_int, axis=0) - picked_int) * picked_int, axis=1)
        placement = ((chosen * capacity + ranks)[:, None] == slot_ids[None, :]).astype(jnp.bfloat16)
        outgoing = contract_rows(placement, normed_two.astype(jnp.bfloat16)).astype(jnp.bfloat16)
        outgoing = outgoing.reshape(experts_all, capacity, model_width)
        arrived = lax.all_to_all(outgoing, ("dp", "col"), split_axis=0, concat_axis=0, tiled=True)
        flat_in = arrived.reshape(-1, model_width)
        before = jnp.dot(flat_in, full_in, preferred_element_type=jnp.float32)
        active = smooth_act(before).astype(jnp.bfloat16)
        result = jnp.dot(active, full_down, preferred_element_type=jnp.float32).astype(jnp.bfloat16)
        sent_back = lax.all_to_all(
            result.reshape(arrived.shape), ("dp", "col"), split_axis=0, concat_axis=0, tiled=True
        )
        sent_back, arrived, before_all = (
            sent_back,
            arrived,
            before.reshape(arrived.shape[0], arrived.shape[1], hidden_units),
        )
        expert_out = jnp.dot(
            placement, sent_back.reshape(-1, model_width), preferred_element_type=jnp.float32
        )
        outputs.append((hidden + gate_value[:, None] * expert_out).astype(jnp.bfloat16))
        saved.append(
            (
                own_rows,
                normed_one,
                queries,
                key_rows,
                value_rows,
                marks,
                log_sums,
                mixed,
                hidden,
                normed_two,
                factor_two,
                chances,
                picked,
                gate_value,
                placement,
                expert_out,
                arrived,
                before_all,
            )
        )
    grad_qkv_sum = jnp.zeros((model_width, 3, local_width), jnp.float32)
    grad_out_sum = jnp.zeros((local_width, model_width), jnp.float32)
    grad_in_sum = jnp.zeros((model_width, hidden_units), jnp.float32)
    grad_down_sum = jnp.zeros((hidden_units, model_width), jnp.float32)
    grad_offsets = jnp.zeros((local_heads, 2 * length), jnp.float32)
    grad_gain_one = jnp.zeros((model_width,), jnp.float32)
    grad_gain_two = jnp.zeros((model_width,), jnp.float32)
    grad_router_sum = jnp.zeros(router.shape, jnp.float32)
    grads_input = []
    for micro_index in range(micro_count):
        (
            own_rows,
            normed_one,
            queries,
            key_rows,
            value_rows,
            marks,
            log_sums,
            mixed,
            hidden,
            normed_two,
            factor_two,
            chances,
            picked,
            gate_value,
            placement,
            expert_out,
            arrived,
            before_all,
        ) = saved[micro_index]
        full_qkv, full_out = fetch_dense(w_qkv, w_out)
        full_in, full_down = fetch_experts(w_in, w_down)
        upstream = cotangent[micro_index, 0].astype(jnp.float32)
        grad_gate = jnp.sum(upstream * expert_out, axis=-1)
        grad_result = (gate_value[:, None] * upstream).astype(jnp.bfloat16)
        to_slots = contract_rows(placement, grad_result).astype(jnp.bfloat16)
        to_slots = to_slots.reshape(experts_all, capacity, model_width)
        at_expert = lax.all_to_all(
            to_slots, ("dp", "col"), split_axis=0, concat_axis=0, tiled=True
        ).reshape(-1, model_width)
        flat_before = before_all.reshape(-1, hidden_units)
        act_value, act_pull = jax.vjp(smooth_act, flat_before)
        flat_active = act_value.astype(jnp.bfloat16)
        grad_down_sum = grad_down_sum + contract_rows(flat_active, at_expert)
        grad_active = contract_cols(at_expert, full_down)
        grad_before = act_pull(grad_active)[0].astype(jnp.bfloat16)
        grad_in_sum = grad_in_sum + contract_rows(arrived.reshape(-1, model_width), grad_before)
        grad_sent = (
            contract_cols(grad_before, full_in)
            .astype(jnp.bfloat16)
            .reshape(experts_all, capacity, model_width)
        )
        came_back = lax.all_to_all(
            grad_sent, ("dp", "col"), split_axis=0, concat_axis=0, tiled=True
        )
        grad_normed_two = jnp.dot(
            placement, came_back.reshape(-1, model_width), preferred_element_type=jnp.float32
        )
        grad_logits = (grad_gate * gate_value)[:, None] * (picked.astype(jnp.float32) - chances)
        grad_router_sum = grad_router_sum + contract_rows(normed_two, grad_logits, HIGHEST)
        grad_normed_two = grad_normed_two + contract_cols(grad_logits, router, HIGHEST)
        grad_norm_part, gain_part = plain_norm_back(grad_normed_two, hidden, factor_two, gain_ffn)
        grad_gain_two = grad_gain_two + gain_part
        grad_hidden = upstream + grad_norm_part
        piece = lax.all_gather(grad_hidden.astype(jnp.bfloat16), "col", axis=0, tiled=True)
        total_out = grad_out_sum
        total_out = total_out + contract_rows(mixed, piece)
        spread_grad = contract_cols(piece, full_out)
        grad_out_sum = total_out
        grad_mixed = spread_grad
        grad_mixed = grad_mixed.astype(jnp.bfloat16).reshape(length, local_heads, head_size)
        grad_keys = jnp.zeros((length, local_heads, head_size), jnp.float32)
        grad_values = jnp.zeros((length, local_heads, head_size), jnp.float32)
        query_grads = []
        for block_index, row_start in enumerate(block_starts):
            scores = score_block(queries, key_rows, block_bias[block_index], marks, marks)
            weights = jnp.exp(scores - log_sums[block_index])
            grad_values = jnp.einsum(
                "hqk,qhd->khd",
                weights.astype(jnp.bfloat16),
                grad_mixed,
                preferred_element_type=jnp.float32,
            )
            grad_weights = jnp.einsum(
                "qhd,khd->hqk", grad_mixed, value_rows, preferred_element_type=jnp.float32
            )
            grad_scores = (
                weights * (grad_weights - jnp.sum(weights * grad_weights, axis=-1, keepdims=True))
            ).astype(jnp.bfloat16)
            grad_offsets = grad_offsets + plain_gather_offsets(
                grad_scores.astype(jnp.float32), row_start, length
            )
            query_grads.append(
                jnp.einsum(
                    "hqk,khd->qhd", grad_scores, key_rows, preferred_element_type=jnp.float32
                )
            )
            grad_keys = jnp.einsum(
                "hqk,qhd->khd", grad_scores, queries, preferred_element_type=jnp.float32
            )
        grad_joined = jnp.stack([query_grads[0], grad_keys, grad_values], axis=1)
        grad_joined = grad_joined.reshape(length, 3, local_width).astype(jnp.bfloat16)
        grad_qkv_sum = grad_qkv_sum + jnp.einsum(
            "td,tcf->dcf", normed_one, grad_joined, preferred_element_type=jnp.float32
        )
        grad_normed_one = lax.psum_scatter(
            jnp.einsum(
                "tcf,dcf->td", grad_joined, full_qkv, preferred_element_type=jnp.float32
            ).astype(jnp.bfloat16),
            "col",
            scatter_dimension=0,
            tiled=True,
        ).astype(jnp.float32)
        factor_one = plain_normalize(own_rows, gain_attn)[1]
        grad_input_part, gain_part = plain_norm_back(grad_normed_one, own_rows, factor_one, gain_attn)
        grad_gain_one = grad_gain_one + gain_part
        grads_input.append(grad_hidden + grad_input_part)
    grad_rel_mine = jnp.dot(offset_table.T, grad_offsets.T, precision=HIGHEST)
    heads_all = local_heads * lax.axis_size("col")
    head_first = lax.axis_index("col") * local_heads
    rel_full = lax.dynamic_update_slice_in_dim(
        jnp.zeros((rel_table.shape[0], heads_all), jnp.float32), grad_rel_mine, head_first, 1
    )
    total_gain_one, total_gain_two, total_router, total_rel = lax.psum(
        (grad_gain_one, grad_gain_two, grad_router_sum, rel_full), ("dp", "row", "col")
    )
    rel_out = lax.dynamic_slice_in_dim(total_rel, head_first, local_heads, 1)
    dense_qkv, dense_out = (
        lax.psum_scatter(grad_qkv_sum, ("dp", "row"), scatter_dimension=0, tiled=True),
        lax.psum_scatter(grad_out_sum, ("dp", "row"), scatter_dimension=1, tiled=True),
    )
    expert_in, expert_down = (
        lax.psum_scatter(
            grad_in_sum[None].astype(jnp.bfloat16), "row", scatter_dimension=1, tiled=True
        ).astype(jnp.float32),
        lax.psum_scatter(
            grad_down_sum[None].astype(jnp.bfloat16), "row", scatter_dimension=2, tiled=True
        ).astype(jnp.float32),
    )
    layer_out = jnp.stack(outputs)[:, None]
    grad_tokens = jnp.stack(grads_input)[:, None]
    return (
        layer_out,
        grad_tokens,
        total_gain_one,
        dense_qkv,
        dense_out,
        rel_out,
        total_gain_two,
        total_router,
        expert_in,
        expert_down,
    )


def solution(mesh):
    shape = tuple(mesh.shape[a] for a in ("dp", "row", "col"))
    token_spec, expert_in, expert_down = P(None, ("dp", "row"), "col", None), P(("dp", "col"), "row", None), P(("dp", "col"), None, "row")
    qkv_spec, out_spec = P(("dp", "row"), None, "col"), P("col", ("dp", "row"))
    in_specs = (
        token_spec, P(None, ("dp", "row"), None), token_spec, P(), P(), qkv_spec, out_spec, P(None, "col"), P(), P(),
        expert_in, expert_down, token_spec,
    )
    out_specs = (token_spec, token_spec, P(), qkv_spec, out_spec, P(None, "col"), P(), P(), expert_in, expert_down)

    def run(*args):
        piece, each = args[5].shape[0] // (shape[0] * shape[1]), 2 * args[0].shape[2] // shape[2] // args[9].shape[1]
        whole_tiles = piece % 16 == 0 and each % 16 == 0 and shape[2] == 4 and args[0].shape[0] == 2
        body = functools.partial(fast, shape) if whole_tiles else plain_shards
        return jax.shard_map(body, mesh=mesh, in_specs=in_specs, out_specs=out_specs, check_vma=False)(*args)

    return run
```
